128 devices in a mesh: dp: 8 (over y_lo, z), row: 2 (over y_hi), col: 8 (over x, core).
Axes of the slice: x: 4, y: 4 (y_hi: 2, y_lo: 2; y = y_hi * 2 + y_lo), z: 4, core: 2. Of those that a mesh axis runs over, the one named last changes fastest.
Arguments:
- tokens: bfloat16 [16384, 1536], P(('dp', 'row', 'col')), may hold values from -6 to 6
- cotangent: bfloat16 [16384, 1536], P(('dp', 'row', 'col')), may hold values from -6 to 6
- lengths: int32 [16, 4], P(('dp', 'row')), may hold values from 1 to 960, 1024 in all within a row
- routes: int32 [16384, 8], P(('dp', 'row', 'col')), may hold values from 0 to 39, all different within a row; in each aligned block of 128 rows (0 to 127, 128 to 255, ...) at most 51 rows name the same one
- norm_gains: float32 [2, 1536], replicated, may hold values from 0.5 to 1.5
- gain_first: float32 [2, 1536], replicated, may hold values from -96 to 96
- gain_second: float32 [2, 1536], replicated, may hold values from 589.824 to 7864.32
- router_w: float32 [1536, 40], replicated, may hold values from -0.078125 to 0.078125
- router_first: float32 [1536, 40], replicated, may hold values from -160 to 160
- router_second: float32 [1536, 40], replicated, may hold values from 1572.48 to 20966.4
- projection_weight: float32 [1536, 8, 320], P('dp', 'col'), may hold values from -0.15625 to 0.15625
- projection_first_moment: float32 [1536, 8, 320], P('dp', 'col'), may hold values from -64 to 64
- projection_second_moment: float32 [1536, 8, 320], P('dp', 'col'), may hold values from 311.296 to 4259.84
- w_proj: float32 [1536, 1536], P('col', 'dp'), may hold values from -1.25 to 1.25
- proj_first: float32 [1536, 1536], P('col', 'dp'), may hold values from -8 to 8
- proj_second: float32 [1536, 1536], P('col', 'dp'), may hold values from 4.9152 to 65.536
- w_gate_up: float32 [40, 1536, 2, 512], P('col', 'dp', None, 'row'), may hold values from -0.15625 to 0.15625
- gate_up_first: float32 [40, 1536, 2, 512], P('col', 'dp', None, 'row'), may hold values from -20 to 20
- gate_up_second: float32 [40, 1536, 2, 512], P('col', 'dp', None, 'row'), may hold values from 24.57 to 327.6
- w_down: float32 [40, 512, 1536], P('col', 'row', 'dp'), may hold values from -1 to 1
- down_first: float32 [40, 512, 1536], P('col', 'row', 'dp'), may hold values from -2.5 to 2.5
- down_second: float32 [40, 512, 1536], P('col', 'row', 'dp'), may hold values from 0.52416 to 7.2072
Outputs:
- output: bfloat16 [16384, 1536], P(('dp', 'row', 'col'))
- dtokens: float32 [16384, 1536], P(('dp', 'row', 'col'))
- gain_new: float32 [2, 1536], replicated
- gain_first_new: float32 [2, 1536], replicated
- gain_second_new: float32 [2, 1536], replicated
- router_new: float32 [1536, 40], replicated
- router_first_new: float32 [1536, 40], replicated
- router_second_new: float32 [1536, 40], replicated
- qkv_new: float32 [1536, 8, 320], P('dp', 'col')
- qkv_first_new: float32 [1536, 8, 320], P('dp', 'col')
- qkv_second_new: float32 [1536, 8, 320], P('dp', 'col')
- proj_new: float32 [1536, 1536], P('col', 'dp')
- proj_first_new: float32 [1536, 1536], P('col', 'dp')
- proj_second_new: float32 [1536, 1536], P('col', 'dp')
- gate_up_new: float32 [40, 1536, 2, 512], P('col', 'dp', None, 'row')
- gate_up_first_new: float32 [40, 1536, 2, 512], P('col', 'dp', None, 'row')
- gate_up_second_new: float32 [40, 1536, 2, 512], P('col', 'dp', None, 'row')
- down_new: float32 [40, 512, 1536], P('col', 'row', 'dp')
- down_first_new: float32 [40, 512, 1536], P('col', 'row', 'dp')
- down_second_new: float32 [40, 512, 1536], P('col', 'row', 'dp')
The draws below stay inside these ranges and needn't reach their ends.
Inputs may be any that keep to these rules, and one draw needn't show every extreme that they name: `lengths`: each row sums to 1024; its largest entry is exactly 960. `routes`: A row names 8 different experts; among the rows of one device no expert is named by more than 51 rows, a bound that some block reaches.
All inputs are finite; a program needn't handle non-finite values.
Results may differ from the reference program's by a relative error of at most 0.025.
Values may be sent and summed in bfloat16 or wider, within the bound.
No kernel may reach another device: no remote copies, remote signals or barrier semaphores. Data moves between devices by JAX's collectives and lax.ppermute only.
A program may use at most 256 MiB of HBM per device.

```python
import math
import jax
import jax.numpy as jnp
import numpy as np
from jax import lax

MODEL_DIM = 1536
HQ = 24
KEY_HEADS = 8
HEAD_SIZE = 64
FF = 512
TOP = 8
NDOC = 4
STEP = 10
QUERY_PER_KEY = 3
HEAD_PROJ_COLS = 320
EXPERTS = 40
GROUP_TOKENS = 1024
TOK_DEV = 128
TOKEN_TOTAL = 16384
GROUPS = 16
LONGEST = 960
CAP = 51


def levels(rng, extent, cuts, smallest, top_value):
    def one(position, parts):
        heights = jax.random.uniform(jax.random.fold_in(jax.random.fold_in(rng, 6), position), (parts,), jnp.float32, smallest / len(cuts), top_value / len(cuts))
        return jnp.repeat(jnp.exp(heights), extent[position] // parts).reshape((-1,) + (1,) * (len(extent) - position - 1))

    level = one(*cuts[0])
    for cut in cuts[1:]:
        level = level * one(*cut)
    return level


def split_up(number_of, total, most, lean):
    portions = [(1 << 20) // math.isqrt(standing ** lean) + 1 for standing in range(2, number_of + 1)]
    rest, given = total - most - (number_of - 1), [1] * (number_of - 1)
    while rest > 0:
        candidates = [i for i in range(number_of - 1) if given[i] < most]
        whole, budget = sum([portions[i] for i in candidates]), rest
        for i in candidates:
            more = min(most - given[i], max(1, budget * portions[i] // whole), rest)
            given[i] = given[i] + more
            rest = rest - more
    return np.array([most] + given)


def uneven(key, amount, total, bound, lean):
    if amount == 2:
        one = jax.random.randint(key, (), max(1, total - bound), min(bound, total - 1) + 1)
        return jnp.stack([one, total - one])
    sizes = jnp.asarray(split_up(amount, total, bound, lean), jnp.int32)
    pairs = (amount - 1) // 2
    source_of, sink = sizes[1:1 + 2 * pairs:2], sizes[2:2 + 2 * pairs:2]
    margin = jnp.minimum(source_of - 1, bound - sink)
    shifted = jax.random.randint(jax.random.fold_in(key, 1), (pairs,), 0, 1 << 20) % (margin + 1)
    sizes = sizes.at[1:1 + 2 * pairs:2].set(source_of - shifted).at[2:2 + 2 * pairs:2].set(sink + shifted)
    return sizes[jax.random.permutation(jax.random.fold_in(key, 2), amount)]


def assign_block(stream_key, own, number, rows, number_of, top, bound, slope):
    order = jax.random.permutation(stream_key, number_of)
    packed, common = portions_of(number_of, rows * top, bound, slope, True), portions_of(number_of, rows * top, bound, slope, False)
    places = jnp.arange(number_of)

    def named(sizes, rotation):
        used = int((sizes > 0).sum())
        fixed = max(1, used // 4)
        passed = fixed + (places - fixed + rotation * (used - fixed)) % max(1, number_of - fixed)
        return jnp.zeros((number_of,), jnp.int32).at[order[jnp.where(places < fixed, places, passed)]].set(jnp.asarray(sizes, jnp.int32))

    sizes = jnp.where(number % 4 == 0, named(packed, number // 4), named(common, number - number // 4 - 1))
    mixed = jax.random.permutation(jax.random.fold_in(own, 3), number_of)
    source_of, taker = mixed[0:number_of // 2 * 2:2], mixed[1:number_of // 2 * 2:2]
    margin = jnp.minimum(sizes[source_of] - 1, bound - sizes[taker]) // 2
    margin = jnp.where((source_of == order[0]) | (taker == order[0]) | (sizes[taker] == 0), 0, jnp.maximum(margin, 0))
    passed = jax.random.randint(jax.random.fold_in(own, 4), (number_of // 2,), 0, 1 << 20) % (margin + 1)
    sizes = sizes.at[source_of].add(-passed).at[taker].add(passed)
    labels = jnp.searchsorted(jnp.cumsum(sizes), jnp.arange(rows * top), side="right").astype(jnp.int32)
    table = labels.reshape(top, rows).T
    table = table[jax.random.permutation(jax.random.fold_in(own, 1), rows)]
    rotation = jax.random.randint(jax.random.fold_in(own, 2), (rows, 1), 0, top)
    return jnp.take_along_axis(table, (jnp.arange(top)[None, :] + rotation) % top, axis=1)


def portions_of(number_of, total, bound, lean, full):
    weights = [(1 << 20) // math.isqrt(rank ** lean) + 1 for rank in range(1, number_of + 1)]
    largest = bound if full else min(bound, max(-(-total // number_of), total * weights[0] // sum(weights)))
    least = 1 if total - largest >= number_of - 1 else 0
    counts, spare = [largest] + [least] * (number_of - 1), total - largest - least * (number_of - 1)
    while spare > 0:
        movable = [i for i in range(1, number_of) if counts[i] < largest] or [i for i in range(1, number_of) if counts[i] < bound]
        whole, budget = sum([weights[i] for i in movable]), spare
        for i in movable:
            extra = min(bound - counts[i], max(1, budget * weights[i] // whole), spare)
            counts[i] = counts[i] + extra
            spare = spare - extra
    return np.array(counts)


def noise(own_key, shape, spread, reach, split=(), kind=jnp.bfloat16):
    values = spread * jax.random.normal(own_key, shape, jnp.float32)
    if split:
        values = values * levels(own_key, shape, split, -0.22, 0.18)
    return jnp.clip(values, -reach, reach).astype(kind)


def setup_inputs(seed: int = 0) -> dict:
    streams_of = jax.random.split(jax.random.key(seed), 23)
    tokens = noise(streams_of[0], (TOKEN_TOTAL, MODEL_DIM), 1.0, 6.0, ((0, 128),))
    cotangent = noise(streams_of[1], (TOKEN_TOTAL, MODEL_DIM), 1.0, 6.0, ((0, 128),))
    lengths = jax.vmap(lambda own: uneven(own, NDOC, GROUP_TOKENS, LONGEST, 2))(jax.random.split(streams_of[2], GROUPS)).reshape((GROUPS, NDOC)).astype(jnp.int32)
    routes_keys = jax.random.split(jax.random.fold_in(streams_of[3], 1), TOKEN_TOTAL // TOK_DEV)
    routes_turns = jax.random.permutation(jax.random.fold_in(streams_of[3], 3), TOKEN_TOTAL // TOK_DEV)
    routes = jax.vmap(lambda own, number: assign_block(jax.random.fold_in(streams_of[3], 2), own, number, TOK_DEV, EXPERTS, TOP, CAP, 1))(routes_keys, routes_turns).reshape((TOKEN_TOTAL, TOP))
    norm_gains = jnp.clip(1.0 + 0.1 * jax.random.normal(streams_of[4], (2, MODEL_DIM), jnp.float32), 0.5, 1.5)
    gain_first = noise(streams_of[5], (2, MODEL_DIM), (0.12 * TOKEN_TOTAL ** 0.5), 96.0, (), jnp.float32)
    gain_second = jnp.clip(jnp.exp(jax.random.uniform(streams_of[6], (2, MODEL_DIM), jnp.float32, math.log(589.824), math.log(7864.32))), 589.824, 7864.32)
    router_w = noise(streams_of[7], (MODEL_DIM, EXPERTS), (4 * MODEL_DIM) ** -0.5, 0.078125, (), jnp.float32)
    router_first = noise(streams_of[8], (MODEL_DIM, EXPERTS), (0.44 * (TOKEN_TOTAL * TOP // EXPERTS) ** 0.5), 160.0, (), jnp.float32)
    router_second = jnp.clip(jnp.exp(jax.random.uniform(streams_of[9], (MODEL_DIM, EXPERTS), jnp.float32, math.log(1572.48), math.log(20966.4))), 1572.48, 20966.4)
    projection_weight = noise(streams_of[10], (MODEL_DIM, KEY_HEADS, HEAD_PROJ_COLS), MODEL_DIM ** -0.5, 0.15625, ((0, 8), (1, 8)), jnp.float32)
    projection_first_moment = noise(streams_of[11], (MODEL_DIM, KEY_HEADS, HEAD_PROJ_COLS), (0.09 * TOKEN_TOTAL ** 0.5), 64.0, ((0, 8), (1, 8)), jnp.float32)
    projection_second_moment = jnp.clip(jnp.exp(math.log(4259.84) - 2.6162426 * jax.random.uniform(streams_of[12], (MODEL_DIM, KEY_HEADS, HEAD_PROJ_COLS), jnp.float32) ** levels(streams_of[12], (MODEL_DIM, KEY_HEADS, HEAD_PROJ_COLS), ((0, 8), (1, 8)), -0.2, 0.2)), 311.296, 4259.84)
    w_proj = noise(streams_of[13], (HQ * HEAD_SIZE, MODEL_DIM), (HQ * HEAD_SIZE // 64) ** -0.5, 1.25, ((0, 8), (1, 8)), jnp.float32)
    proj_first = noise(streams_of[14], (HQ * HEAD_SIZE, MODEL_DIM), (0.011 * TOKEN_TOTAL ** 0.5), 8.0, ((0, 8), (1, 8)), jnp.float32)
    proj_second = jnp.clip(jnp.exp(math.log(65.536) - 2.5902672 * jax.random.uniform(streams_of[15], (HQ * HEAD_SIZE, MODEL_DIM), jnp.float32) ** levels(streams_of[15], (HQ * HEAD_SIZE, MODEL_DIM), ((0, 8), (1, 8)), -0.2, 0.2)), 4.9152, 65.536)
    w_gate_up = noise(streams_of[16], (EXPERTS, MODEL_DIM, 2, FF), MODEL_DIM ** -0.5, 0.15625, ((0, 8), (1, 8), (3, 2)), jnp.float32)
    gate_up_first = noise(streams_of[17], (EXPERTS, MODEL_DIM, 2, FF), (0.055 * (TOKEN_TOTAL * TOP // EXPERTS) ** 0.5), 20.0, ((0, 8), (1, 8), (3, 2)), jnp.float32)
    gate_up_second = jnp.clip(jnp.exp(math.log(327.6) - 2.5902672 * jax.random.uniform(streams_of[18], (EXPERTS, MODEL_DIM, 2, FF), jnp.float32) ** levels(streams_of[18], (EXPERTS, MODEL_DIM, 2, FF), ((0, 8), (1, 8), (3, 2)), -0.2, 0.2)), 24.57, 327.6)
    w_down = noise(streams_of[19], (EXPERTS, FF, MODEL_DIM), (FF // 16) ** -0.5, 1.0, ((0, 8), (1, 2), (2, 8)), jnp.float32)
    down_first = noise(streams_of[20], (EXPERTS, FF, MODEL_DIM), (0.008 * (TOKEN_TOTAL * TOP // EXPERTS) ** 0.5), 2.5, ((0, 8), (1, 2), (2, 8)), jnp.float32)
    down_second = jnp.clip(jnp.exp(math.log(7.2072) - 2.62103878 * jax.random.uniform(streams_of[21], (EXPERTS, FF, MODEL_DIM), jnp.float32) ** levels(streams_of[21], (EXPERTS, FF, MODEL_DIM), ((0, 8), (1, 2), (2, 8)), -0.2, 0.2)), 0.52416, 7.2072)
    return {"tokens": tokens, "cotangent": cotangent, "lengths": lengths, "routes": routes, "norm_gains": norm_gains, "gain_first": gain_first, "gain_second": gain_second, "router_w": router_w, "router_first": router_first, "router_second": router_second, "projection_weight": projection_weight, "projection_first_moment": projection_first_moment, "projection_second_moment": projection_second_moment, "w_proj": w_proj, "proj_first": proj_first, "proj_second": proj_second, "w_gate_up": w_gate_up, "gate_up_first": gate_up_first, "gate_up_second": gate_up_second, "w_down": w_down, "down_first": down_first, "down_second": down_second}


@jax.custom_vjp
def reduced_form(v):
    return lax.optimization_barrier(v.astype(jnp.bfloat16)).astype(jnp.float32)

@jax.custom_vjp
def reduced_backward(v):
    return v

def low_keep(v):
    return (reduced_form(v), None)

def low_pass(kept, grad):
    return (grad,)

def back_keep(v):
    return (v, None)

def back_low(kept, grad):
    return (reduced_form(grad),)
reduced_form.defvjp(low_keep, low_pass)
reduced_backward.defvjp(back_keep, back_low)
EXACT_MATH = lax.Precision.HIGHEST
NORM_EPS = 1e-05
NEG_FILL = -1e+30
BETA_ONE = 0.9
BETA_TWO = 0.95
ADAM_EPS = 1e-08
DECAY_RATE = 0.1
RATE_GAIN = 0.5
RATE_ROUTER = 0.03
RATE_NARROW = 0.05
RATE_WIDE = 0.4

def inv_rms(values):
    return lax.rsqrt(lax.optimization_barrier(jnp.mean(values * values, axis=-1, keepdims=True)) + NORM_EPS)

def doc_index(lengths_row, token_places):
    doc_ends = jnp.cumsum(lengths_row).astype(jnp.int32)
    return lax.optimization_barrier(jnp.sum((token_places[:, None] >= doc_ends[None, :]).astype(jnp.int32), axis=1))

def slot_ranks(route_rows, experts):
    flat_ids = route_rows.reshape(-1)
    route_hits = (flat_ids[:, None] == jnp.arange(experts, dtype=jnp.int32)[None, :]).astype(jnp.int32)
    earlier = jnp.cumsum(route_hits, axis=0) - route_hits
    return (flat_ids, lax.optimization_barrier(jnp.sum(earlier * route_hits, axis=1)).astype(jnp.int32))

def adamw(weight, gradient, moment_one, moment_two, step_rate, weight_decay):
    first_new = BETA_ONE * moment_one + (1.0 - BETA_ONE) * gradient
    second_new = BETA_TWO * moment_two + (1.0 - BETA_TWO) * gradient * gradient
    boost_one = 1.0 / (1.0 - BETA_ONE ** STEP)
    boost_two = 1.0 / (1.0 - BETA_TWO ** STEP)
    direction = first_new * boost_one / (jnp.sqrt(second_new * boost_two) + ADAM_EPS)
    return (weight - step_rate * (direction + weight_decay * weight), first_new, second_new)

def group_layer(rows_in, norm_gains, router_w, projection_weight, w_proj, w_gate_up, w_down, lengths_row, route_rows):
    normalised_input = reduced_form(rows_in * inv_rms(rows_in) * norm_gains[0])
    projection_rows = jnp.dot(normalised_input, projection_weight.reshape(MODEL_DIM, KEY_HEADS * HEAD_PROJ_COLS), precision=EXACT_MATH).reshape(GROUP_TOKENS, KEY_HEADS, HEAD_PROJ_COLS)
    query_span_width = QUERY_PER_KEY * HEAD_SIZE
    query_rows = reduced_backward(reduced_form(projection_rows[:, :, :query_span_width])).reshape(GROUP_TOKENS, KEY_HEADS, QUERY_PER_KEY, HEAD_SIZE)
    key_rows = reduced_backward(reduced_form(projection_rows[:, :, query_span_width:query_span_width + HEAD_SIZE]))
    value_rows = reduced_backward(reduced_form(projection_rows[:, :, query_span_width + HEAD_SIZE:]))
    token_places = jnp.arange(GROUP_TOKENS, dtype=jnp.int32)
    document_index = doc_index(lengths_row, token_places)
    rows_per_block = min(512, GROUP_TOKENS)
    count_blocks = GROUP_TOKENS // rows_per_block
    score_scale = HEAD_SIZE ** (-0.5)

    def attend_heads(block_args):
        query_blk, doc_blk, spot_blk = block_args
        scores = jnp.einsum('ihgd,jhd->hgij', query_blk, key_rows, precision=EXACT_MATH) * score_scale
        scores = reduced_backward(scores)
        allowed = (doc_blk[:, None] == document_index[None, :]) & (spot_blk[:, None] >= token_places[None, :])
        scores = jnp.where(allowed[None, None], scores, NEG_FILL)
        attn_probs = reduced_form(jax.nn.softmax(scores, axis=-1))
        return jnp.einsum('hgij,jhd->ihgd', attn_probs, value_rows, precision=EXACT_MATH)
    visited_blocks = lax.map(jax.checkpoint(attend_heads), (query_rows.reshape(count_blocks, rows_per_block, KEY_HEADS, QUERY_PER_KEY, HEAD_SIZE), document_index.reshape(count_blocks, rows_per_block), token_places.reshape(count_blocks, rows_per_block)))
    attended = reduced_backward(reduced_form(visited_blocks.reshape(GROUP_TOKENS, HQ * HEAD_SIZE)))
    attn_out = reduced_backward(jnp.dot(attended, w_proj, precision=EXACT_MATH))
    residual = rows_in + attn_out
    normed_two = reduced_form(residual * inv_rms(residual) * norm_gains[1])
    logits = jnp.dot(normed_two, router_w, precision=EXACT_MATH)
    chosen = jnp.take_along_axis(logits, route_rows, axis=1)
    gate_probs = jax.nn.softmax(chosen, axis=-1)
    blocks_n = GROUP_TOKENS // TOK_DEV
    span = blocks_n * CAP
    flat_ids, slot_rank = jax.vmap(lambda part_rows: slot_ranks(part_rows, EXPERTS))(route_rows.reshape(blocks_n, TOK_DEV, TOP))
    rows_at = (flat_ids * span + jnp.arange(blocks_n, dtype=jnp.int32)[:, None] * CAP + slot_rank).reshape(-1).astype(jnp.int32)
    owners = jnp.repeat(jnp.arange(GROUP_TOKENS, dtype=jnp.int32), TOP).astype(jnp.int32)
    table = jnp.full((EXPERTS * span,), GROUP_TOKENS, jnp.int32).at[rows_at].set(owners)
    padded = jnp.concatenate([normed_two, jnp.zeros((1, MODEL_DIM), jnp.float32)], axis=0)

    def expert(block_args):
        row_ids, gate_up_w, down_w = block_args
        inputs = reduced_backward(padded[row_ids])
        gate_up = jnp.dot(inputs, gate_up_w.reshape(MODEL_DIM, 2 * FF), precision=EXACT_MATH)
        gate_pre = reduced_backward(gate_up[:, :FF])
        up_pre = reduced_backward(gate_up[:, FF:])
        hidden = reduced_form(jax.nn.silu(gate_pre) * up_pre)
        return reduced_backward(reduced_form(jnp.dot(hidden, down_w, precision=EXACT_MATH)))
    expert_outs = lax.map(jax.checkpoint(expert), (table.reshape(EXPERTS, span), w_gate_up, w_down))
    picked = expert_outs.reshape(EXPERTS * span, MODEL_DIM)[rows_at].reshape(GROUP_TOKENS, TOP, MODEL_DIM)
    mixture = lax.optimization_barrier(jnp.sum(gate_probs[:, :, None] * picked, axis=1))
    return residual + mixture

def reference(tokens, cotangent, lengths, routes, norm_gains, gain_first, gain_second, router_w, router_first, router_second, projection_weight, projection_first_moment, projection_second_moment, w_proj, proj_first, proj_second, w_gate_up, gate_up_first, gate_up_second, w_down, down_first, down_second):
    groups_n = TOKEN_TOTAL // GROUP_TOKENS

    def forward(tokens_f, gains_f, router_f, qkv_f, proj_f, gate_up_f, down_f):
        router_low = reduced_form(router_f)
        qkv_low = reduced_form(qkv_f)
        proj_low = reduced_form(proj_f)
        gate_up_low = reduced_form(gate_up_f)
        down_low = reduced_form(down_f)

        def one_group(running, group_args):
            rows_in, lengths_row, route_rows = group_args
            return (running, group_layer(rows_in, gains_f, router_low, qkv_low, proj_low, gate_up_low, down_low, lengths_row, route_rows))
        unused, outs = lax.scan(jax.checkpoint(one_group), jnp.zeros((), jnp.float32), (tokens_f.reshape(groups_n, GROUP_TOKENS, MODEL_DIM), lengths, routes.reshape(groups_n, GROUP_TOKENS, TOP)))
        return outs.reshape(TOKEN_TOTAL, MODEL_DIM)
    result, pullback = jax.vjp(forward, tokens.astype(jnp.float32), norm_gains, router_w, projection_weight, w_proj, w_gate_up, w_down)
    gradients = pullback(cotangent.astype(jnp.float32))
    dtokens, grad_gains, grad_router, grad_qkv, grad_proj, grad_gate_up, grad_down = gradients
    gain_new, gain_first_new, gain_second_new = adamw(norm_gains, grad_gains, gain_first, gain_second, RATE_GAIN, 0.0)
    router_new, router_first_new, router_second_new = adamw(router_w, grad_router, router_first, router_second, RATE_ROUTER, DECAY_RATE)
    qkv_new, qkv_first_new, qkv_second_new = adamw(projection_weight, grad_qkv, projection_first_moment, projection_second_moment, RATE_NARROW, DECAY_RATE)
    proj_new, proj_first_new, proj_second_new = adamw(w_proj, grad_proj, proj_first, proj_second, RATE_WIDE, DECAY_RATE)
    gate_up_new, gate_up_first_new, gate_up_second_new = adamw(w_gate_up, grad_gate_up, gate_up_first, gate_up_second, RATE_NARROW, DECAY_RATE)
    down_new, down_first_new, down_second_new = adamw(w_down, grad_down, down_first, down_second, RATE_WIDE, DECAY_RATE)
    return (result.astype(jnp.bfloat16), dtokens, gain_new, gain_first_new, gain_second_new, router_new, router_first_new, router_second_new, qkv_new, qkv_first_new, qkv_second_new, proj_new, proj_first_new, proj_second_new, gate_up_new, gate_up_first_new, gate_up_second_new, down_new, down_first_new, down_second_new)
```

```python
import functools

import jax
import jax.numpy as jnp
from jax import lax
from jax.experimental import pallas as pl
from jax.experimental.pallas import tpu as pltpu
from jax.sharding import PartitionSpec as P

HEAD_SIZE = 64
STEP = 10
QUERY_PER_KEY = 3
SPAN = QUERY_PER_KEY * HEAD_SIZE
QKV = SPAN + 2 * HEAD_SIZE
MODEL = 1536
ROWS = 128
STORED = 192
GROUP = 1024
PLANE = 2048
FF_DEV = 256
EXPERTS = 40
EXPERTS_DEV = 5
SLOTS = 112
TILE = 512
PAIR = 256
QUERY_TILE = 256
EXTRA = 128
CHUNKS = ((0, 1), (1, 2), (3, 2))

EXACT_MATH = lax.Precision.HIGHEST
NORM_EPS = 1e-05
NEG_FILL = -1e30
BETA_ONE = 0.9
BETA_TWO = 0.95
ADAM_EPS = 1e-08
DECAY_RATE = 0.1
RATE_GAIN = 0.5
RATE_ROUTER = 0.03
RATE_NARROW = 0.05
RATE_WIDE = 0.4
SCALE = HEAD_SIZE ** (-0.5)
F32 = jnp.float32
BF16 = jnp.bfloat16
VMEM_LIMIT = 60 * 1024 * 1024


def inv_rms(values):
    return lax.rsqrt(jnp.mean(values * values, axis=-1, keepdims=True) + NORM_EPS)


def adamw(weight, gradient, moment_one, moment_two, step_rate, weight_decay):
    first_new = BETA_ONE * moment_one + (1.0 - BETA_ONE) * gradient
    second_new = BETA_TWO * moment_two + (1.0 - BETA_TWO) * gradient * gradient
    boost_one = 1.0 / (1.0 - BETA_ONE**STEP)
    boost_two = 1.0 / (1.0 - BETA_TWO**STEP)
    direction = first_new * boost_one / (jnp.sqrt(second_new * boost_two) + ADAM_EPS)
    return (weight - step_rate * (direction + weight_decay * weight), first_new, second_new)


def norm_back(values, inverse, gain_row, upstream):
    normalized = values * inverse
    scaled = upstream * gain_row
    grad_gain = jnp.sum(upstream * normalized, axis=0)
    grad_values = inverse * (
        scaled - normalized * jnp.mean(scaled * normalized, axis=-1, keepdims=True)
    )
    return (grad_values, grad_gain)


def dot(a, b):
    return jnp.dot(a, b, preferred_element_type=F32)


def dot_nt(a, b):
    return lax.dot_general(a, b, (((1,), (1,)), ((), ())), preferred_element_type=F32)


def dot_tn(a, b):
    return lax.dot_general(a, b, (((0,), (0,)), ((), ())), preferred_element_type=F32)


def row_blocks(refs):
    blocks = []
    for ref in refs:
        for start in range(0, ref.shape[0], ROWS):
            blocks.append((ref, start))
    return blocks


def place(order_ref, block):
    return pl.ds(pl.multiple_of(order_ref[block] * ROWS, ROWS), ROWS)


def stored_rows(spread_ref, block):
    return pl.ds(pl.multiple_of(spread_ref[block] * STORED, STORED), STORED)


def visible(doc_row_ref, doc_col_ref, tile):
    keys = (tile + 1) * QUERY_TILE
    key_at = lax.broadcasted_iota(jnp.int32, (keys, QUERY_TILE), 0)
    query_at = lax.broadcasted_iota(jnp.int32, (keys, QUERY_TILE), 1) + tile * QUERY_TILE
    same = doc_col_ref[:keys, :] == doc_row_ref[:, tile * QUERY_TILE : keys]
    return same & (key_at <= query_at)


def attend_kernel(order_ref, spread_ref, doc_row_ref, doc_col_ref, *refs):
    normed_ref, w_ref, qkv_ref, att_ref, lse_ref, near_ref, far_ref = refs[-7:]
    pieces, weights = refs[:8], refs[8:-7]
    for block, (ref, start) in enumerate(row_blocks(pieces)):
        normed_ref[place(order_ref, block), :] = ref[start : start + ROWS, :]
    for block, ref in enumerate(weights):
        for other in range(2):
            w_ref[stored_rows(spread_ref, 2 * block + other), :] = ref[other]
    for tile in range(GROUP // QUERY_TILE):
        rows = slice(tile * QUERY_TILE, (tile + 1) * QUERY_TILE)
        qkv_ref[rows, :] = dot(normed_ref[rows, :], w_ref[...])[:, :QKV].astype(BF16)
    keys_all = qkv_ref[:, SPAN : SPAN + HEAD_SIZE]
    values_t = qkv_ref[:, SPAN + HEAD_SIZE : QKV].astype(F32).T.astype(BF16)
    lse_ref[...] = jnp.zeros_like(lse_ref)
    for tile in range(GROUP // QUERY_TILE):
        keys = (tile + 1) * QUERY_TILE
        rows = slice(tile * QUERY_TILE, keys)
        allowed = visible(doc_row_ref, doc_col_ref, tile)
        outs = [jnp.zeros((HEAD_SIZE, QUERY_TILE), F32)]
        for head in range(QUERY_PER_KEY):
            query = qkv_ref[rows, head * HEAD_SIZE : (head + 1) * HEAD_SIZE]
            scores = jnp.where(allowed, dot_nt(keys_all[:keys], query) * SCALE, NEG_FILL)
            peak = jnp.max(scores, axis=0, keepdims=True)
            weights = jnp.exp(scores - peak)
            total = jnp.sum(weights, axis=0, keepdims=True)
            probs = (weights * (1.0 / total)).astype(BF16)
            outs.append(dot(values_t[:, :keys], probs))
            lse_ref[head : head + 1, rows] = peak + jnp.log(total)
        att_ref[rows, :] = jnp.concatenate(outs, axis=0).T.astype(BF16)
    proj = w_ref[:, SPAN + HEAD_SIZE :]
    for block in range(GROUP // ROWS):
        part_ref = near_ref if block < 4 else far_ref
        part_ref[block % 4 * ROWS : (block % 4 + 1) * ROWS, :] = dot_nt(
            att_ref[place(order_ref, block), :], proj
        ).astype(BF16)


def attend_back_kernel(
    order_ref,
    spread_ref,
    doc_row_ref,
    doc_col_ref,
    gain_ref,
    w_ref,
    normed_ref,
    qkv_ref,
    att_ref,
    lse_ref,
    *refs,
):
    pieces, refs = refs[:8], refs[8:]
    near_ref, far_ref, *grads_refs, dgain_ref = refs[:7]
    dattn_ref, datt_ref, dqkv_ref, dkv_ref, whole_ref = refs[7:]
    for block, (ref, start) in enumerate(row_blocks(pieces)):
        dattn_ref[place(order_ref, block), :] = ref[start : start + ROWS, :]
    proj = w_ref[:, SPAN + HEAD_SIZE :]
    for tile in range(GROUP // QUERY_TILE):
        rows = slice(tile * QUERY_TILE, (tile + 1) * QUERY_TILE)
        datt_ref[rows, :] = dot(dattn_ref[rows, :], proj).astype(BF16)
    keys_all = qkv_ref[:, SPAN : SPAN + HEAD_SIZE]
    values_all = qkv_ref[:, SPAN + HEAD_SIZE : QKV]
    keys_t = keys_all.astype(F32).T.astype(BF16)
    dkv_ref[...] = jnp.zeros_like(dkv_ref)
    for tile in range(GROUP // QUERY_TILE):
        keys = (tile + 1) * QUERY_TILE
        rows = slice(tile * QUERY_TILE, keys)
        allowed = visible(doc_row_ref, doc_col_ref, tile)
        outs = []
        for head in range(QUERY_PER_KEY):
            query = qkv_ref[rows, head * HEAD_SIZE : (head + 1) * HEAD_SIZE]
            dout = datt_ref[rows, (head + 1) * HEAD_SIZE : (head + 2) * HEAD_SIZE]
            scores = jnp.where(allowed, dot_nt(keys_all[:keys], query) * SCALE, NEG_FILL)
            probs = jnp.exp(scores - lse_ref[head : head + 1, rows])
            dprobs = dot_nt(values_all[:keys], dout)
            shift = jnp.sum(probs * dprobs, axis=0, keepdims=True)
            dscores = (probs * (dprobs - shift)).astype(BF16)
            dkv_ref[:keys, :HEAD_SIZE] += dot(dscores, query)
            dkv_ref[:keys, HEAD_SIZE:] += dot(probs.astype(BF16), dout)
            outs.append(dot(keys_t[:, :keys], dscores))
        dqkv_ref[rows, :SPAN] = (jnp.concatenate(outs, axis=0).T * SCALE).astype(BF16)
    dqkv_ref[:, SPAN : SPAN + HEAD_SIZE] = (dkv_ref[:, :HEAD_SIZE] * SCALE).astype(BF16)
    dqkv_ref[:, SPAN + HEAD_SIZE :] = dkv_ref[:, HEAD_SIZE:].astype(BF16)
    qkv_mat = w_ref[:, :QKV]
    dgain = jnp.zeros((1, MODEL), F32)
    for block in range(GROUP // ROWS):
        at = place(order_ref, block)
        part = dot_nt(dqkv_ref[at, :], qkv_mat)
        dgain = dgain + jnp.sum(part * normed_ref[at, :].astype(F32), axis=0, keepdims=True)
        part_ref = near_ref if block < 4 else far_ref
        part_ref[block % 4 * ROWS : (block % 4 + 1) * ROWS, :] = part.astype(BF16)
    dgain_ref[...] = dgain / gain_ref[...]
    for start in range(0, MODEL, PAIR):
        cols = slice(start, start + PAIR)
        qkv_part = dot_tn(dqkv_ref[...], normed_ref[:, cols])
        proj_part = dot_tn(att_ref[...], dattn_ref[:, cols])[HEAD_SIZE:]
        whole_ref[cols, :] = jnp.concatenate([qkv_part, proj_part], axis=0).T.astype(BF16)
    for block in range(8):
        grads_refs[block // 2][block % 2] = whole_ref[stored_rows(spread_ref, block), :]


def vmem_spec():
    return pl.BlockSpec(memory_space=pltpu.VMEM)


def smem_spec():
    return pl.BlockSpec(memory_space=pltpu.SMEM)


def attend(order, spread, doc_row, doc_col, pieces, weights):
    return pl.pallas_call(
        attend_kernel,
        in_specs=[smem_spec()] * 2 + [vmem_spec()] * (2 + len(pieces) + len(weights)),
        out_specs=[vmem_spec()] * 7,
        out_shape=[
            jax.ShapeDtypeStruct((GROUP, MODEL), BF16),
            jax.ShapeDtypeStruct((MODEL, 2 * PAIR), BF16),
            jax.ShapeDtypeStruct((GROUP, QKV), BF16),
            jax.ShapeDtypeStruct((GROUP, PAIR), BF16),
            jax.ShapeDtypeStruct((8, GROUP), F32),
            jax.ShapeDtypeStruct((GROUP // 2, MODEL), BF16),
            jax.ShapeDtypeStruct((GROUP // 2, MODEL), BF16),
        ],
        compiler_params=pltpu.CompilerParams(vmem_limit_bytes=VMEM_LIMIT),
        cost_estimate=pl.CostEstimate(
            flops=4 * 10**9, bytes_accessed=12 * 10**6, transcendentals=2 * 10**6
        ),
        name="attend",
    )(order, spread, doc_row, doc_col, *pieces, *weights)


def attend_back(order, spread, doc_row, doc_col, gain, weights, normed, qkv, att, lse, pieces):
    return pl.pallas_call(
        attend_back_kernel,
        in_specs=[smem_spec()] * 2 + [vmem_spec()] * (8 + len(pieces)),
        out_specs=[vmem_spec()] * 7,
        out_shape=[
            jax.ShapeDtypeStruct((GROUP // 2, MODEL), BF16),
            jax.ShapeDtypeStruct((GROUP // 2, MODEL), BF16),
        ]
        + [jax.ShapeDtypeStruct((2, STORED, 2 * PAIR), BF16)] * 4
        + [
            jax.ShapeDtypeStruct((1, MODEL), F32),
        ],
        scratch_shapes=[
            pltpu.VMEM((GROUP, MODEL), BF16),
            pltpu.VMEM((GROUP, PAIR), BF16),
            pltpu.VMEM((GROUP, QKV), BF16),
            pltpu.VMEM((GROUP, 2 * HEAD_SIZE), F32),
            pltpu.VMEM((MODEL, 2 * PAIR), BF16),
        ],
        compiler_params=pltpu.CompilerParams(vmem_limit_bytes=VMEM_LIMIT),
        cost_estimate=pl.CostEstimate(
            flops=8 * 10**9, bytes_accessed=16 * 10**6, transcendentals=2 * 10**6
        ),
        name="attend_back",
    )(order, spread, doc_row, doc_col, gain, weights, normed, qkv, att, lse, *pieces)


def moe_kernel(first_ref, rank_ref, bias_ref, router_ref, w_ref, *refs, begin, count, more):
    sources, refs = (refs[:4], refs[4:8]), refs[8:]
    if more:
        prev_out_ref, prev_dn_ref = refs[:2]
        refs = refs[2:]
    out_ref, dn_ref, g_ref, in_all, dout_all, hid_all, dgu_all, held, sems = refs
    step = pl.program_id(0)
    last = PLANE // TILE - 1

    def copies(tile):
        return [
            pltpu.make_async_copy(
                sources[kind][tile], held.at[kind, tile % 2], sems.at[kind, tile % 2]
            )
            for kind in range(2)
        ]

    for tile in range(last + 1):

        @pl.when(step == max(tile - 1, 0))
        def _():
            for copy in copies(tile):
                copy.start()

    for tile in range(last + 1):

        @pl.when(step == tile)
        def _():
            for copy in copies(tile):
                copy.wait()

    t_ref, c_ref = held.at[0, lax.rem(step, 2)], held.at[1, lax.rem(step, 2)]
    pairs = TILE // PAIR
    height = pairs * SLOTS
    spot = pl.ds(pl.multiple_of(step * height, 16), height)
    logits = dot_nt(router_ref[...], t_ref[...]) + bias_ref[...]
    logits = jnp.exp(logits - jnp.max(logits, axis=0, keepdims=True))
    gates = logits / jnp.sum(logits, axis=0, keepdims=True)
    slot_at = lax.broadcasted_iota(jnp.int32, (SLOTS, PAIR), 0)
    picks, slot_gates, ins, cots = [], [], [], []
    for pair in range(pairs):
        cols = slice(pair * PAIR, (pair + 1) * PAIR)
        hits = [slot_at == rank_ref[pair, begin + e : begin + e + 1, :] for e in range(count)]
        slot_gates.append(
            [
                jnp.sum(
                    jnp.where(hits[e], gates[begin + e : begin + e + 1, cols], 0.0),
                    axis=1,
                    keepdims=True,
                )
                for e in range(count)
            ]
        )
        pick = jnp.concatenate([jnp.where(h, 1.0, 0.0).astype(BF16) for h in hits], axis=0)
        picks.append(pick)
        ins.append(dot(pick, t_ref[cols, :]).astype(BF16))
        cots.append(dot(pick, c_ref[cols, :]).astype(BF16))
    mixed = [[] for _ in range(pairs)]
    dins = [[] for _ in range(pairs)]
    lane = lax.broadcasted_iota(jnp.int32, (height, EXTRA), 1)
    for e in range(count):
        part = slice(e * SLOTS, (e + 1) * SLOTS)
        rows_in = jnp.concatenate([v[part] for v in ins], axis=0)
        rows_cot = jnp.concatenate([v[part] for v in cots], axis=0)
        gate = jnp.concatenate([v[e] for v in slot_gates], axis=0)
        gate_up_w = w_ref[:, e, :, : 2 * FF_DEV].reshape(MODEL, 2 * FF_DEV)
        down_w = w_ref[:, e, :, 2 * FF_DEV :].reshape(MODEL, FF_DEV)
        gate_up = dot(rows_in, gate_up_w)
        pre, up = gate_up[:, :FF_DEV], gate_up[:, FF_DEV:]
        sig = 1.0 / (1.0 + jnp.exp(-pre))
        silu = pre * sig
        hidden = (silu * up).astype(BF16)
        plain = dot(rows_cot, down_w)
        dgate = jnp.sum(hidden.astype(F32) * plain, axis=1, keepdims=True)
        dhidden = plain * gate
        dpre = dhidden * up * sig * (1.0 + pre * (1.0 - sig))
        dgu = jnp.concatenate([dpre, dhidden * silu], axis=1).astype(BF16)
        in_all[e, spot, :] = rows_in
        dout_all[e, spot, :] = (rows_cot.astype(F32) * gate).astype(BF16)
        hid_all[e, spot, :] = hidden
        dgu_all[e, spot, :] = dgu
        mix = (dot_nt(hidden, down_w) * gate).astype(BF16)
        din = dot_nt(dgu, gate_up_w).astype(BF16)
        high = dgate.astype(BF16).astype(F32)
        tail = jnp.where(lane == first_ref[0] + (begin + e), high, 0.0) + jnp.where(
            lane == first_ref[0] + (begin + e + EXPERTS), dgate - high, 0.0
        )
        din = jnp.concatenate([din, tail.astype(BF16)], axis=1)
        for pair in range(pairs):
            rows = slice(pair * SLOTS, (pair + 1) * SLOTS)
            mixed[pair].append(mix[rows])
            dins[pair].append(din[rows])
    for pair in range(pairs):
        cols = slice(pair * PAIR, (pair + 1) * PAIR)
        out = dot_tn(picks[pair], jnp.concatenate(mixed[pair], axis=0))
        dn = dot_tn(picks[pair], jnp.concatenate(dins[pair], axis=0))
        if more:
            out = out + prev_out_ref[cols, :].astype(F32)
            dn = dn + prev_dn_ref[cols, :].astype(F32)
        out_ref[cols, :] = out.astype(BF16)
        dn_ref[cols, :] = dn.astype(BF16)

    @pl.when(step == last)
    def _():
        for e in range(count):
            for start in range(0, MODEL, 2 * 192):
                cols = slice(start, start + 384)
                gate_up_g = dot_tn(in_all[e, :, cols], dgu_all[e])
                down_g = dot_tn(dout_all[e, :, cols], hid_all[e])
                both = jnp.concatenate([gate_up_g, down_g], axis=1).astype(BF16)
                for half in range(2):
                    g_ref[start // 192 + half, e, :, :] = both[half * 192 : (half + 1) * 192, :]


def moe(chunk, first, rank, bias, router_t, weights, rows, cots, previous):
    begin, count = chunk
    height = PLANE // PAIR * SLOTS
    wide = pl.BlockSpec((TILE, MODEL), lambda i: (i, 0))
    wider = pl.BlockSpec((TILE, MODEL + EXTRA), lambda i: (i, 0))
    whole = pl.BlockSpec((8, count, 192, 3 * FF_DEV), lambda i: (0, 0, 0, 0), pipeline_mode=pl.Buffered(1))
    flops = 2 * count * height * MODEL * (9 * FF_DEV + 5 * PAIR)
    return pl.pallas_call(
        functools.partial(moe_kernel, begin=begin, count=count, more=previous is not None),
        grid=(PLANE // TILE,),
        in_specs=[
            smem_spec(),
            pl.BlockSpec((TILE // PAIR, 8, PAIR), lambda i: (i, 0, 0)),
            pl.BlockSpec((EXPERTS, TILE), lambda i: (0, i)),
            pl.BlockSpec((EXPERTS, MODEL), lambda i: (0, 0)),
            whole,
        ]
        + [pl.BlockSpec(memory_space=pl.ANY)] * 8
        + ([wide, wider] if previous is not None else []),
        out_specs=[wide, wider, pl.BlockSpec((8, count, 192, 3 * FF_DEV), lambda i: (0, 0, 0, 0))],
        out_shape=[
            jax.ShapeDtypeStruct((PLANE, MODEL), BF16),
            jax.ShapeDtypeStruct((PLANE, MODEL + EXTRA), BF16),
            jax.ShapeDtypeStruct((8, count, 192, 3 * FF_DEV), BF16),
        ],
        scratch_shapes=[
            pltpu.VMEM((count, height, MODEL), BF16),
            pltpu.VMEM((count, height, MODEL), BF16),
            pltpu.VMEM((count, height, FF_DEV), BF16),
            pltpu.VMEM((count, height, 2 * FF_DEV), BF16),
            pltpu.VMEM((2, 2, TILE, MODEL), BF16),
            pltpu.SemaphoreType.DMA((2, 2)),
        ],
        compiler_params=pltpu.CompilerParams(vmem_limit_bytes=VMEM_LIMIT),
        cost_estimate=pl.CostEstimate(
            flops=flops, bytes_accessed=50 * 10**6, transcendentals=count * height * FF_DEV
        ),
        name="moe",
    )(first, rank, bias, router_t, weights, *rows, *cots, *(previous or ()))


def slot_tables(routes_all, col):
    ids = jnp.remainder(routes_all - EXPERTS_DEV * col, EXPERTS)
    hits = jnp.any(ids[None] == jnp.arange(EXPERTS, dtype=jnp.int32)[:, None, None], axis=-1)
    bias = jnp.where(hits, 0.0, NEG_FILL).astype(F32)
    local = hits[:EXPERTS_DEV].reshape(EXPERTS_DEV, PLANE // PAIR, PAIR)
    upto = jnp.arange(PAIR)[:, None] <= jnp.arange(PAIR)[None, :]
    counts = jnp.einsum(
        "epi,ij->pej", local.astype(BF16), upto.astype(BF16), preferred_element_type=F32
    ).astype(jnp.int32)
    rank = jnp.where(local.transpose(1, 0, 2), counts - 1, -1)
    rank = jnp.pad(rank, ((0, 0), (0, 8 - EXPERTS_DEV), (0, 0)), constant_values=-1)
    return bias, rank


def across_col(value, distance):
    pairs = [(2 * x + c, 2 * ((x + distance) % 4) + c) for x in range(4) for c in range(2)]
    return lax.ppermute(value, "col", pairs)


def other_core(value):
    return lax.ppermute(value, "col", [(s, s ^ 1) for s in range(8)])


def other_row(value):
    return lax.ppermute(value, "row", [(0, 1), (1, 0)])


def along_z(value, distance):
    pairs = [(4 * y + z, 4 * y + (z + distance) % 4) for y in range(2) for z in range(4)]
    return lax.ppermute(value, "dp", pairs)


def other_y(value):
    return lax.ppermute(value, "dp", [(s, s ^ 4) for s in range(8)])


def total(values):
    result = values[0].astype(F32)
    for value in values[1:]:
        result = result + value.astype(F32)
    return result


def gather_col(value):
    near = [value] + [across_col(value, d) for d in (1, 2, 3)]
    return near + [other_core(v) for v in near]


def gather_plane(value):
    near = []
    for mine in (value, other_row(value)):
        near.append(jnp.concatenate([mine] + [across_col(mine, d) for d in (1, 2, 3)], axis=0))
    return near + [other_core(v) for v in near]


def scatter_blocks(near, far):
    blocks = [
        total([near[d * ROWS : (d + 1) * ROWS], far[d * ROWS : (d + 1) * ROWS]]) for d in range(4)
    ]
    return [blocks[0]] + [across_col(blocks[d].astype(BF16), -d) for d in (1, 2, 3)]


def scatter_col(near, far):
    return total(scatter_blocks(near, other_core(far)))


def scatter_plane(value):
    half = value.shape[0] // 2
    quarter = half // 2
    far = other_core(value[half:])
    theirs = total(scatter_blocks(value[quarter:half], far[quarter:]))
    mine = total(scatter_blocks(value[:quarter], far[:quarter]))
    return mine + other_row(theirs.astype(BF16)).astype(F32)


def gather_dp(value):
    both = jnp.stack([value, other_y(value)])
    return [both] + [along_z(both, d) for d in (1, 2, 3)]


def scatter_dp(values):
    both = total([values[0]] + [along_z(values[d], -d) for d in (1, 2, 3)])
    mine = (both[0] + other_y(both[1].astype(BF16)).astype(F32)).astype(BF16)
    return total([mine, other_row(mine)])


def sum_all(value):
    value = value + other_core(value)
    value = value + across_col(value, 2)
    value = value + lax.ppermute(value, "col", [(s, s ^ 2) for s in range(8)])
    value = value + other_row(value)
    value = value + other_y(value)
    value = value + along_z(value, 2)
    return value + lax.ppermute(value, "dp", [(s, s ^ 1) for s in range(8)])


def per_device(
    tokens,
    cotangent,
    lengths,
    routes,
    norm_gains,
    gain_first,
    gain_second,
    router_w,
    router_first,
    router_second,
    projection_weight,
    projection_first_moment,
    projection_second_moment,
    w_proj,
    proj_first,
    proj_second,
    w_gate_up,
    gate_up_first,
    gate_up_second,
    w_down,
    down_first,
    down_second,
):
    col, row, dp = lax.axis_index("col"), lax.axis_index("row"), lax.axis_index("dp")
    across, core = col // 2, col % 2
    attn_w = jnp.concatenate([projection_weight[:, 0, :], w_proj.T], axis=1).astype(BF16)
    attn_pieces = gather_dp(attn_w)
    expert_w = jnp.concatenate(
        [w_gate_up.reshape(EXPERTS_DEV, 192, 2 * FF_DEV), w_down.transpose(0, 2, 1)], axis=2
    ).astype(BF16)
    expert_ws = [
        lax.all_gather(expert_w[b : b + n], "dp", axis=0, tiled=False) for b, n in CHUNKS
    ]

    residual_in = tokens.astype(F32)
    inverse_one = inv_rms(residual_in)
    normed_one = (residual_in * inverse_one * norm_gains[0]).astype(BF16)
    normed_pieces = gather_col(normed_one)
    steps = jnp.arange(4, dtype=jnp.int32)
    away = 2 * jnp.remainder(across - steps, 4)
    order = jnp.concatenate([away + core, away + 1 - core])
    spread = (
        jnp.remainder(dp % 4 - steps, 4)[:, None]
        + 4 * jnp.stack([dp // 4, 1 - dp // 4]).astype(jnp.int32)[None, :]
    ).reshape(-1)
    token_places = jnp.arange(GROUP, dtype=jnp.int32)
    doc_ends = jnp.cumsum(lengths[0])
    documents = jnp.sum((token_places[:, None] >= doc_ends[None, :]).astype(jnp.int32), axis=1)
    doc_row, doc_col = documents[None, :], documents[:, None]
    normed_full, attn_full, qkv, att, lse, *attn_parts = attend(
        order, spread, doc_row, doc_col, normed_pieces, attn_pieces
    )
    attn_out = scatter_col(*attn_parts)

    cot_ready, _ = lax.optimization_barrier((cotangent, normed_pieces))
    cots = gather_plane(cot_ready)
    routes_all = lax.all_gather(routes, ("row", "col"), axis=0, tiled=False)
    plane = jnp.stack([row * 8, (1 - row) * 8])[None, :, None] + order.reshape(2, 1, 4)
    routes_all = routes_all[plane.reshape(-1)].reshape(PLANE, -1)

    residual = residual_in + attn_out
    inverse_two = inv_rms(residual)
    normed_two = (residual * inverse_two * norm_gains[1]).astype(BF16)
    rows_all = gather_plane(normed_two)
    router_low = router_w.astype(BF16)
    bias, rank = slot_tables(routes_all, col)
    router_t = jnp.roll(router_low.T, -EXPERTS_DEV * col, axis=0)
    first = (EXPERTS_DEV * col).astype(jnp.int32).reshape(1)
    previous = None
    expert_grads = []
    for chunk, weights in zip(CHUNKS, expert_ws):
        *previous, grads = moe(chunk, first, rank, bias, router_t, weights, rows_all, cots, previous)
        expert_grads.append(grads)
    mix_part, dn_part = previous
    dn = scatter_plane(dn_part)
    mix_part, _ = lax.optimization_barrier((mix_part, dn))
    mixture = scatter_plane(mix_part)
    expert_sums = [
        lax.psum_scatter(g, "dp", scatter_dimension=0, tiled=False) for g in expert_grads
    ]
    output = (residual + mixture).astype(BF16)

    logits = jnp.dot(normed_two, router_low, preferred_element_type=F32)
    route_hits = jnp.any(
        routes[:, None, :] == jnp.arange(EXPERTS, dtype=jnp.int32)[None, :, None], axis=-1
    )
    gates = jax.nn.softmax(jnp.where(route_hits, logits, NEG_FILL), axis=-1)
    dgate = dn[:, MODEL : MODEL + EXPERTS] + dn[:, MODEL + EXPERTS : MODEL + 2 * EXPERTS]
    dlogits = gates * (dgate - jnp.sum(gates * dgate, axis=-1, keepdims=True))
    dnormed_two = dn[:, :MODEL] + jnp.dot(dlogits, router_low.astype(F32).T, precision=EXACT_MATH)
    grad_router = lax.dot_general(
        dlogits, normed_two.astype(F32), (((0,), (0,)), ((), ())), precision=EXACT_MATH
    )
    upstream = cotangent.astype(F32)
    dresid_norm, grad_gain_two = norm_back(residual, inverse_two, norm_gains[1], dnormed_two)
    dresidual = upstream + dresid_norm
    dattn_pieces = gather_col(dresidual.astype(BF16))
    near, far, *attn_grads, grad_gain_one = attend_back(
        order,
        spread,
        doc_row,
        doc_col,
        norm_gains[:1],
        attn_full,
        normed_full,
        qkv,
        att,
        lse,
        dattn_pieces,
    )
    dnormed = scatter_col(near, far)
    dtokens_norm, _ = norm_back(residual_in, inverse_one, norm_gains[0], dnormed)
    dtokens = dresidual + dtokens_norm
    attn_sums = scatter_dp(attn_grads)
    early = sum_all(jnp.concatenate([grad_router, grad_gain_two[None]], axis=0))
    sum_router = early[:EXPERTS].T
    sum_gains = jnp.concatenate([sum_all(grad_gain_one), early[EXPERTS:]], axis=0)
    sum_qkv = attn_sums[:, None, :QKV]
    sum_proj = attn_sums[:, QKV:].T
    expert_sum = jnp.concatenate(expert_sums, axis=0).astype(F32)
    sum_gate_up = expert_sum[:, :, : 2 * FF_DEV].reshape(EXPERTS_DEV, 192, 2, FF_DEV)
    sum_down = expert_sum[:, :, 2 * FF_DEV :].transpose(0, 2, 1)
    return (
        output,
        dtokens,
        *adamw(norm_gains, sum_gains, gain_first, gain_second, RATE_GAIN, 0.0),
        *adamw(router_w, sum_router, router_first, router_second, RATE_ROUTER, DECAY_RATE),
        *adamw(
            projection_weight,
            sum_qkv,
            projection_first_moment,
            projection_second_moment,
            RATE_NARROW,
            DECAY_RATE,
        ),
        *adamw(w_proj, sum_proj, proj_first, proj_second, RATE_WIDE, DECAY_RATE),
        *adamw(w_gate_up, sum_gate_up, gate_up_first, gate_up_second, RATE_NARROW, DECAY_RATE),
        *adamw(w_down, sum_down, down_first, down_second, RATE_WIDE, DECAY_RATE),
    )


def solution(mesh):
    by_token = P(("dp", "row", "col"), None)
    qkv_at, proj_at = P("dp", "col", None), P("col", "dp")
    gate_up_at, down_at = P("col", "dp", None, "row"), P("col", "row", "dp")
    return jax.shard_map(
        per_device,
        mesh=mesh,
        in_specs=(by_token, by_token, P(("dp", "row"), None), by_token)
        + (P(),) * 6
        + (qkv_at,) * 3
        + (proj_at,) * 3
        + (gate_up_at,) * 3
        + (down_at,) * 3,
        out_specs=(by_token, by_token)
        + (P(),) * 6
        + (qkv_at,) * 3
        + (proj_at,) * 3
        + (gate_up_at,) * 3
        + (down_at,) * 3,
        check_vma=False,
    )
```

```python
import functools

import jax
import jax.numpy as jnp
from jax import lax
from jax.experimental import pallas as pl
from jax.experimental.pallas import tpu as pltpu
from jax.sharding import PartitionSpec as P

HEAD_SIZE = 64
STEP = 10
QUERY_PER_KEY = 3
SPAN = QUERY_PER_KEY * HEAD_SIZE
QKV = SPAN + 2 * HEAD_SIZE
MODEL = 1536
ROWS = 128
STORED = 192
GROUP = 1024
PLANE = 2048
FF_DEV = 256
EXPERTS = 40
EXPERTS_DEV = 5
TOP = 8
SLOTS = 112
TILE = 512
PAIR = 256
QUERY_TILE = 256
EXTRA = 128
SMALL = 48
CHUNKS = ((0, 3), (3, 2))

EXACT_MATH = lax.Precision.HIGHEST
NORM_EPS = 1e-05
NEG_FILL = -1e30
BETA_ONE = 0.9
BETA_TWO = 0.95
ADAM_EPS = 1e-08
DECAY_RATE = 0.1
RATE_GAIN = 0.5
RATE_ROUTER = 0.03
RATE_NARROW = 0.05
RATE_WIDE = 0.4
SCALE = HEAD_SIZE ** (-0.5)
F32 = jnp.float32
BF16 = jnp.bfloat16
VMEM_LIMIT = 60 * 1024 * 1024


def row_pairs(stored):
    parts = stored.reshape(EXPERTS_DEV, STORED, 2, FF_DEV // 128, 128)
    return parts.transpose(0, 1, 3, 2, 4).reshape(-1, 128)


def paired_rows(rows):
    parts = rows.reshape(EXPERTS_DEV, STORED, FF_DEV // 128, 2, 128)
    return parts.transpose(0, 1, 3, 2, 4).reshape(EXPERTS_DEV, STORED, 2, FF_DEV)


def adamw_kernel(g_ref, *refs):
    olds, news = refs[:6], refs[6:]
    for half in range(FF_DEV // 128):
        for kind in range(2):
            at = pl.ds(2 * half + kind, STORED, stride=4)
            start = kind * FF_DEV + half * 128
            gradient = g_ref[0, :, start : start + 128].astype(F32)
            weight, first, second = (ref[at, :] for ref in olds[:3])
            results = adamw(weight, gradient, first, second, RATE_NARROW, DECAY_RATE)
            for ref, result in zip(news[:3], results):
                ref[at, :] = result
    gradient = g_ref[0, :, 2 * FF_DEV :].astype(F32)
    weight, first, second = (ref[0] for ref in olds[3:])
    results = adamw(weight, gradient, first, second, RATE_WIDE, DECAY_RATE)
    for ref, result in zip(news[3:], results):
        ref[0] = result


def update_experts(gradient, gate_up, down):
    pair_rows = pl.BlockSpec((4 * STORED, 128), lambda i: (i, 0))
    down_rows = pl.BlockSpec((1, STORED, FF_DEV), lambda i: (i, 0, 0))
    specs = [pair_rows] * 3 + [down_rows] * 3
    pair_shape = jax.ShapeDtypeStruct((EXPERTS_DEV * 4 * STORED, 128), F32)
    down_shape = jax.ShapeDtypeStruct((EXPERTS_DEV, STORED, FF_DEV), F32)
    new = pl.pallas_call(
        adamw_kernel,
        grid=(EXPERTS_DEV,),
        in_specs=[pl.BlockSpec((1, STORED, 3 * FF_DEV), lambda i: (i, 0, 0))] + specs,
        out_specs=specs,
        out_shape=[pair_shape] * 3 + [down_shape] * 3,
        cost_estimate=pl.CostEstimate(
            flops=20 * 10**6, bytes_accessed=20 * 10**6, transcendentals=10**6
        ),
        name="update_experts",
    )(gradient, *[row_pairs(v) for v in gate_up], *[v.transpose(0, 2, 1) for v in down])
    return [paired_rows(v) for v in new[:3]] + [v.transpose(0, 2, 1) for v in new[3:]]


def inv_rms(values):
    return lax.rsqrt(jnp.mean(values * values, axis=-1, keepdims=True) + NORM_EPS)


def adamw(weight, gradient, moment_one, moment_two, step_rate, weight_decay):
    first_new = BETA_ONE * moment_one + (1.0 - BETA_ONE) * gradient
    second_new = BETA_TWO * moment_two + (1.0 - BETA_TWO) * gradient * gradient
    boost_one = 1.0 / (1.0 - BETA_ONE**STEP)
    boost_two = 1.0 / (1.0 - BETA_TWO**STEP)
    direction = first_new * boost_one / (jnp.sqrt(second_new * boost_two) + ADAM_EPS)
    return (weight - step_rate * (direction + weight_decay * weight), first_new, second_new)


def norm_back(values, inverse, gain_row, upstream):
    normalized = values * inverse
    scaled = upstream * gain_row
    grad_gain = jnp.sum(upstream * normalized, axis=0)
    grad_values = inverse * (
        scaled - normalized * jnp.mean(scaled * normalized, axis=-1, keepdims=True)
    )
    return (grad_values, grad_gain)


def dot(a, b):
    return jnp.dot(a, b, preferred_element_type=F32)


def dot_nt(a, b):
    return lax.dot_general(a, b, (((1,), (1,)), ((), ())), preferred_element_type=F32)


def dot_tn(a, b):
    return lax.dot_general(a, b, (((0,), (0,)), ((), ())), preferred_element_type=F32)


def row_blocks(refs):
    blocks = []
    for ref in refs:
        for start in range(0, ref.shape[0], ROWS):
            blocks.append((ref, start))
    return blocks


def place(order_ref, block):
    return pl.ds(pl.multiple_of(order_ref[block] * ROWS, ROWS), ROWS)


def stored_rows(spread_ref, block):
    return pl.ds(pl.multiple_of(spread_ref[block] * STORED, STORED), STORED)


def visible(doc_row_ref, doc_col_ref, tile):
    keys = (tile + 1) * QUERY_TILE
    key_at = lax.broadcasted_iota(jnp.int32, (keys, QUERY_TILE), 0)
    query_at = lax.broadcasted_iota(jnp.int32, (keys, QUERY_TILE), 1) + tile * QUERY_TILE
    same = doc_col_ref[:keys, :] == doc_row_ref[:, tile * QUERY_TILE : keys]
    return same & (key_at <= query_at)


def attend_kernel(order_ref, doc_row_ref, doc_col_ref, *refs):
    normed_ref, qkv_ref, att_ref, lse_ref, near_ref, far_ref = refs[-6:]
    pieces, w_ref = refs[:8], refs[8]
    for block, (ref, start) in enumerate(row_blocks(pieces)):
        normed_ref[place(order_ref, block), :] = ref[start : start + ROWS, :]
    for tile in range(GROUP // QUERY_TILE):
        rows = slice(tile * QUERY_TILE, (tile + 1) * QUERY_TILE)
        qkv_ref[rows, :] = dot(normed_ref[rows, :], w_ref[...])[:, :QKV].astype(BF16)
    keys_all = qkv_ref[:, SPAN : SPAN + HEAD_SIZE]
    values_t = qkv_ref[:, SPAN + HEAD_SIZE : QKV].astype(F32).T.astype(BF16)
    lse_ref[...] = jnp.zeros_like(lse_ref)
    for tile in range(GROUP // QUERY_TILE):
        keys = (tile + 1) * QUERY_TILE
        rows = slice(tile * QUERY_TILE, keys)
        allowed = visible(doc_row_ref, doc_col_ref, tile)
        outs = [jnp.zeros((HEAD_SIZE, QUERY_TILE), F32)]
        for head in range(QUERY_PER_KEY):
            query = qkv_ref[rows, head * HEAD_SIZE : (head + 1) * HEAD_SIZE]
            scores = jnp.where(allowed, dot_nt(keys_all[:keys], query) * SCALE, NEG_FILL)
            peak = jnp.max(scores, axis=0, keepdims=True)
            weights = jnp.exp(scores - peak)
            total = jnp.sum(weights, axis=0, keepdims=True)
            probs = (weights * (1.0 / total)).astype(BF16)
            outs.append(dot(values_t[:, :keys], probs))
            lse_ref[head : head + 1, rows] = peak + jnp.log(total)
        att_ref[rows, :] = jnp.concatenate(outs, axis=0).T.astype(BF16)
    proj = w_ref[:, SPAN + HEAD_SIZE :]
    for block in range(GROUP // ROWS):
        part_ref = near_ref if block < 4 else far_ref
        part_ref[block % 4 * ROWS : (block % 4 + 1) * ROWS, :] = dot_nt(
            att_ref[place(order_ref, block), :], proj
        ).astype(BF16)


def attend_back_kernel(
    order_ref,
    spread_ref,
    doc_row_ref,
    doc_col_ref,
    gain_ref,
    small_ref,
    w_ref,
    normed_ref,
    qkv_ref,
    att_ref,
    lse_ref,
    *refs,
):
    pieces, refs = refs[:8], refs[8:]
    near_ref, far_ref, *grads_refs = refs[:4]
    dattn_ref, datt_ref, dqkv_ref, dkv_ref, whole_ref = refs[4:]
    for block, (ref, start) in enumerate(row_blocks(pieces)):
        dattn_ref[place(order_ref, block), :] = ref[start : start + ROWS, :]
    proj = w_ref[:, SPAN + HEAD_SIZE :]
    for tile in range(GROUP // QUERY_TILE):
        rows = slice(tile * QUERY_TILE, (tile + 1) * QUERY_TILE)
        datt_ref[rows, :] = dot(dattn_ref[rows, :], proj).astype(BF16)
    keys_all = qkv_ref[:, SPAN : SPAN + HEAD_SIZE]
    values_all = qkv_ref[:, SPAN + HEAD_SIZE : QKV]
    keys_t = keys_all.astype(F32).T.astype(BF16)
    dkv_ref[...] = jnp.zeros_like(dkv_ref)
    for tile in range(GROUP // QUERY_TILE):
        keys = (tile + 1) * QUERY_TILE
        rows = slice(tile * QUERY_TILE, keys)
        allowed = visible(doc_row_ref, doc_col_ref, tile)
        outs = []
        for head in range(QUERY_PER_KEY):
            query = qkv_ref[rows, head * HEAD_SIZE : (head + 1) * HEAD_SIZE]
            dout = datt_ref[rows, (head + 1) * HEAD_SIZE : (head + 2) * HEAD_SIZE]
            scores = jnp.where(allowed, dot_nt(keys_all[:keys], query) * SCALE, NEG_FILL)
            probs = jnp.exp(scores - lse_ref[head : head + 1, rows])
            dprobs = dot_nt(values_all[:keys], dout)
            shift = jnp.sum(probs * dprobs, axis=0, keepdims=True)
            dscores = (probs * (dprobs - shift)).astype(BF16)
            dkv_ref[:keys, :HEAD_SIZE] += dot(dscores, query)
            dkv_ref[:keys, HEAD_SIZE:] += dot(probs.astype(BF16), dout)
            outs.append(dot(keys_t[:, :keys], dscores))
        dqkv_ref[rows, :SPAN] = (jnp.concatenate(outs, axis=0).T * SCALE).astype(BF16)
    dqkv_ref[:, SPAN : SPAN + HEAD_SIZE] = (dkv_ref[:, :HEAD_SIZE] * SCALE).astype(BF16)
    dqkv_ref[:, SPAN + HEAD_SIZE :] = dkv_ref[:, HEAD_SIZE:].astype(BF16)
    qkv_mat = w_ref[:, :QKV]
    dgain = jnp.zeros((1, MODEL), F32)
    for block in range(GROUP // ROWS):
        at = place(order_ref, block)
        part = dot_nt(dqkv_ref[at, :], qkv_mat)
        dgain = dgain + jnp.sum(part * normed_ref[at, :].astype(F32), axis=0, keepdims=True)
        part_ref = near_ref if block < 4 else far_ref
        part_ref[block % 4 * ROWS : (block % 4 + 1) * ROWS, :] = part.astype(BF16)
    small_at = lax.broadcasted_iota(jnp.int32, (SMALL, MODEL), 0)
    small = jnp.where(small_at == EXPERTS + 1, dgain / gain_ref[...], small_ref[...])
    far_ref[GROUP // 2 :, :] = small.astype(BF16)
    for start in range(0, MODEL, PAIR):
        cols = slice(start, start + PAIR)
        qkv_part = dot_tn(dqkv_ref[...], normed_ref[:, cols])
        proj_part = dot_tn(att_ref[...], dattn_ref[:, cols])[HEAD_SIZE:]
        both = jnp.concatenate([qkv_part, proj_part], axis=0)
        whole_ref[cols, :] = both.T.astype(BF16)
    for block in range(8):
        grads_refs[block // 4][block % 4] = whole_ref[stored_rows(spread_ref, block), :]


def vmem_spec():
    return pl.BlockSpec(memory_space=pltpu.VMEM)


def smem_spec():
    return pl.BlockSpec(memory_space=pltpu.SMEM)


def attend(order, doc_row, doc_col, pieces, weights):
    return pl.pallas_call(
        attend_kernel,
        in_specs=[smem_spec()] + [vmem_spec()] * (3 + len(pieces)),
        out_specs=[vmem_spec()] * 6,
        out_shape=[
            jax.ShapeDtypeStruct((GROUP, MODEL), BF16),
            jax.ShapeDtypeStruct((GROUP, QKV), BF16),
            jax.ShapeDtypeStruct((GROUP, PAIR), BF16),
            jax.ShapeDtypeStruct((8, GROUP), F32),
            jax.ShapeDtypeStruct((GROUP // 2, MODEL), BF16),
            jax.ShapeDtypeStruct((GROUP // 2, MODEL), BF16),
        ],
        compiler_params=pltpu.CompilerParams(vmem_limit_bytes=VMEM_LIMIT),
        cost_estimate=pl.CostEstimate(
            flops=10**6, bytes_accessed=10**5, transcendentals=0
        ),
        name="attend",
    )(order, doc_row, doc_col, *pieces, weights)


def attend_back(order, spread, doc_row, doc_col, gain, small, weights, normed, qkv, att, lse, pieces):
    return pl.pallas_call(
        attend_back_kernel,
        in_specs=[smem_spec()] * 2 + [vmem_spec()] * (9 + len(pieces)),
        out_specs=[vmem_spec()] * 4,
        out_shape=[
            jax.ShapeDtypeStruct((GROUP // 2, MODEL), BF16),
            jax.ShapeDtypeStruct((GROUP // 2 + SMALL, MODEL), BF16),
        ]
        + [jax.ShapeDtypeStruct((4, STORED, 2 * PAIR), BF16)] * 2,
        scratch_shapes=[
            pltpu.VMEM((GROUP, MODEL), BF16),
            pltpu.VMEM((GROUP, PAIR), BF16),
            pltpu.VMEM((GROUP, QKV), BF16),
            pltpu.VMEM((GROUP, 2 * HEAD_SIZE), F32),
            pltpu.VMEM((MODEL, 2 * PAIR), BF16),
        ],
        compiler_params=pltpu.CompilerParams(vmem_limit_bytes=VMEM_LIMIT),
        cost_estimate=pl.CostEstimate(
            flops=10**6, bytes_accessed=10**5, transcendentals=0
        ),
        name="attend_back",
    )(order, spread, doc_row, doc_col, gain, small, weights, normed, qkv, att, lse, *pieces)


def moe_kernel(first_ref, router_ref, w_ref, *refs, begin, count, more):
    sources, refs = (refs[:4], refs[4:8]), refs[8:]
    if more:
        prev_out_ref, prev_dn_ref = refs[:2]
        refs = refs[3:]
        outs, refs = (refs[:2], refs[2:4]), refs[4:]
    else:
        out_ref, dn_ref = refs[:2]
        refs = refs[2:]
    g_ref, in_all, dout_all, hid_all, dgu_all, held_t, held_c, sems, done, done_sems = refs
    step = pl.program_id(0)
    pairs = TILE // PAIR
    height = pairs * SLOTS
    last = PLANE // TILE - 1

    def copies(tile):
        return [
            pltpu.make_async_copy(
                sources[kind][tile], held.at[tile % 2], sems.at[kind, tile % 2]
            )
            for kind, held in enumerate((held_t, held_c))
        ]

    for tile in range(last + 1):

        @pl.when(step == max(tile - 1, 0))
        def _():
            for copy in copies(tile):
                copy.start()

    for tile in range(last + 1):

        @pl.when(step == tile)
        def _():
            for copy in copies(tile):
                copy.wait()

    t_ref, c_ref = held_t.at[lax.rem(step, 2)], held_c.at[lax.rem(step, 2)]
    ids = c_ref[:, MODEL:].astype(F32).T.astype(jnp.int32)
    expert_at = lax.broadcasted_iota(jnp.int32, (EXPERTS, TILE), 0) + first_ref[0]
    expert_at = jnp.where(expert_at >= EXPERTS, expert_at - EXPERTS, expert_at)
    hits = ids[:1] == expert_at
    for choice in range(1, TOP):
        hits = hits | (ids[choice : choice + 1] == expert_at)
    mine = jnp.where(hits[:8], 1.0, 0.0)
    upto = lax.broadcasted_iota(jnp.int32, (PAIR, PAIR), 0) <= lax.broadcasted_iota(
        jnp.int32, (PAIR, PAIR), 1
    )
    upto = jnp.where(upto, 1.0, 0.0).astype(BF16)
    ranks = []
    for pair in range(pairs):
        here = mine[:, pair * PAIR : (pair + 1) * PAIR]
        ranks.append(jnp.where(here > 0.5, dot(here.astype(BF16), upto) - 1.0, -1.0).astype(jnp.int32))
    spot = pl.ds(pl.multiple_of(step * height, 16), height)
    logits = jnp.where(hits, dot_nt(router_ref[...], t_ref[...]), NEG_FILL)
    logits = jnp.exp(logits - jnp.max(logits, axis=0, keepdims=True))
    gates = logits / jnp.sum(logits, axis=0, keepdims=True)
    slot_at = lax.broadcasted_iota(jnp.int32, (SLOTS, PAIR), 0)
    picks, slot_gates, ins, cots = [], [], [], []
    for pair in range(pairs):
        cols = slice(pair * PAIR, (pair + 1) * PAIR)
        taken = [slot_at == ranks[pair][begin + e : begin + e + 1, :] for e in range(count)]
        slot_gates.append(
            [
                jnp.sum(
                    jnp.where(taken[e], gates[begin + e : begin + e + 1, cols], 0.0),
                    axis=1,
                    keepdims=True,
                )
                for e in range(count)
            ]
        )
        pick = jnp.concatenate([jnp.where(h, 1.0, 0.0).astype(BF16) for h in taken], axis=0)
        picks.append(pick)
        ins.append(dot(pick, t_ref[cols, :]).astype(BF16))
        cots.append(dot(pick, c_ref[cols, :MODEL]).astype(BF16))
    mixed = [[] for _ in range(pairs)]
    dins = [[] for _ in range(pairs)]
    lane = lax.broadcasted_iota(jnp.int32, (height, EXTRA), 1)
    for e in range(count):
        part = slice(e * SLOTS, (e + 1) * SLOTS)
        rows_in = jnp.concatenate([v[part] for v in ins], axis=0)
        rows_cot = jnp.concatenate([v[part] for v in cots], axis=0)
        gate = jnp.concatenate([v[e] for v in slot_gates], axis=0)
        gate_up_w = w_ref[:, e, :, : 2 * FF_DEV].reshape(MODEL, 2 * FF_DEV)
        down_w = w_ref[:, e, :, 2 * FF_DEV :].reshape(MODEL, FF_DEV)
        gate_up = dot(rows_in, gate_up_w)
        pre, up = gate_up[:, :FF_DEV], gate_up[:, FF_DEV:]
        sig = 1.0 / (1.0 + jnp.exp(-pre))
        silu = pre * sig
        hidden = (silu * up).astype(BF16)
        plain = dot(rows_cot, down_w)
        dgate = jnp.sum(hidden.astype(F32) * plain, axis=1, keepdims=True)
        dhidden = plain * gate
        dpre = dhidden * up * sig * (1.0 + pre * (1.0 - sig))
        dgu = jnp.concatenate([dpre, dhidden * silu], axis=1).astype(BF16)
        in_all[e, spot, :] = rows_in
        dout_all[e, spot, :] = (rows_cot.astype(F32) * gate).astype(BF16)
        hid_all[e, spot, :] = hidden
        dgu_all[e, spot, :] = dgu
        mix = (dot_nt(hidden, down_w) * gate).astype(BF16)
        din = dot_nt(dgu, gate_up_w).astype(BF16)
        high = dgate.astype(BF16).astype(F32)
        tail = jnp.where(lane == first_ref[0] + (begin + e), high, 0.0) + jnp.where(
            lane == first_ref[0] + (begin + e + EXPERTS), dgate - high, 0.0
        )
        din = jnp.concatenate([din, tail.astype(BF16)], axis=1)
        for pair in range(pairs):
            rows = slice(pair * SLOTS, (pair + 1) * SLOTS)
            mixed[pair].append(mix[rows])
            dins[pair].append(din[rows])
    for pair in range(pairs):
        cols = slice(pair * PAIR, (pair + 1) * PAIR)
        out = dot_tn(picks[pair], jnp.concatenate(mixed[pair], axis=0))
        dn = dot_tn(picks[pair], jnp.concatenate(dins[pair], axis=0))
        if more:
            out = out + prev_out_ref[cols, :].astype(F32)
            dn = dn + prev_dn_ref[cols, :].astype(F32)
        if not more:
            out_ref[cols, :] = out.astype(BF16)
            dn_ref[cols, :] = dn.astype(BF16)
            continue

        for side in range(2):

            @pl.when(step // 2 == side)
            def _():
                outs[side][0][cols, :] = out.astype(BF16)
                outs[side][1][cols, :] = dn.astype(BF16)

    @pl.when(step == last)
    def _():
        sent = []
        for e in range(count):
            if e >= 2:
                sent[e - 2].wait()
            for start in range(0, MODEL, 2 * STORED):
                cols = slice(start, start + 2 * STORED)
                gate_up_g = dot_tn(in_all[e, :, cols], dgu_all[e])
                down_g = dot_tn(dout_all[e, :, cols], hid_all[e])
                both = jnp.concatenate([gate_up_g, down_g], axis=1).astype(BF16)
                for half in range(2):
                    at = slice(half * STORED, (half + 1) * STORED)
                    done[e % 2, start // STORED + half, :, :] = both[at, :]
            sent.append(
                pltpu.make_async_copy(done.at[e % 2], g_ref.at[:, begin + e], done_sems.at[e % 2])
            )
            sent[e].start()
        for copy in sent[-2:]:
            copy.wait()


def moe(chunk, first, router_t, weights, rows, cots, previous):
    begin, count = chunk
    height = PLANE // PAIR * SLOTS
    wide = pl.BlockSpec((TILE, MODEL), lambda i: (i, 0))
    wider = pl.BlockSpec((TILE, MODEL + EXTRA), lambda i: (i, 0))
    if previous is None:
        sums = [wide, wider]
        shapes = [(PLANE, MODEL), (PLANE, MODEL + EXTRA)]
    else:
        sides = (lambda i: (jnp.minimum(i, 1), 0)), (lambda i: (jnp.maximum(i - 2, 0), 0))
        sums = [pl.BlockSpec((TILE, w), side) for side in sides for w in (MODEL, MODEL + EXTRA)]
        shapes = [(PLANE // 2, MODEL), (PLANE // 2, MODEL + EXTRA)] * 2
    whole = pl.BlockSpec((8, count, 192, 3 * FF_DEV), lambda i: (0, 0, 0, 0), pipeline_mode=pl.Buffered(1))
    flops = 2 * count * height * MODEL * (9 * FF_DEV + 5 * PAIR)
    return pl.pallas_call(
        functools.partial(moe_kernel, begin=begin, count=count, more=previous is not None),
        grid=(PLANE // TILE,),
        in_specs=[
            smem_spec(),
            pl.BlockSpec((EXPERTS, MODEL), lambda i: (0, 0)),
            whole,
        ]
        + [pl.BlockSpec(memory_space=pl.ANY)] * 8
        + ([wide, wider, pl.BlockSpec(memory_space=pl.ANY)] if previous is not None else []),
        out_specs=sums + [pl.BlockSpec(memory_space=pl.ANY)],
        out_shape=[jax.ShapeDtypeStruct(shape, BF16) for shape in shapes]
        + [
            jax.ShapeDtypeStruct((8, EXPERTS_DEV, STORED, 3 * FF_DEV), BF16),
        ],
        input_output_aliases={} if previous is None else {13: 4},
        scratch_shapes=[
            pltpu.VMEM((count, height, MODEL), BF16),
            pltpu.VMEM((count, height, MODEL), BF16),
            pltpu.VMEM((count, height, FF_DEV), BF16),
            pltpu.VMEM((count, height, 2 * FF_DEV), BF16),
            pltpu.VMEM((2, TILE, MODEL), BF16),
            pltpu.VMEM((2, TILE, MODEL + EXTRA), BF16),
            pltpu.SemaphoreType.DMA((2, 2)),
            pltpu.VMEM((2, 8, STORED, 3 * FF_DEV), BF16),
            pltpu.SemaphoreType.DMA((2,)),
        ],
        compiler_params=pltpu.CompilerParams(vmem_limit_bytes=VMEM_LIMIT),
        cost_estimate=pl.CostEstimate(
            flops=10**6, bytes_accessed=10**5, transcendentals=0
        ),
        name="moe",
    )(first, router_t, weights, *rows, *cots, *(previous or ()))


def across_col(value, distance):
    pairs = [(2 * x + c, 2 * ((x + distance) % 4) + c) for x in range(4) for c in range(2)]
    return lax.ppermute(value, "col", pairs)


def other_core(value):
    return lax.ppermute(value, "col", [(s, s ^ 1) for s in range(8)])


def other_row(value):
    return lax.ppermute(value, "row", [(0, 1), (1, 0)])


def along_z(value, distance):
    pairs = [(4 * y + z, 4 * y + (z + distance) % 4) for y in range(2) for z in range(4)]
    return lax.ppermute(value, "dp", pairs)


def other_y(value):
    return lax.ppermute(value, "dp", [(s, s ^ 4) for s in range(8)])


def total(values):
    result = values[0].astype(F32)
    for value in values[1:]:
        result = result + value.astype(F32)
    return result


def after(value, *before):
    return lax.optimization_barrier((value, before))[0]


def spread_col(value):
    return [value] + [across_col(value, d) for d in (1, 2, 3)]


def gather_col(value):
    near = spread_col(value)
    return near + [other_core(v) for v in near]


def scatter_blocks(near, far):
    sums = [
        total([near[d * ROWS : (d + 1) * ROWS], far[d * ROWS : (d + 1) * ROWS]]) for d in range(4)
    ]
    return sums[:1] + [v.astype(BF16) for v in sums[1:]]


def collect_col(blocks):
    return [blocks[0]] + [across_col(blocks[d], -d) for d in (1, 2, 3)]


def flip_x(value):
    return lax.ppermute(value, "col", [(s, s ^ 2) for s in range(8)])


def flip_z(value):
    return lax.ppermute(value, "dp", [(s, s ^ 1) for s in range(8)])


def add_both(value, move):
    return (value.astype(F32) + move(value).astype(F32)).astype(value.dtype)


def per_device(
    tokens,
    cotangent,
    lengths,
    routes,
    norm_gains,
    gain_first,
    gain_second,
    router_w,
    router_first,
    router_second,
    projection_weight,
    projection_first_moment,
    projection_second_moment,
    w_proj,
    proj_first,
    proj_second,
    w_gate_up,
    gate_up_first,
    gate_up_second,
    w_down,
    down_first,
    down_second,
):
    col, row, dp = lax.axis_index("col"), lax.axis_index("row"), lax.axis_index("dp")
    across, core = col // 2, col % 2
    steps = jnp.arange(4, dtype=jnp.int32)
    away = 2 * jnp.remainder(across - steps, 4)
    order = jnp.concatenate([away + core, away + 1 - core])
    spread = jnp.bitwise_xor(dp, jnp.arange(8, dtype=jnp.int32))
    token_places = jnp.arange(GROUP, dtype=jnp.int32)
    doc_ends = jnp.cumsum(lengths[0])
    documents = jnp.sum((token_places[:, None] >= doc_ends[None, :]).astype(jnp.int32), axis=1)
    doc_row, doc_col = documents[None, :], documents[:, None]

    residual_in = tokens.astype(F32)
    inverse_one = inv_rms(residual_in)
    normed_one = (residual_in * inverse_one * norm_gains[0]).astype(BF16)
    attn_w = jnp.concatenate([projection_weight[:, 0, :], w_proj.T], axis=1).astype(BF16)
    normed_near = spread_col(normed_one)
    normed_pieces = normed_near + [other_core(v) for v in normed_near]
    attn_full = lax.all_gather(attn_w, "dp", axis=0, tiled=True)

    gate_up_w, down_w = after((w_gate_up, w_down), attn_w, normed_one)
    expert_w = jnp.concatenate(
        [gate_up_w.reshape(EXPERTS_DEV, 192, 2 * FF_DEV), down_w.transpose(0, 2, 1)], axis=2
    ).astype(BF16)
    expert_ws = []
    for b, n in CHUNKS:
        expert_ws.append(lax.all_gather(expert_w[b : b + n], "dp", axis=0, tiled=False))

    tagged = jnp.concatenate(
        [cotangent, routes.astype(BF16), jnp.zeros((ROWS, EXTRA - routes.shape[1]), BF16)], axis=1
    )
    cots = [jnp.concatenate(spread_col(tagged), axis=0)]
    theirs = other_row(tagged)
    cots.append(jnp.concatenate(spread_col(theirs), axis=0))
    attn_full = after(attn_full, normed_pieces, cots)
    normed_full, qkv, att, lse, near, far = attend(
        order, doc_row, doc_col, normed_pieces, attn_full
    )
    attn_out = total(collect_col(scatter_blocks(near, other_core(far))))
    cots = cots + [other_core(v) for v in cots]
    router_low = router_w.astype(BF16)
    router_t = jnp.roll(router_low.T, -EXPERTS_DEV * col, axis=0)
    first = (EXPERTS_DEV * col).astype(jnp.int32).reshape(1)

    residual = residual_in + attn_out
    inverse_two = inv_rms(residual)
    normed_two = (residual * inverse_two * norm_gains[1]).astype(BF16)
    normed_two = after(normed_two, cots)
    rows_all = [
        jnp.concatenate(spread_col(v), axis=0) for v in (normed_two, other_row(normed_two))
    ]
    rows_all = rows_all + [other_core(v) for v in rows_all]
    logits = jnp.dot(normed_two, router_low, preferred_element_type=F32)
    route_hits = jnp.any(
        routes[:, None, :] == jnp.arange(EXPERTS, dtype=jnp.int32)[None, :, None], axis=-1
    )
    gates = jax.nn.softmax(jnp.where(route_hits, logits, NEG_FILL), axis=-1)

    previous = None
    for chunk, weights in zip(CHUNKS, expert_ws):
        previous = moe(chunk, first, router_t, weights, rows_all, cots, previous)
    mix_near, dn_near, mix_far, dn_far, expert_grads = previous
    expert_sum = lax.psum_scatter(expert_grads, "dp", scatter_dimension=0, tiled=False)

    far = other_core(dn_far)
    theirs = collect_col(scatter_blocks(dn_near[TILE:], far[TILE:]))
    mine = collect_col(scatter_blocks(dn_near[:TILE], far[:TILE]))
    mix_far = other_core(after(mix_far, far))
    mix_blocks = []
    for d in range(4):
        parts = [slice(start + d * ROWS, start + (d + 1) * ROWS) for start in (0, TILE)]
        parts = [total([mix_near[part], mix_far[part]]) for part in parts]
        mix_blocks.append(jnp.concatenate(parts, axis=0).astype(BF16))
    mine = after(mine, mix_blocks)
    dn = total(mine) + other_row(total(theirs).astype(BF16)).astype(F32)
    dgate = dn[:, MODEL : MODEL + EXPERTS] + dn[:, MODEL + EXPERTS : MODEL + 2 * EXPERTS]
    dlogits = gates * (dgate - jnp.sum(gates * dgate, axis=-1, keepdims=True))
    dnormed_two = dn[:, :MODEL] + jnp.dot(dlogits, router_low.astype(F32).T, precision=EXACT_MATH)
    upstream = cotangent.astype(F32)
    dresid_norm, grad_gain_two = norm_back(residual, inverse_two, norm_gains[1], dnormed_two)
    dresidual = upstream + dresid_norm
    dattn_near = spread_col(dresidual.astype(BF16))
    dattn_far = [other_core(v) for v in dattn_near]

    grad_router = lax.dot_general(
        dlogits, normed_two.astype(F32), (((0,), (0,)), ((), ())), precision=EXACT_MATH
    )
    small = jnp.concatenate(
        [grad_router, grad_gain_two[None], jnp.zeros((SMALL - EXPERTS - 1, MODEL), F32)], axis=0
    )
    dattn_pieces = after(dattn_near + dattn_far, small)
    near, far, *attn_grads = attend_back(
        order,
        spread,
        doc_row,
        doc_col,
        norm_gains[:1],
        small,
        attn_full,
        normed_full,
        qkv,
        att,
        lse,
        dattn_pieces,
    )
    theirs = other_core(far)
    blocks = scatter_blocks(near, theirs)
    small = total([far[GROUP // 2 :], theirs[GROUP // 2 :]]).astype(BF16)
    moved = [across_col(jnp.concatenate([blocks[d], small], axis=0), -d) for d in (1, 2, 3)]
    attn_moved = other_y(after(attn_grads[1], blocks))
    moved, attn_moved = lax.optimization_barrier((moved, attn_moved))
    mix_moved = collect_col(after(mix_blocks, moved))
    smalls = jnp.stack([small] + [v[ROWS:] for v in moved])[jnp.remainder(steps - across, 4)]
    small = total([smalls[d] for d in range(4)]).astype(BF16).reshape(-1, 2 * PAIR)
    dnormed = total([blocks[0]] + [v[:ROWS] for v in moved])
    dtokens_norm, _ = norm_back(residual_in, inverse_one, norm_gains[0], dnormed)
    dtokens = dresidual + dtokens_norm
    halves = total([attn_grads[0], attn_moved]).astype(BF16)
    sent = jnp.concatenate([halves[2:].reshape(-1, 2 * PAIR), small], axis=0)
    kept = jnp.concatenate([halves[:2].reshape(-1, 2 * PAIR), small], axis=0)
    kept = total([kept, along_z(sent, 2)]).astype(BF16)
    sent = kept[STORED:]
    kept = jnp.concatenate([kept[:STORED], kept[2 * STORED :]], axis=0)
    kept = total([kept, flip_z(sent)]).astype(BF16)
    kept = add_both(kept, other_row)
    attn_sums = kept[:STORED].astype(F32)
    small = add_both(kept[STORED:], other_y)
    experts_new = update_experts(
        expert_sum, (w_gate_up, gate_up_first, gate_up_second), (w_down, down_first, down_second)
    )
    mix_moved = after(mix_moved, experts_new, dtokens, attn_sums)
    mixed = total(mix_moved)
    mixture = mixed[:ROWS] + other_row(mixed[ROWS:].astype(BF16)).astype(F32)
    output = (residual + mixture).astype(BF16)
    small = small.reshape(-1, MODEL).astype(F32)
    sum_router = small[:EXPERTS].T
    sum_gains = jnp.stack([small[EXPERTS + 1], small[EXPERTS]])
    sum_qkv = attn_sums[:, None, :QKV]
    sum_proj = attn_sums[:, QKV : 2 * PAIR].T
    return (
        output,
        dtokens,
        *adamw(norm_gains, sum_gains, gain_first, gain_second, RATE_GAIN, 0.0),
        *adamw(router_w, sum_router, router_first, router_second, RATE_ROUTER, DECAY_RATE),
        *adamw(
            projection_weight,
            sum_qkv,
            projection_first_moment,
            projection_second_moment,
            RATE_NARROW,
            DECAY_RATE,
        ),
        *adamw(w_proj, sum_proj, proj_first, proj_second, RATE_WIDE, DECAY_RATE),
        *experts_new,
    )


def solution(mesh):
    by_token = P(("dp", "row", "col"), None)
    qkv_at, proj_at = P("dp", "col", None), P("col", "dp")
    gate_up_at, down_at = P("col", "dp", None, "row"), P("col", "row", "dp")
    return jax.shard_map(
        per_device,
        mesh=mesh,
        in_specs=(by_token, by_token, P(("dp", "row"), None), by_token)
        + (P(),) * 6
        + (qkv_at,) * 3
        + (proj_at,) * 3
        + (gate_up_at,) * 3
        + (down_at,) * 3,
        out_specs=(by_token, by_token)
        + (P(),) * 6
        + (qkv_at,) * 3
        + (proj_at,) * 3
        + (gate_up_at,) * 3
        + (down_at,) * 3,
        check_vma=False,
    )
```

```python
import functools

import jax
import jax.numpy as jnp
from jax import lax
from jax.experimental import pallas as pl
from jax.experimental.pallas import tpu as pltpu
from jax.sharding import PartitionSpec as P

HEAD_SIZE = 64
STEP = 10
QUERY_PER_KEY = 3
SPAN = QUERY_PER_KEY * HEAD_SIZE
QKV = SPAN + 2 * HEAD_SIZE
MODEL = 1536
ROWS = 128
STORED = 192
GROUP = 1024
PLANE = 2048
FF_DEV = 256
EXPERTS = 40
EXPERTS_DEV = 5
TOP = 8
SLOTS = 112
TILE = 512
PAIR = 256
QUERY_TILE = 256
EXTRA = 128
SMALL = 48
CHUNKS = ((0, 3), (3, 2))

EXACT_MATH = lax.Precision.HIGHEST
NORM_EPS = 1e-05
NEG_FILL = -1e30
BETA_ONE = 0.9
BETA_TWO = 0.95
ADAM_EPS = 1e-08
DECAY_RATE = 0.1
RATE_GAIN = 0.5
RATE_ROUTER = 0.03
RATE_NARROW = 0.05
RATE_WIDE = 0.4
SCALE = HEAD_SIZE ** (-0.5)
F32 = jnp.float32
BF16 = jnp.bfloat16
VMEM_LIMIT = 60 * 1024 * 1024


def row_pairs(stored):
    parts = stored.reshape(EXPERTS_DEV, STORED, 2, FF_DEV // 128, 128)
    return parts.transpose(0, 1, 3, 2, 4).reshape(-1, 128)


def paired_rows(rows):
    parts = rows.reshape(EXPERTS_DEV, STORED, FF_DEV // 128, 2, 128)
    return parts.transpose(0, 1, 3, 2, 4).reshape(EXPERTS_DEV, STORED, 2, FF_DEV)


def adamw_kernel(g_ref, *refs):
    olds, news = refs[:6], refs[6:]
    for half in range(FF_DEV // 128):
        for kind in range(2):
            at = pl.ds(2 * half + kind, STORED, stride=4)
            start = kind * FF_DEV + half * 128
            gradient = g_ref[0, :, start : start + 128].astype(F32)
            weight, first, second = (ref[at, :] for ref in olds[:3])
            results = adamw(weight, gradient, first, second, RATE_NARROW, DECAY_RATE)
            for ref, result in zip(news[:3], results):
                ref[at, :] = result
    gradient = g_ref[0, :, 2 * FF_DEV :].astype(F32)
    weight, first, second = (ref[0] for ref in olds[3:])
    results = adamw(weight, gradient, first, second, RATE_WIDE, DECAY_RATE)
    for ref, result in zip(news[3:], results):
        ref[0] = result


def update_experts(gradient, gate_up, down):
    pair_rows = pl.BlockSpec((4 * STORED, 128), lambda i: (i, 0))
    down_rows = pl.BlockSpec((1, STORED, FF_DEV), lambda i: (i, 0, 0))
    specs = [pair_rows] * 3 + [down_rows] * 3
    pair_shape = jax.ShapeDtypeStruct((EXPERTS_DEV * 4 * STORED, 128), F32)
    down_shape = jax.ShapeDtypeStruct((EXPERTS_DEV, STORED, FF_DEV), F32)
    new = pl.pallas_call(
        adamw_kernel,
        grid=(EXPERTS_DEV,),
        in_specs=[pl.BlockSpec((1, STORED, 3 * FF_DEV), lambda i: (i, 0, 0))] + specs,
        out_specs=specs,
        out_shape=[pair_shape] * 3 + [down_shape] * 3,
        cost_estimate=pl.CostEstimate(
            flops=20 * 10**6, bytes_accessed=20 * 10**6, transcendentals=10**6
        ),
        name="update_experts",
    )(gradient, *[row_pairs(v) for v in gate_up], *[v.transpose(0, 2, 1) for v in down])
    return [paired_rows(v) for v in new[:3]] + [v.transpose(0, 2, 1) for v in new[3:]]


def proj_kernel(g_ref, *refs):
    olds, news = refs[:3], refs[3:]
    gradient = g_ref[:, PAIR : 2 * PAIR].astype(F32).T[HEAD_SIZE:]
    weight, first, second = (ref[...] for ref in olds)
    results = adamw(weight, gradient, first, second, RATE_WIDE, DECAY_RATE)
    for ref, result in zip(news, results):
        ref[...] = result


def update_proj(sums, *states):
    return pl.pallas_call(
        proj_kernel,
        out_shape=[jax.ShapeDtypeStruct((SPAN, STORED), F32)] * 3,
        name="update_proj",
    )(sums, *states)


def inv_rms(values):
    return lax.rsqrt(jnp.mean(values * values, axis=-1, keepdims=True) + NORM_EPS)


def adamw(weight, gradient, moment_one, moment_two, step_rate, weight_decay):
    first_new = BETA_ONE * moment_one + (1.0 - BETA_ONE) * gradient
    second_new = BETA_TWO * moment_two + (1.0 - BETA_TWO) * gradient * gradient
    boost_one = 1.0 / (1.0 - BETA_ONE**STEP)
    boost_two = 1.0 / (1.0 - BETA_TWO**STEP)
    direction = first_new * boost_one / (jnp.sqrt(second_new * boost_two) + ADAM_EPS)
    return (weight - step_rate * (direction + weight_decay * weight), first_new, second_new)


def norm_back(values, inverse, gain_row, upstream):
    normalized = values * inverse
    scaled = upstream * gain_row
    grad_gain = jnp.sum(upstream * normalized, axis=0)
    grad_values = inverse * (
        scaled - normalized * jnp.mean(scaled * normalized, axis=-1, keepdims=True)
    )
    return (grad_values, grad_gain)


def dot(a, b):
    return jnp.dot(a, b, preferred_element_type=F32)


def dot_nt(a, b):
    return lax.dot_general(a, b, (((1,), (1,)), ((), ())), preferred_element_type=F32)


def dot_tn(a, b):
    return lax.dot_general(a, b, (((0,), (0,)), ((), ())), preferred_element_type=F32)


def row_blocks(refs):
    blocks = []
    for ref in refs:
        for start in range(0, ref.shape[0], ROWS):
            blocks.append((ref, start))
    return blocks


def place(order_ref, block):
    return pl.ds(pl.multiple_of(order_ref[block] * ROWS, ROWS), ROWS)


def stored_rows(spread_ref, block):
    return pl.ds(pl.multiple_of(spread_ref[block] * STORED, STORED), STORED)


def visible(doc_row_ref, doc_col_ref, tile):
    keys = (tile + 1) * QUERY_TILE
    key_at = lax.broadcasted_iota(jnp.int32, (keys, QUERY_TILE), 0)
    query_at = lax.broadcasted_iota(jnp.int32, (keys, QUERY_TILE), 1) + tile * QUERY_TILE
    same = doc_col_ref[:keys, :] == doc_row_ref[:, tile * QUERY_TILE : keys]
    return same & (key_at <= query_at)


def attend_kernel(order_ref, doc_row_ref, doc_col_ref, *refs):
    normed_ref, qkv_ref, att_ref, lse_ref, near_ref, far_ref = refs[-6:]
    pieces, w_ref = refs[:2], refs[2]
    for block, (ref, start) in enumerate(row_blocks(pieces)):
        normed_ref[place(order_ref, block), :] = ref[start : start + ROWS, :]
    for tile in range(GROUP // QUERY_TILE):
        rows = slice(tile * QUERY_TILE, (tile + 1) * QUERY_TILE)
        qkv_ref[rows, :] = dot(normed_ref[rows, :], w_ref[...])[:, :QKV].astype(BF16)
    keys_all = qkv_ref[:, SPAN : SPAN + HEAD_SIZE]
    values_t = qkv_ref[:, SPAN + HEAD_SIZE : QKV].astype(F32).T.astype(BF16)
    lse_ref[...] = jnp.zeros_like(lse_ref)
    for tile in range(GROUP // QUERY_TILE):
        keys = (tile + 1) * QUERY_TILE
        rows = slice(tile * QUERY_TILE, keys)
        allowed = visible(doc_row_ref, doc_col_ref, tile)
        outs = [jnp.zeros((HEAD_SIZE, QUERY_TILE), F32)]
        for head in range(QUERY_PER_KEY):
            query = qkv_ref[rows, head * HEAD_SIZE : (head + 1) * HEAD_SIZE]
            scores = jnp.where(allowed, dot_nt(keys_all[:keys], query) * SCALE, NEG_FILL)
            peak = jnp.max(scores, axis=0, keepdims=True)
            weights = jnp.exp(scores - peak)
            total = jnp.sum(weights, axis=0, keepdims=True)
            probs = (weights * (1.0 / total)).astype(BF16)
            outs.append(dot(values_t[:, :keys], probs))
            lse_ref[head : head + 1, rows] = peak + jnp.log(total)
        att_ref[rows, :] = jnp.concatenate(outs, axis=0).T.astype(BF16)
    proj = w_ref[:, SPAN + HEAD_SIZE :]
    for block in range(GROUP // ROWS):
        part_ref = near_ref if block < 4 else far_ref
        part_ref[block % 4 * ROWS : (block % 4 + 1) * ROWS, :] = dot_nt(
            att_ref[place(order_ref, block), :], proj
        ).astype(BF16)


def attend_back_kernel(
    order_ref,
    spread_ref,
    doc_row_ref,
    doc_col_ref,
    gain_ref,
    small_ref,
    w_ref,
    normed_ref,
    qkv_ref,
    att_ref,
    lse_ref,
    *refs,
):
    pieces, refs = refs[:8], refs[8:]
    near_ref, far_ref, *grads_refs = refs[:4]
    dattn_ref, datt_ref, dqkv_ref, dkv_ref, whole_ref = refs[4:]
    for block, (ref, start) in enumerate(row_blocks(pieces)):
        dattn_ref[place(order_ref, block), :] = ref[start : start + ROWS, :]
    proj = w_ref[:, SPAN + HEAD_SIZE :]
    for tile in range(GROUP // QUERY_TILE):
        rows = slice(tile * QUERY_TILE, (tile + 1) * QUERY_TILE)
        datt_ref[rows, :] = dot(dattn_ref[rows, :], proj).astype(BF16)
    keys_all = qkv_ref[:, SPAN : SPAN + HEAD_SIZE]
    values_all = qkv_ref[:, SPAN + HEAD_SIZE : QKV]
    keys_t = keys_all.astype(F32).T.astype(BF16)
    dkv_ref[...] = jnp.zeros_like(dkv_ref)
    for tile in range(GROUP // QUERY_TILE):
        keys = (tile + 1) * QUERY_TILE
        rows = slice(tile * QUERY_TILE, keys)
        allowed = visible(doc_row_ref, doc_col_ref, tile)
        outs = []
        for head in range(QUERY_PER_KEY):
            query = qkv_ref[rows, head * HEAD_SIZE : (head + 1) * HEAD_SIZE]
            dout = datt_ref[rows, (head + 1) * HEAD_SIZE : (head + 2) * HEAD_SIZE]
            scores = jnp.where(allowed, dot_nt(keys_all[:keys], query) * SCALE, NEG_FILL)
            probs = jnp.exp(scores - lse_ref[head : head + 1, rows])
            dprobs = dot_nt(values_all[:keys], dout)
            shift = jnp.sum(probs * dprobs, axis=0, keepdims=True)
            dscores = (probs * (dprobs - shift)).astype(BF16)
            dkv_ref[:keys, :HEAD_SIZE] += dot(dscores, query)
            dkv_ref[:keys, HEAD_SIZE:] += dot(probs.astype(BF16), dout)
            outs.append(dot(keys_t[:, :keys], dscores))
        dqkv_ref[rows, :SPAN] = (jnp.concatenate(outs, axis=0).T * SCALE).astype(BF16)
    dqkv_ref[:, SPAN : SPAN + HEAD_SIZE] = (dkv_ref[:, :HEAD_SIZE] * SCALE).astype(BF16)
    dqkv_ref[:, SPAN + HEAD_SIZE :] = dkv_ref[:, HEAD_SIZE:].astype(BF16)
    qkv_mat = w_ref[:, :QKV]
    dgain = jnp.zeros((1, MODEL), F32)
    for block in range(GROUP // ROWS):
        at = place(order_ref, block)
        part = dot_nt(dqkv_ref[at, :], qkv_mat)
        dgain = dgain + jnp.sum(part * normed_ref[at, :].astype(F32), axis=0, keepdims=True)
        part_ref = near_ref if block < 4 else far_ref
        part_ref[block % 4 * ROWS : (block % 4 + 1) * ROWS, :] = part.astype(BF16)
    small_at = lax.broadcasted_iota(jnp.int32, (SMALL, MODEL), 0)
    small = jnp.where(small_at == EXPERTS + 1, dgain / gain_ref[...], small_ref[...])
    far_ref[GROUP // 2 :, :] = small.astype(BF16)
    for start in range(0, MODEL, PAIR):
        cols = slice(start, start + PAIR)
        qkv_part = dot_tn(dqkv_ref[...], normed_ref[:, cols])
        proj_part = dot_tn(att_ref[...], dattn_ref[:, cols])[HEAD_SIZE:]
        both = jnp.concatenate([qkv_part, proj_part], axis=0)
        whole_ref[cols, :] = both.T.astype(BF16)
    for block in range(8):
        grads_refs[block // 4][block % 4] = whole_ref[stored_rows(spread_ref, block), :]


def vmem_spec():
    return pl.BlockSpec(memory_space=pltpu.VMEM)


def smem_spec():
    return pl.BlockSpec(memory_space=pltpu.SMEM)


def attend(order, doc_row, doc_col, pieces, weights):
    return pl.pallas_call(
        attend_kernel,
        in_specs=[smem_spec()] + [vmem_spec()] * (3 + len(pieces)),
        out_specs=[vmem_spec()] * 6,
        out_shape=[
            jax.ShapeDtypeStruct((GROUP, MODEL), BF16),
            jax.ShapeDtypeStruct((GROUP, QKV), BF16),
            jax.ShapeDtypeStruct((GROUP, PAIR), BF16),
            jax.ShapeDtypeStruct((8, GROUP), F32),
            jax.ShapeDtypeStruct((GROUP // 2, MODEL), BF16),
            jax.ShapeDtypeStruct((GROUP // 2, MODEL), BF16),
        ],
        compiler_params=pltpu.CompilerParams(vmem_limit_bytes=VMEM_LIMIT),
        cost_estimate=pl.CostEstimate(
            flops=10**6, bytes_accessed=10**5, transcendentals=0
        ),
        name="attend",
    )(order, doc_row, doc_col, *pieces, weights)


def attend_back(order, spread, doc_row, doc_col, gain, small, weights, normed, qkv, att, lse, pieces):
    return pl.pallas_call(
        attend_back_kernel,
        in_specs=[smem_spec()] * 2 + [vmem_spec()] * (9 + len(pieces)),
        out_specs=[vmem_spec()] * 4,
        out_shape=[
            jax.ShapeDtypeStruct((GROUP // 2, MODEL), BF16),
            jax.ShapeDtypeStruct((GROUP // 2 + SMALL, MODEL), BF16),
        ]
        + [jax.ShapeDtypeStruct((4, STORED, 2 * PAIR), BF16)] * 2,
        scratch_shapes=[
            pltpu.VMEM((GROUP, MODEL), BF16),
            pltpu.VMEM((GROUP, PAIR), BF16),
            pltpu.VMEM((GROUP, QKV), BF16),
            pltpu.VMEM((GROUP, 2 * HEAD_SIZE), F32),
            pltpu.VMEM((MODEL, 2 * PAIR), BF16),
        ],
        compiler_params=pltpu.CompilerParams(vmem_limit_bytes=VMEM_LIMIT),
        cost_estimate=pl.CostEstimate(
            flops=10**6, bytes_accessed=10**5, transcendentals=0
        ),
        name="attend_back",
    )(order, spread, doc_row, doc_col, gain, small, weights, normed, qkv, att, lse, *pieces)


def moe_kernel(first_ref, router_ref, stored_ref, *refs, begin, count, more):
    sources, refs = (refs[:4], refs[4:8]), refs[8:]
    if more:
        prev_out_ref, prev_dn_ref = refs[:2]
        refs = refs[3:]
        outs, refs = (refs[:2], refs[2:4]), refs[4:]
    else:
        out_ref, dn_ref = refs[:2]
        refs = refs[2:]
    g_ref, in_all, dout_all, hid_all, dgu_all, held_t, held_c, sems, done, done_sems = refs[:10]
    w_ref, w_sems = refs[10:]
    step = pl.program_id(0)
    pairs = TILE // PAIR
    height = pairs * SLOTS
    last = PLANE // TILE - 1

    def copies(tile):
        return [
            pltpu.make_async_copy(
                sources[kind][tile], held.at[tile % 2], sems.at[kind, tile % 2]
            )
            for kind, held in enumerate((held_t, held_c))
        ]

    def fetch(e):
        return pltpu.make_async_copy(stored_ref.at[:, e], w_ref.at[:, e], w_sems.at[e])

    for tile in range(last + 1):

        @pl.when(step == max(tile - 1, 0))
        def _():
            for copy in copies(tile):
                copy.start()
            if tile == 0:
                for e in range(count):
                    fetch(e).start()

    for tile in range(last + 1):

        @pl.when(step == tile)
        def _():
            for copy in copies(tile):
                copy.wait()

    t_ref, c_ref = held_t.at[lax.rem(step, 2)], held_c.at[lax.rem(step, 2)]
    ids = c_ref[:, MODEL:].astype(F32).T.astype(jnp.int32)
    expert_at = lax.broadcasted_iota(jnp.int32, (EXPERTS, TILE), 0) + first_ref[0]
    expert_at = jnp.where(expert_at >= EXPERTS, expert_at - EXPERTS, expert_at)
    hits = ids[:1] == expert_at
    for choice in range(1, TOP):
        hits = hits | (ids[choice : choice + 1] == expert_at)
    mine = jnp.where(hits[:8], 1.0, 0.0)
    upto = lax.broadcasted_iota(jnp.int32, (PAIR, PAIR), 0) <= lax.broadcasted_iota(
        jnp.int32, (PAIR, PAIR), 1
    )
    upto = jnp.where(upto, 1.0, 0.0).astype(BF16)
    ranks = []
    for pair in range(pairs):
        here = mine[:, pair * PAIR : (pair + 1) * PAIR]
        ranks.append(jnp.where(here > 0.5, dot(here.astype(BF16), upto) - 1.0, -1.0).astype(jnp.int32))
    spot = pl.ds(pl.multiple_of(step * height, 16), height)
    logits = jnp.where(hits, dot_nt(router_ref[...], t_ref[...]), NEG_FILL)
    logits = jnp.exp(logits - jnp.max(logits, axis=0, keepdims=True))
    gates = logits / jnp.sum(logits, axis=0, keepdims=True)
    slot_at = lax.broadcasted_iota(jnp.int32, (SLOTS, PAIR), 0)
    picks, slot_gates, ins, cots = [], [], [], []
    for pair in range(pairs):
        cols = slice(pair * PAIR, (pair + 1) * PAIR)
        taken = [slot_at == ranks[pair][begin + e : begin + e + 1, :] for e in range(count)]
        slot_gates.append(
            [
                jnp.sum(
                    jnp.where(taken[e], gates[begin + e : begin + e + 1, cols], 0.0),
                    axis=1,
                    keepdims=True,
                )
                for e in range(count)
            ]
        )
        pick = jnp.concatenate([jnp.where(h, 1.0, 0.0).astype(BF16) for h in taken], axis=0)
        picks.append(pick)
        ins.append(dot(pick, t_ref[cols, :]).astype(BF16))
        cots.append(dot(pick, c_ref[cols, :MODEL]).astype(BF16))
    mixed = [[] for _ in range(pairs)]
    dins = [[] for _ in range(pairs)]
    lane = lax.broadcasted_iota(jnp.int32, (height, EXTRA), 1)
    for e in range(count):
        part = slice(e * SLOTS, (e + 1) * SLOTS)

        @pl.when(step == 0)
        def _():
            fetch(e).wait()

        rows_in = jnp.concatenate([v[part] for v in ins], axis=0)
        rows_cot = jnp.concatenate([v[part] for v in cots], axis=0)
        gate = jnp.concatenate([v[e] for v in slot_gates], axis=0)
        gate_up_w = w_ref[:, e, :, : 2 * FF_DEV].reshape(MODEL, 2 * FF_DEV)
        down_w = w_ref[:, e, :, 2 * FF_DEV :].reshape(MODEL, FF_DEV)
        gate_up = dot(rows_in, gate_up_w)
        pre, up = gate_up[:, :FF_DEV], gate_up[:, FF_DEV:]
        sig = 1.0 / (1.0 + jnp.exp(-pre))
        silu = pre * sig
        hidden = (silu * up).astype(BF16)
        plain = dot(rows_cot, down_w)
        dgate = jnp.sum(hidden.astype(F32) * plain, axis=1, keepdims=True)
        dhidden = plain * gate
        dpre = dhidden * up * sig * (1.0 + pre * (1.0 - sig))
        dgu = jnp.concatenate([dpre, dhidden * silu], axis=1).astype(BF16)
        in_all[e, spot, :] = rows_in
        dout_all[e, spot, :] = (rows_cot.astype(F32) * gate).astype(BF16)
        hid_all[e, spot, :] = hidden
        dgu_all[e, spot, :] = dgu
        mix = (dot_nt(hidden, down_w) * gate).astype(BF16)
        din = dot_nt(dgu, gate_up_w).astype(BF16)
        high = dgate.astype(BF16).astype(F32)
        tail = jnp.where(lane == first_ref[0] + (begin + e), high, 0.0) + jnp.where(
            lane == first_ref[0] + (begin + e + EXPERTS), dgate - high, 0.0
        )
        din = jnp.concatenate([din, tail.astype(BF16)], axis=1)
        for pair in range(pairs):
            rows = slice(pair * SLOTS, (pair + 1) * SLOTS)
            mixed[pair].append(mix[rows])
            dins[pair].append(din[rows])
    for pair in range(pairs):
        cols = slice(pair * PAIR, (pair + 1) * PAIR)
        out = dot_tn(picks[pair], jnp.concatenate(mixed[pair], axis=0))
        dn = dot_tn(picks[pair], jnp.concatenate(dins[pair], axis=0))
        if more:
            out = out + prev_out_ref[cols, :].astype(F32)
            dn = dn + prev_dn_ref[cols, :].astype(F32)
        if not more:
            out_ref[cols, :] = out.astype(BF16)
            dn_ref[cols, :] = dn.astype(BF16)
            continue

        for side in range(2):

            @pl.when(step // 2 == side)
            def _():
                outs[side][0][cols, :] = out.astype(BF16)
                outs[side][1][cols, :] = dn.astype(BF16)

    @pl.when(step == last)
    def _():
        sent = []
        for e in range(count):
            if e >= 2:
                sent[e - 2].wait()
            for start in range(0, MODEL, 2 * STORED):
                cols = slice(start, start + 2 * STORED)
                gate_up_g = dot_tn(in_all[e, :, cols], dgu_all[e])
                down_g = dot_tn(dout_all[e, :, cols], hid_all[e])
                both = jnp.concatenate([gate_up_g, down_g], axis=1).astype(BF16)
                for half in range(2):
                    at = slice(half * STORED, (half + 1) * STORED)
                    done[e % 2, start // STORED + half, :, :] = both[at, :]
            sent.append(
                pltpu.make_async_copy(done.at[e % 2], g_ref.at[:, begin + e], done_sems.at[e % 2])
            )
            sent[e].start()
        for copy in sent[-2:]:
            copy.wait()


def moe(chunk, first, router_t, weights, rows, cots, previous):
    begin, count = chunk
    height = PLANE // PAIR * SLOTS
    wide = pl.BlockSpec((TILE, MODEL), lambda i: (i, 0))
    wider = pl.BlockSpec((TILE, MODEL + EXTRA), lambda i: (i, 0))
    if previous is None:
        sums = [wide, wider]
        shapes = [(PLANE, MODEL), (PLANE, MODEL + EXTRA)]
    else:
        sides = (lambda i: (jnp.minimum(i, 1), 0)), (lambda i: (jnp.maximum(i - 2, 0), 0))
        sums = [pl.BlockSpec((TILE, w), side) for side in sides for w in (MODEL, MODEL + EXTRA)]
        shapes = [(PLANE // 2, MODEL), (PLANE // 2, MODEL + EXTRA)] * 2
    flops = 2 * count * height * MODEL * (9 * FF_DEV + 5 * PAIR)
    return pl.pallas_call(
        functools.partial(moe_kernel, begin=begin, count=count, more=previous is not None),
        grid=(PLANE // TILE,),
        in_specs=[
            smem_spec(),
            pl.BlockSpec((EXPERTS, MODEL), lambda i: (0, 0)),
            pl.BlockSpec(memory_space=pl.ANY),
        ]
        + [pl.BlockSpec(memory_space=pl.ANY)] * 8
        + ([wide, wider, pl.BlockSpec(memory_space=pl.ANY)] if previous is not None else []),
        out_specs=sums + [pl.BlockSpec(memory_space=pl.ANY)],
        out_shape=[jax.ShapeDtypeStruct(shape, BF16) for shape in shapes]
        + [
            jax.ShapeDtypeStruct((8, EXPERTS_DEV, STORED, 3 * FF_DEV), BF16),
        ],
        input_output_aliases={} if previous is None else {13: 4},
        scratch_shapes=[
            pltpu.VMEM((count, height, MODEL), BF16),
            pltpu.VMEM((count, height, MODEL), BF16),
            pltpu.VMEM((count, height, FF_DEV), BF16),
            pltpu.VMEM((count, height, 2 * FF_DEV), BF16),
            pltpu.VMEM((2, TILE, MODEL), BF16),
            pltpu.VMEM((2, TILE, MODEL + EXTRA), BF16),
            pltpu.SemaphoreType.DMA((2, 2)),
            pltpu.VMEM((2, 8, STORED, 3 * FF_DEV), BF16),
            pltpu.SemaphoreType.DMA((2,)),
            pltpu.VMEM((8, count, STORED, 3 * FF_DEV), BF16),
            pltpu.SemaphoreType.DMA((count,)),
        ],
        compiler_params=pltpu.CompilerParams(vmem_limit_bytes=VMEM_LIMIT),
        cost_estimate=pl.CostEstimate(
            flops=10**6, bytes_accessed=10**5, transcendentals=0
        ),
        name="moe",
    )(first, router_t, weights, *rows, *cots, *(previous or ()))


def across_col(value, distance):
    pairs = [(2 * x + c, 2 * ((x + distance) % 4) + c) for x in range(4) for c in range(2)]
    return lax.ppermute(value, "col", pairs)


def other_core(value):
    return lax.ppermute(value, "col", [(s, s ^ 1) for s in range(8)])


def other_row(value):
    return lax.ppermute(value, "row", [(0, 1), (1, 0)])


def along_z(value, distance):
    pairs = [(4 * y + z, 4 * y + (z + distance) % 4) for y in range(2) for z in range(4)]
    return lax.ppermute(value, "dp", pairs)


def other_y(value):
    return lax.ppermute(value, "dp", [(s, s ^ 4) for s in range(8)])


def total(values):
    result = values[0].astype(F32)
    for value in values[1:]:
        result = result + value.astype(F32)
    return result


def after(value, *before):
    return lax.optimization_barrier((value, before))[0]


def spread_col(value):
    return [value] + [across_col(value, d) for d in (1, 2, 3)]


def relay_col(value):
    ahead, behind = across_col(value, 1), across_col(value, -1)
    half = value.shape[0] // 2
    opposite = [across_col(ahead[:half], 1), across_col(behind[half:], -1)]
    return [value, ahead, jnp.concatenate(opposite, axis=0), behind]


def gather_col(value):
    near = spread_col(value)
    return near + [other_core(v) for v in near]


def scatter_blocks(near, far):
    sums = [
        total([near[d * ROWS : (d + 1) * ROWS], far[d * ROWS : (d + 1) * ROWS]]) for d in range(4)
    ]
    return sums[:1] + [v.astype(BF16) for v in sums[1:]]


def collect_col(blocks):
    return [blocks[0]] + [across_col(blocks[d], -d) for d in (1, 2, 3)]


def flip_x(value):
    return lax.ppermute(value, "col", [(s, s ^ 2) for s in range(8)])


def flip_z(value):
    return lax.ppermute(value, "dp", [(s, s ^ 1) for s in range(8)])


def add_both(value, move):
    return (value.astype(F32) + move(value).astype(F32)).astype(value.dtype)


def per_device(
    tokens,
    cotangent,
    lengths,
    routes,
    norm_gains,
    gain_first,
    gain_second,
    router_w,
    router_first,
    router_second,
    projection_weight,
    projection_first_moment,
    projection_second_moment,
    w_proj,
    proj_first,
    proj_second,
    w_gate_up,
    gate_up_first,
    gate_up_second,
    w_down,
    down_first,
    down_second,
):
    col, row, dp = lax.axis_index("col"), lax.axis_index("row"), lax.axis_index("dp")
    across, core = col // 2, col % 2
    steps = jnp.arange(4, dtype=jnp.int32)
    away = 2 * jnp.remainder(across - steps, 4)
    order = jnp.concatenate([away + core, away + 1 - core])
    spread = jnp.bitwise_xor(dp, jnp.arange(8, dtype=jnp.int32))
    token_places = jnp.arange(GROUP, dtype=jnp.int32)
    doc_ends = jnp.cumsum(lengths[0])
    documents = jnp.sum((token_places[:, None] >= doc_ends[None, :]).astype(jnp.int32), axis=1)
    doc_row, doc_col = documents[None, :], documents[:, None]

    residual_in = tokens.astype(F32)
    inverse_one = inv_rms(residual_in)
    normed_one = (residual_in * inverse_one * norm_gains[0]).astype(BF16)
    attn_w = jnp.concatenate([projection_weight[:, 0, :], w_proj.T], axis=1).astype(BF16)
    normed_near = relay_col(normed_one)
    normed_near = jnp.concatenate(normed_near, axis=0)
    normed_pieces = [normed_near, other_core(normed_near)]
    attn_full = lax.all_gather(attn_w, "dp", axis=0, tiled=True)

    gate_up_w, down_w = after((w_gate_up, w_down), attn_w, normed_one)
    expert_w = jnp.concatenate(
        [gate_up_w.reshape(EXPERTS_DEV, 192, 2 * FF_DEV), down_w.transpose(0, 2, 1)], axis=2
    ).astype(BF16)
    expert_ws = []
    for b, n in CHUNKS:
        expert_ws.append(lax.all_gather(expert_w[b : b + n], "dp", axis=0, tiled=False))

    tagged = jnp.concatenate(
        [cotangent, routes.astype(BF16), jnp.zeros((ROWS, EXTRA - routes.shape[1]), BF16)], axis=1
    )
    cots = [jnp.concatenate(relay_col(tagged), axis=0)]
    theirs = other_row(tagged)
    cots.append(jnp.concatenate(relay_col(theirs), axis=0))
    attn_full = after(attn_full, normed_pieces, cots)
    normed_full, qkv, att, lse, near, far = attend(
        order, doc_row, doc_col, normed_pieces, attn_full
    )
    attn_out = total(collect_col(scatter_blocks(near, other_core(far))))
    cots = cots + [other_core(v) for v in cots]
    router_low = router_w.astype(BF16)
    router_t = jnp.roll(router_low.T, -EXPERTS_DEV * col, axis=0)
    first = (EXPERTS_DEV * col).astype(jnp.int32).reshape(1)

    residual = residual_in + attn_out
    inverse_two = inv_rms(residual)
    normed_two = (residual * inverse_two * norm_gains[1]).astype(BF16)
    normed_two = after(normed_two, cots)
    rows_all = [
        jnp.concatenate(relay_col(v), axis=0) for v in (normed_two, other_row(normed_two))
    ]
    rows_all = rows_all + [other_core(v) for v in rows_all]
    logits = jnp.dot(normed_two, router_low, preferred_element_type=F32)
    route_hits = jnp.any(
        routes[:, None, :] == jnp.arange(EXPERTS, dtype=jnp.int32)[None, :, None], axis=-1
    )
    gates = jax.nn.softmax(jnp.where(route_hits, logits, NEG_FILL), axis=-1)

    previous = None
    for chunk, weights in zip(CHUNKS, expert_ws):
        previous = moe(chunk, first, router_t, weights, rows_all, cots, previous)
    mix_near, dn_near, mix_far, dn_far, expert_grads = previous
    expert_sum = lax.psum_scatter(expert_grads, "dp", scatter_dimension=0, tiled=False)

    far = other_core(dn_far)
    theirs = collect_col(scatter_blocks(dn_near[TILE:], far[TILE:]))
    mine = collect_col(scatter_blocks(dn_near[:TILE], far[:TILE]))
    mix_far = other_core(after(mix_far, far))
    mix_blocks = []
    for d in range(4):
        parts = [slice(start + d * ROWS, start + (d + 1) * ROWS) for start in (0, TILE)]
        parts = [total([mix_near[part], mix_far[part]]) for part in parts]
        mix_blocks.append(jnp.concatenate(parts, axis=0).astype(BF16))
    mine = after(mine, mix_blocks)
    dn = total(mine) + other_row(total(theirs).astype(BF16)).astype(F32)
    dgate = dn[:, MODEL : MODEL + EXPERTS] + dn[:, MODEL + EXPERTS : MODEL + 2 * EXPERTS]
    dlogits = gates * (dgate - jnp.sum(gates * dgate, axis=-1, keepdims=True))
    dnormed_two = dn[:, :MODEL] + jnp.dot(dlogits, router_low.astype(F32).T, precision=EXACT_MATH)
    upstream = cotangent.astype(F32)
    dresid_norm, grad_gain_two = norm_back(residual, inverse_two, norm_gains[1], dnormed_two)
    dresidual = upstream + dresid_norm
    dattn_near = spread_col(dresidual.astype(BF16))
    dattn_far = [other_core(v) for v in dattn_near]

    grad_router = lax.dot_general(
        dlogits, normed_two.astype(F32), (((0,), (0,)), ((), ())), precision=EXACT_MATH
    )
    small = jnp.concatenate(
        [grad_router, grad_gain_two[None], jnp.zeros((SMALL - EXPERTS - 1, MODEL), F32)], axis=0
    )
    dattn_pieces = after(dattn_near + dattn_far, small)
    near, far, *attn_grads = attend_back(
        order,
        spread,
        doc_row,
        doc_col,
        norm_gains[:1],
        small,
        attn_full,
        normed_full,
        qkv,
        att,
        lse,
        dattn_pieces,
    )
    theirs = other_core(far)
    blocks = scatter_blocks(near, theirs)
    small = total([far[GROUP // 2 :], theirs[GROUP // 2 :]]).astype(BF16)
    moved = [across_col(jnp.concatenate([blocks[d], small], axis=0), -d) for d in (1, 2, 3)]
    attn_moved = other_y(after(attn_grads[1], blocks))
    moved, = lax.optimization_barrier((moved,))
    attn_moved = after(attn_moved, moved)
    mix_moved = collect_col(after(mix_blocks, moved))
    pairs = total([small, moved[1][ROWS:]]), total([moved[0][ROWS:], moved[2][ROWS:]])
    small = (pairs[0] + pairs[1]).astype(BF16).reshape(-1, 2 * PAIR)
    dnormed = total([blocks[0]] + [v[:ROWS] for v in moved])
    dtokens_norm, _ = norm_back(residual_in, inverse_one, norm_gains[0], dnormed)
    dtokens = dresidual + dtokens_norm
    halves = total([attn_grads[0], attn_moved]).astype(BF16)
    sent = jnp.concatenate([halves[2:].reshape(-1, 2 * PAIR), small], axis=0)
    kept = jnp.concatenate([halves[:2].reshape(-1, 2 * PAIR), small], axis=0)
    experts_new = update_experts(
        expert_sum, (w_gate_up, gate_up_first, gate_up_second), (w_down, down_first, down_second)
    )
    kept = total([kept, after(along_z(sent, 2), experts_new)]).astype(BF16)
    sent = kept[STORED:]
    kept = jnp.concatenate([kept[:STORED], kept[2 * STORED :]], axis=0)
    kept = total([kept, flip_z(sent)]).astype(BF16)
    kept = add_both(kept, other_row)
    attn_sums = kept[:STORED]
    small = add_both(kept[STORED:], other_y)
    sum_qkv = attn_sums[:, None, :QKV].astype(F32)
    proj_new = update_proj(attn_sums, w_proj, proj_first, proj_second)
    mix_moved = after(mix_moved, dtokens, attn_sums)
    mixed = total(mix_moved)
    mix_theirs = after(other_row(mixed[ROWS:].astype(BF16)), proj_new, small)
    mixture = mixed[:ROWS] + mix_theirs.astype(F32)
    output = (residual + mixture).astype(BF16)
    small = small.reshape(-1, MODEL).astype(F32)
    sum_router = small[:EXPERTS].T
    sum_gains = jnp.stack([small[EXPERTS + 1], small[EXPERTS]])
    return (
        output,
        dtokens,
        *adamw(norm_gains, sum_gains, gain_first, gain_second, RATE_GAIN, 0.0),
        *adamw(router_w, sum_router, router_first, router_second, RATE_ROUTER, DECAY_RATE),
        *adamw(
            projection_weight,
            sum_qkv,
            projection_first_moment,
            projection_second_moment,
            RATE_NARROW,
            DECAY_RATE,
        ),
        *proj_new,
        *experts_new,
    )


def solution(mesh):
    by_token = P(("dp", "row", "col"), None)
    qkv_at, proj_at = P("dp", "col", None), P("col", "dp")
    gate_up_at, down_at = P("col", "dp", None, "row"), P("col", "row", "dp")
    return jax.shard_map(
        per_device,
        mesh=mesh,
        in_specs=(by_token, by_token, P(("dp", "row"), None), by_token)
        + (P(),) * 6
        + (qkv_at,) * 3
        + (proj_at,) * 3
        + (gate_up_at,) * 3
        + (down_at,) * 3,
        out_specs=(by_token, by_token)
        + (P(),) * 6
        + (qkv_at,) * 3
        + (proj_at,) * 3
        + (gate_up_at,) * 3
        + (down_at,) * 3,
        check_vma=False,
    )
```

```python
import functools

import jax
import jax.numpy as jnp
from jax import lax
from jax.experimental import pallas as pl
from jax.experimental.pallas import tpu as pltpu
from jax.sharding import PartitionSpec as P

HEAD_SIZE = 64
STEP = 10
QUERY_PER_KEY = 3
SPAN = QUERY_PER_KEY * HEAD_SIZE
QKV = SPAN + 2 * HEAD_SIZE
MODEL = 1536
ROWS = 128
STORED = 192
GROUP = 1024
PLANE = 2048
FF_DEV = 256
EXPERTS = 40
EXPERTS_DEV = 5
TOP = 8
SLOTS = 112
TILE = 512
PAIR = 256
QUERY_TILE = 512
EXTRA = 128
SMALL = 48
CHUNKS = ((0, 3), (3, 2))

EXACT_MATH = lax.Precision.HIGHEST
NORM_EPS = 1e-05
NEG_FILL = -1e30
BETA_ONE = 0.9
BETA_TWO = 0.95
ADAM_EPS = 1e-08
DECAY_RATE = 0.1
RATE_GAIN = 0.5
RATE_ROUTER = 0.03
RATE_NARROW = 0.05
RATE_WIDE = 0.4
SCALE = HEAD_SIZE ** (-0.5)
F32 = jnp.float32
BF16 = jnp.bfloat16
VMEM_LIMIT = 60 * 1024 * 1024


def row_pairs(stored):
    parts = stored.reshape(EXPERTS_DEV, STORED, 2, FF_DEV // 128, 128)
    return parts.transpose(0, 1, 3, 2, 4).reshape(-1, 128)


def paired_rows(rows):
    parts = rows.reshape(EXPERTS_DEV, STORED, FF_DEV // 128, 2, 128)
    return parts.transpose(0, 1, 3, 2, 4).reshape(EXPERTS_DEV, STORED, 2, FF_DEV)


def adamw_kernel(g_ref, *refs):
    olds, news = refs[:6], refs[6:]
    for half in range(FF_DEV // 128):
        for kind in range(2):
            at = pl.ds(2 * half + kind, STORED // 2, stride=4)
            start = kind * FF_DEV + half * 128
            gradient = g_ref[0, :, start : start + 128].astype(F32)
            weight, first, second = (ref[at, :] for ref in olds[:3])
            results = adamw(weight, gradient, first, second, RATE_NARROW, DECAY_RATE)
            for ref, result in zip(news[:3], results):
                ref[at, :] = result
    gradient = g_ref[0, :, 2 * FF_DEV :].astype(F32)
    weight, first, second = (ref[0] for ref in olds[3:])
    results = adamw(weight, gradient, first, second, RATE_WIDE, DECAY_RATE)
    for ref, result in zip(news[3:], results):
        ref[0] = result


def update_experts(gradient, gate_up, down):
    pair_rows = pl.BlockSpec((2 * STORED, 128), lambda e, i: (2 * e + i, 0))
    down_rows = pl.BlockSpec((1, STORED // 2, FF_DEV), lambda e, i: (e, i, 0))
    specs = [pair_rows] * 3 + [down_rows] * 3
    pair_shape = jax.ShapeDtypeStruct((EXPERTS_DEV * 4 * STORED, 128), F32)
    down_shape = jax.ShapeDtypeStruct((EXPERTS_DEV, STORED, FF_DEV), F32)
    new = pl.pallas_call(
        adamw_kernel,
        grid=(EXPERTS_DEV, 2),
        in_specs=[pl.BlockSpec((1, STORED // 2, 3 * FF_DEV), lambda e, i: (e, i, 0))] + specs,
        out_specs=specs,
        out_shape=[pair_shape] * 3 + [down_shape] * 3,
        cost_estimate=pl.CostEstimate(
            flops=20 * 10**6, bytes_accessed=20 * 10**6, transcendentals=10**6
        ),
        name="update_experts",
    )(gradient, *[row_pairs(v) for v in gate_up], *[v.transpose(0, 2, 1) for v in down])
    return [paired_rows(v) for v in new[:3]] + [v.transpose(0, 2, 1) for v in new[3:]]


def proj_kernel(g_ref, *refs):
    olds, news = refs[:3], refs[3:]
    gradient = g_ref[:, PAIR : 2 * PAIR].astype(F32).T[HEAD_SIZE:]
    weight, first, second = (ref[...] for ref in olds)
    results = adamw(weight, gradient, first, second, RATE_WIDE, DECAY_RATE)
    for ref, result in zip(news, results):
        ref[...] = result


def update_proj(sums, *states):
    return pl.pallas_call(
        proj_kernel,
        out_shape=[jax.ShapeDtypeStruct((SPAN, STORED), F32)] * 3,
        name="update_proj",
    )(sums, *states)


def inv_rms(values):
    return lax.rsqrt(jnp.mean(values * values, axis=-1, keepdims=True) + NORM_EPS)


def adamw(weight, gradient, moment_one, moment_two, step_rate, weight_decay):
    first_new = BETA_ONE * moment_one + (1.0 - BETA_ONE) * gradient
    second_new = BETA_TWO * moment_two + (1.0 - BETA_TWO) * gradient * gradient
    boost_one = 1.0 / (1.0 - BETA_ONE**STEP)
    boost_two = 1.0 / (1.0 - BETA_TWO**STEP)
    direction = first_new * boost_one / (jnp.sqrt(second_new * boost_two) + ADAM_EPS)
    return (weight - step_rate * (direction + weight_decay * weight), first_new, second_new)


def norm_back(values, inverse, gain_row, upstream):
    normalized = values * inverse
    scaled = upstream * gain_row
    grad_gain = jnp.sum(upstream * normalized, axis=0)
    grad_values = inverse * (
        scaled - normalized * jnp.mean(scaled * normalized, axis=-1, keepdims=True)
    )
    return (grad_values, grad_gain)


def dot(a, b):
    return jnp.dot(a, b, preferred_element_type=F32)


def dot_nt(a, b):
    return lax.dot_general(a, b, (((1,), (1,)), ((), ())), preferred_element_type=F32)


def dot_tn(a, b):
    return lax.dot_general(a, b, (((0,), (0,)), ((), ())), preferred_element_type=F32)


def row_blocks(refs):
    blocks = []
    for ref in refs:
        for start in range(0, ref.shape[0], ROWS):
            blocks.append((ref, start))
    return blocks


def place(order_ref, block):
    return pl.ds(pl.multiple_of(order_ref[block] * ROWS, ROWS), ROWS)


def stored_rows(spread_ref, block):
    return pl.ds(pl.multiple_of(spread_ref[block] * STORED, STORED), STORED)


def visible(doc_row_ref, doc_col_ref, tile):
    keys = (tile + 1) * QUERY_TILE
    key_at = lax.broadcasted_iota(jnp.int32, (keys, QUERY_TILE), 0)
    query_at = lax.broadcasted_iota(jnp.int32, (keys, QUERY_TILE), 1) + tile * QUERY_TILE
    same = doc_col_ref[:keys, :] == doc_row_ref[:, tile * QUERY_TILE : keys]
    return same & (key_at <= query_at)


def attend_kernel(order_ref, doc_row_ref, doc_col_ref, *refs):
    normed_ref, qkv_ref, att_ref, lse_ref, near_ref, far_ref = refs[-6:]
    pieces, w_ref = refs[:2], refs[2]
    for block, (ref, start) in enumerate(row_blocks(pieces)):
        normed_ref[place(order_ref, block), :] = ref[start : start + ROWS, :]
    for tile in range(GROUP // QUERY_TILE):
        rows = slice(tile * QUERY_TILE, (tile + 1) * QUERY_TILE)
        qkv_ref[rows, :] = dot(normed_ref[rows, :], w_ref[...])[:, :QKV].astype(BF16)
    keys_all = qkv_ref[:, SPAN : SPAN + HEAD_SIZE]
    values_t = qkv_ref[:, SPAN + HEAD_SIZE : QKV].astype(F32).T.astype(BF16)
    lse_ref[...] = jnp.zeros_like(lse_ref)
    for tile in range(GROUP // QUERY_TILE):
        keys = (tile + 1) * QUERY_TILE
        rows = slice(tile * QUERY_TILE, keys)
        allowed = visible(doc_row_ref, doc_col_ref, tile)
        outs = [jnp.zeros((HEAD_SIZE, QUERY_TILE), F32)]
        for head in range(QUERY_PER_KEY):
            query = qkv_ref[rows, head * HEAD_SIZE : (head + 1) * HEAD_SIZE]
            scores = jnp.where(allowed, dot_nt(keys_all[:keys], query) * SCALE, NEG_FILL)
            peak = jnp.max(scores, axis=0, keepdims=True)
            weights = jnp.exp(scores - peak)
            total = jnp.sum(weights, axis=0, keepdims=True)
            probs = (weights * (1.0 / total)).astype(BF16)
            outs.append(dot(values_t[:, :keys], probs))
            lse_ref[head : head + 1, rows] = peak + jnp.log(total)
        att_ref[rows, :] = jnp.concatenate(outs, axis=0).T.astype(BF16)
    proj = w_ref[:, SPAN + HEAD_SIZE :]
    for side, part_ref in enumerate((near_ref, far_ref)):
        rows = [att_ref[place(order_ref, 4 * side + block), :] for block in range(4)]
        part_ref[...] = dot_nt(jnp.concatenate(rows, axis=0), proj).astype(BF16)


def attend_back_kernel(
    order_ref,
    spread_ref,
    doc_row_ref,
    doc_col_ref,
    gain_ref,
    small_ref,
    w_ref,
    normed_ref,
    qkv_ref,
    att_ref,
    lse_ref,
    *refs,
):
    pieces, refs = refs[:8], refs[8:]
    near_ref, far_ref, *grads_refs = refs[:4]
    dattn_ref, datt_ref, dqkv_ref, dkv_ref, whole_ref = refs[4:]
    for block, (ref, start) in enumerate(row_blocks(pieces)):
        dattn_ref[place(order_ref, block), :] = ref[start : start + ROWS, :]
    proj = w_ref[:, SPAN + HEAD_SIZE :]
    for tile in range(GROUP // QUERY_TILE):
        rows = slice(tile * QUERY_TILE, (tile + 1) * QUERY_TILE)
        datt_ref[rows, :] = dot(dattn_ref[rows, :], proj).astype(BF16)
    keys_all = qkv_ref[:, SPAN : SPAN + HEAD_SIZE]
    values_all = qkv_ref[:, SPAN + HEAD_SIZE : QKV]
    keys_t = keys_all.astype(F32).T.astype(BF16)
    dkv_ref[...] = jnp.zeros_like(dkv_ref)
    for tile in range(GROUP // QUERY_TILE):
        keys = (tile + 1) * QUERY_TILE
        rows = slice(tile * QUERY_TILE, keys)
        allowed = visible(doc_row_ref, doc_col_ref, tile)
        outs = []
        for head in range(QUERY_PER_KEY):
            query = qkv_ref[rows, head * HEAD_SIZE : (head + 1) * HEAD_SIZE]
            dout = datt_ref[rows, (head + 1) * HEAD_SIZE : (head + 2) * HEAD_SIZE]
            scores = jnp.where(allowed, dot_nt(keys_all[:keys], query) * SCALE, NEG_FILL)
            probs = jnp.exp(scores - lse_ref[head : head + 1, rows])
            dprobs = dot_nt(values_all[:keys], dout)
            shift = jnp.sum(probs * dprobs, axis=0, keepdims=True)
            dscores = (probs * (dprobs - shift)).astype(BF16)
            dkv_ref[:keys, :HEAD_SIZE] += dot(dscores, query)
            dkv_ref[:keys, HEAD_SIZE:] += dot(probs.astype(BF16), dout)
            outs.append(dot(keys_t[:, :keys], dscores))
        dqkv_ref[rows, :SPAN] = (jnp.concatenate(outs, axis=0).T * SCALE).astype(BF16)
    dqkv_ref[:, SPAN : SPAN + HEAD_SIZE] = (dkv_ref[:, :HEAD_SIZE] * SCALE).astype(BF16)
    dqkv_ref[:, SPAN + HEAD_SIZE :] = dkv_ref[:, HEAD_SIZE:].astype(BF16)
    qkv_mat = w_ref[:, :QKV]
    dgain = jnp.zeros((1, MODEL), F32)
    for side, part_ref in enumerate((near_ref, far_ref)):
        places = [place(order_ref, 4 * side + block) for block in range(4)]
        rows = jnp.concatenate([dqkv_ref[at, :] for at in places], axis=0)
        part = dot_nt(rows, qkv_mat)
        for block, at in enumerate(places):
            here = part[block * ROWS : (block + 1) * ROWS] * normed_ref[at, :].astype(F32)
            dgain = dgain + jnp.sum(here, axis=0, keepdims=True)
        part_ref[: GROUP // 2, :] = part.astype(BF16)
    small_at = lax.broadcasted_iota(jnp.int32, (SMALL, MODEL), 0)
    small = jnp.where(small_at == EXPERTS + 1, dgain / gain_ref[...], small_ref[...])
    far_ref[GROUP // 2 :, :] = small.astype(BF16)
    for start in range(0, MODEL, PAIR):
        cols = slice(start, start + PAIR)
        qkv_part = dot_tn(dqkv_ref[...], normed_ref[:, cols])
        proj_part = dot_tn(att_ref[...], dattn_ref[:, cols])[HEAD_SIZE:]
        both = jnp.concatenate([qkv_part, proj_part], axis=0)
        whole_ref[cols, :] = both.T.astype(BF16)
    for block in range(8):
        grads_refs[block // 4][block % 4] = whole_ref[stored_rows(spread_ref, block), :]


def vmem_spec():
    return pl.BlockSpec(memory_space=pltpu.VMEM)


def smem_spec():
    return pl.BlockSpec(memory_space=pltpu.SMEM)


def attend(order, doc_row, doc_col, pieces, weights):
    return pl.pallas_call(
        attend_kernel,
        in_specs=[smem_spec()] + [vmem_spec()] * (3 + len(pieces)),
        out_specs=[vmem_spec()] * 6,
        out_shape=[
            jax.ShapeDtypeStruct((GROUP, MODEL), BF16),
            jax.ShapeDtypeStruct((GROUP, QKV), BF16),
            jax.ShapeDtypeStruct((GROUP, PAIR), BF16),
            jax.ShapeDtypeStruct((8, GROUP), F32),
            jax.ShapeDtypeStruct((GROUP // 2, MODEL), BF16),
            jax.ShapeDtypeStruct((GROUP // 2, MODEL), BF16),
        ],
        compiler_params=pltpu.CompilerParams(vmem_limit_bytes=VMEM_LIMIT),
        cost_estimate=pl.CostEstimate(
            flops=10**6, bytes_accessed=10**5, transcendentals=0
        ),
        name="attend",
    )(order, doc_row, doc_col, *pieces, weights)


def attend_back(order, spread, doc_row, doc_col, gain, small, weights, normed, qkv, att, lse, pieces):
    return pl.pallas_call(
        attend_back_kernel,
        in_specs=[smem_spec()] * 2 + [vmem_spec()] * (9 + len(pieces)),
        out_specs=[vmem_spec()] * 4,
        out_shape=[
            jax.ShapeDtypeStruct((GROUP // 2, MODEL), BF16),
            jax.ShapeDtypeStruct((GROUP // 2 + SMALL, MODEL), BF16),
        ]
        + [jax.ShapeDtypeStruct((4, STORED, 2 * PAIR), BF16)] * 2,
        scratch_shapes=[
            pltpu.VMEM((GROUP, MODEL), BF16),
            pltpu.VMEM((GROUP, PAIR), BF16),
            pltpu.VMEM((GROUP, QKV), BF16),
            pltpu.VMEM((GROUP, 2 * HEAD_SIZE), F32),
            pltpu.VMEM((MODEL, 2 * PAIR), BF16),
        ],
        compiler_params=pltpu.CompilerParams(vmem_limit_bytes=VMEM_LIMIT),
        cost_estimate=pl.CostEstimate(
            flops=10**6, bytes_accessed=10**5, transcendentals=0
        ),
        name="attend_back",
    )(order, spread, doc_row, doc_col, gain, small, weights, normed, qkv, att, lse, *pieces)


def moe_kernel(first_ref, router_ref, stored_ref, *refs, begin, count, more):
    sources, refs = (refs[:4], refs[4:8]), refs[8:]
    if more:
        prev_out_ref, prev_dn_ref = refs[:2]
        refs = refs[3:]
        outs, refs = (refs[:2], refs[2:4]), refs[4:]
    else:
        out_ref, dn_ref = refs[:2]
        refs = refs[2:]
    g_ref, in_all, dout_all, hid_all, dgu_all, held_t, held_c, sems, done, done_sems = refs[:10]
    w_ref, w_sems = refs[10:]
    step = pl.program_id(0)
    pairs = TILE // PAIR
    height = pairs * SLOTS
    last = PLANE // TILE - 1

    def copies(tile):
        return [
            pltpu.make_async_copy(
                sources[kind][tile], held.at[tile % 2], sems.at[kind, tile % 2]
            )
            for kind, held in enumerate((held_t, held_c))
        ]

    def fetch(e):
        return pltpu.make_async_copy(stored_ref.at[:, e], w_ref.at[:, e], w_sems.at[e])

    for tile in range(last + 1):

        @pl.when(step == max(tile - 1, 0))
        def _():
            for copy in copies(tile):
                copy.start()
            if tile == 0:
                for e in range(count):
                    fetch(e).start()

    for tile in range(last + 1):

        @pl.when(step == tile)
        def _():
            for copy in copies(tile):
                copy.wait()

    t_ref, c_ref = held_t.at[lax.rem(step, 2)], held_c.at[lax.rem(step, 2)]
    ids = c_ref[:, MODEL:].astype(F32).T.astype(jnp.int32)
    expert_at = lax.broadcasted_iota(jnp.int32, (EXPERTS, TILE), 0) + first_ref[0]
    expert_at = jnp.where(expert_at >= EXPERTS, expert_at - EXPERTS, expert_at)
    hits = ids[:1] == expert_at
    for choice in range(1, TOP):
        hits = hits | (ids[choice : choice + 1] == expert_at)
    mine = jnp.where(hits[:8], 1.0, 0.0)
    upto = lax.broadcasted_iota(jnp.int32, (PAIR, PAIR), 0) <= lax.broadcasted_iota(
        jnp.int32, (PAIR, PAIR), 1
    )
    upto = jnp.where(upto, 1.0, 0.0).astype(BF16)
    ranks = []
    for pair in range(pairs):
        here = mine[:, pair * PAIR : (pair + 1) * PAIR]
        ranks.append(jnp.where(here > 0.5, dot(here.astype(BF16), upto) - 1.0, -1.0).astype(jnp.int32))
    spot = pl.ds(pl.multiple_of(step * height, 16), height)
    logits = jnp.where(hits, dot_nt(router_ref[...], t_ref[...]), NEG_FILL)
    logits = jnp.exp(logits - jnp.max(logits, axis=0, keepdims=True))
    gates = logits / jnp.sum(logits, axis=0, keepdims=True)
    slot_at = lax.broadcasted_iota(jnp.int32, (SLOTS, PAIR), 0)
    picks, slot_gates, ins, cots = [], [], [], []
    for pair in range(pairs):
        cols = slice(pair * PAIR, (pair + 1) * PAIR)
        taken = [slot_at == ranks[pair][begin + e : begin + e + 1, :] for e in range(count)]
        slot_gates.append(
            [
                jnp.sum(
                    jnp.where(taken[e], gates[begin + e : begin + e + 1, cols], 0.0),
                    axis=1,
                    keepdims=True,
                )
                for e in range(count)
            ]
        )
        pick = jnp.concatenate([jnp.where(h, 1.0, 0.0).astype(BF16) for h in taken], axis=0)
        picks.append(pick)
        ins.append(dot(pick, t_ref[cols, :]).astype(BF16))
        cots.append(dot(pick, c_ref[cols, :MODEL]).astype(BF16))
    mixed = [[] for _ in range(pairs)]
    dins = [[] for _ in range(pairs)]
    lane = lax.broadcasted_iota(jnp.int32, (height, EXTRA), 1)
    for e in range(count):
        part = slice(e * SLOTS, (e + 1) * SLOTS)

        @pl.when(step == 0)
        def _():
            fetch(e).wait()

        rows_in = jnp.concatenate([v[part] for v in ins], axis=0)
        rows_cot = jnp.concatenate([v[part] for v in cots], axis=0)
        gate = jnp.concatenate([v[e] for v in slot_gates], axis=0)
        gate_up_w = w_ref[:, e, :, : 2 * FF_DEV].reshape(MODEL, 2 * FF_DEV)
        down_w = w_ref[:, e, :, 2 * FF_DEV :].reshape(MODEL, FF_DEV)
        gate_up = dot(rows_in, gate_up_w)
        pre, up = gate_up[:, :FF_DEV], gate_up[:, FF_DEV:]
        sig = 0.5 * jnp.tanh(0.5 * pre) + 0.5
        silu = pre * sig
        hidden = (silu * up).astype(BF16)
        plain = dot(rows_cot, down_w)
        dgate = jnp.sum(hidden.astype(F32) * plain, axis=1, keepdims=True)
        dhidden = plain * gate
        dpre = dhidden * up * sig * (1.0 + pre * (1.0 - sig))
        dgu = jnp.concatenate([dpre, dhidden * silu], axis=1).astype(BF16)
        in_all[e, spot, :] = rows_in
        dout_all[e, spot, :] = (rows_cot.astype(F32) * gate).astype(BF16)
        hid_all[e, spot, :] = hidden
        dgu_all[e, spot, :] = dgu
        mix = (dot_nt(hidden, down_w) * gate).astype(BF16)
        din = dot_nt(dgu, gate_up_w).astype(BF16)
        high = dgate.astype(BF16).astype(F32)
        tail = jnp.where(lane == first_ref[0] + (begin + e), high, 0.0) + jnp.where(
            lane == first_ref[0] + (begin + e + EXPERTS), dgate - high, 0.0
        )
        din = jnp.concatenate([din, tail.astype(BF16)], axis=1)
        for pair in range(pairs):
            rows = slice(pair * SLOTS, (pair + 1) * SLOTS)
            mixed[pair].append(mix[rows])
            dins[pair].append(din[rows])
    for pair in range(pairs):
        cols = slice(pair * PAIR, (pair + 1) * PAIR)
        out = dot_tn(picks[pair], jnp.concatenate(mixed[pair], axis=0))
        dn = dot_tn(picks[pair], jnp.concatenate(dins[pair], axis=0))
        if more:
            out = out + prev_out_ref[cols, :].astype(F32)
            dn = dn + prev_dn_ref[cols, :].astype(F32)
        if not more:
            out_ref[cols, :] = out.astype(BF16)
            dn_ref[cols, :] = dn.astype(BF16)
            continue

        for side in range(2):

            @pl.when(step // 2 == side)
            def _():
                outs[side][0][cols, :] = out.astype(BF16)
                outs[side][1][cols, :] = dn.astype(BF16)

    @pl.when(step == last)
    def _():
        sent = []
        for e in range(count):
            if e >= 2:
                sent[e - 2].wait()
            for start in range(0, MODEL, 2 * STORED):
                cols = slice(start, start + 2 * STORED)
                gate_up_g = dot_tn(in_all[e, :, cols], dgu_all[e])
                down_g = dot_tn(dout_all[e, :, cols], hid_all[e])
                both = jnp.concatenate([gate_up_g, down_g], axis=1).astype(BF16)
                for half in range(2):
                    at = slice(half * STORED, (half + 1) * STORED)
                    done[e % 2, start // STORED + half, :, :] = both[at, :]
            sent.append(
                pltpu.make_async_copy(done.at[e % 2], g_ref.at[:, begin + e], done_sems.at[e % 2])
            )
            sent[e].start()
        for copy in sent[-2:]:
            copy.wait()


def moe(chunk, first, router_t, weights, rows, cots, previous):
    begin, count = chunk
    height = PLANE // PAIR * SLOTS
    wide = pl.BlockSpec((TILE, MODEL), lambda i: (i, 0))
    wider = pl.BlockSpec((TILE, MODEL + EXTRA), lambda i: (i, 0))
    if previous is None:
        sums = [wide, wider]
        shapes = [(PLANE, MODEL), (PLANE, MODEL + EXTRA)]
    else:
        sides = (lambda i: (jnp.minimum(i, 1), 0)), (lambda i: (jnp.maximum(i - 2, 0), 0))
        sums = [pl.BlockSpec((TILE, w), side) for side in sides for w in (MODEL, MODEL + EXTRA)]
        shapes = [(PLANE // 2, MODEL), (PLANE // 2, MODEL + EXTRA)] * 2
    flops = 2 * count * height * MODEL * (9 * FF_DEV + 5 * PAIR)
    return pl.pallas_call(
        functools.partial(moe_kernel, begin=begin, count=count, more=previous is not None),
        grid=(PLANE // TILE,),
        in_specs=[
            smem_spec(),
            pl.BlockSpec((EXPERTS, MODEL), lambda i: (0, 0)),
            pl.BlockSpec(memory_space=pl.ANY),
        ]
        + [pl.BlockSpec(memory_space=pl.ANY)] * 8
        + ([wide, wider, pl.BlockSpec(memory_space=pl.ANY)] if previous is not None else []),
        out_specs=sums + [pl.BlockSpec(memory_space=pl.ANY)],
        out_shape=[jax.ShapeDtypeStruct(shape, BF16) for shape in shapes]
        + [
            jax.ShapeDtypeStruct((8, EXPERTS_DEV, STORED, 3 * FF_DEV), BF16),
        ],
        input_output_aliases={} if previous is None else {13: 4},
        scratch_shapes=[
            pltpu.VMEM((count, height, MODEL), BF16),
            pltpu.VMEM((count, height, MODEL), BF16),
            pltpu.VMEM((count, height, FF_DEV), BF16),
            pltpu.VMEM((count, height, 2 * FF_DEV), BF16),
            pltpu.VMEM((2, TILE, MODEL), BF16),
            pltpu.VMEM((2, TILE, MODEL + EXTRA), BF16),
            pltpu.SemaphoreType.DMA((2, 2)),
            pltpu.VMEM((2, 8, STORED, 3 * FF_DEV), BF16),
            pltpu.SemaphoreType.DMA((2,)),
            pltpu.VMEM((8, count, STORED, 3 * FF_DEV), BF16),
            pltpu.SemaphoreType.DMA((count,)),
        ],
        compiler_params=pltpu.CompilerParams(vmem_limit_bytes=VMEM_LIMIT),
        cost_estimate=pl.CostEstimate(
            flops=10**6, bytes_accessed=10**5, transcendentals=0
        ),
        name="moe",
    )(first, router_t, weights, *rows, *cots, *(previous or ()))


def across_col(value, distance):
    pairs = [(2 * x + c, 2 * ((x + distance) % 4) + c) for x in range(4) for c in range(2)]
    return lax.ppermute(value, "col", pairs)


def other_core(value):
    return lax.ppermute(value, "col", [(s, s ^ 1) for s in range(8)])


def other_row(value):
    return lax.ppermute(value, "row", [(0, 1), (1, 0)])


def along_z(value, distance):
    pairs = [(4 * y + z, 4 * y + (z + distance) % 4) for y in range(2) for z in range(4)]
    return lax.ppermute(value, "dp", pairs)


def other_y(value):
    return lax.ppermute(value, "dp", [(s, s ^ 4) for s in range(8)])


def total(values):
    result = values[0].astype(F32)
    for value in values[1:]:
        result = result + value.astype(F32)
    return result


def after(value, *before):
    return lax.optimization_barrier((value, before))[0]


def spread_col(value):
    return [value] + [across_col(value, d) for d in (1, 2, 3)]


def relay_col(value):
    ahead, behind = across_col(value, 1), across_col(value, -1)
    half = value.shape[0] // 2
    opposite = [across_col(ahead[:half], 1), across_col(behind[half:], -1)]
    return [value, ahead, jnp.concatenate(opposite, axis=0), behind]


def gather_col(value):
    near = spread_col(value)
    return near + [other_core(v) for v in near]


def scatter_blocks(near, far):
    sums = [
        total([near[d * ROWS : (d + 1) * ROWS], far[d * ROWS : (d + 1) * ROWS]]) for d in range(4)
    ]
    return sums[:1] + [v.astype(BF16) for v in sums[1:]]


def collect_col(blocks):
    return [blocks[0]] + [across_col(blocks[d], -d) for d in (1, 2, 3)]


def flip_x(value):
    return lax.ppermute(value, "col", [(s, s ^ 2) for s in range(8)])


def flip_z(value):
    return lax.ppermute(value, "dp", [(s, s ^ 1) for s in range(8)])


def add_both(value, move):
    return (value.astype(F32) + move(value).astype(F32)).astype(value.dtype)


def per_device(
    tokens,
    cotangent,
    lengths,
    routes,
    norm_gains,
    gain_first,
    gain_second,
    router_w,
    router_first,
    router_second,
    projection_weight,
    projection_first_moment,
    projection_second_moment,
    w_proj,
    proj_first,
    proj_second,
    w_gate_up,
    gate_up_first,
    gate_up_second,
    w_down,
    down_first,
    down_second,
):
    col, row, dp = lax.axis_index("col"), lax.axis_index("row"), lax.axis_index("dp")
    across, core = col // 2, col % 2
    steps = jnp.arange(4, dtype=jnp.int32)
    away = 2 * jnp.remainder(across - steps, 4)
    order = jnp.concatenate([away + core, away + 1 - core])
    spread = jnp.bitwise_xor(dp, jnp.arange(8, dtype=jnp.int32))
    token_places = jnp.arange(GROUP, dtype=jnp.int32)
    doc_ends = jnp.cumsum(lengths[0])
    documents = jnp.sum((token_places[:, None] >= doc_ends[None, :]).astype(jnp.int32), axis=1)
    doc_row, doc_col = documents[None, :], documents[:, None]

    residual_in = tokens.astype(F32)
    inverse_one = inv_rms(residual_in)
    normed_one = (residual_in * inverse_one * norm_gains[0]).astype(BF16)
    attn_w = jnp.concatenate([projection_weight[:, 0, :], w_proj.T], axis=1).astype(BF16)
    normed_near = relay_col(normed_one)
    normed_near = jnp.concatenate(normed_near, axis=0)
    normed_pieces = [normed_near, other_core(normed_near)]
    attn_full = lax.all_gather(attn_w, "dp", axis=0, tiled=True)

    gate_up_w, down_w = after((w_gate_up, w_down), attn_w, normed_one)
    expert_w = jnp.concatenate(
        [gate_up_w.reshape(EXPERTS_DEV, 192, 2 * FF_DEV), down_w.transpose(0, 2, 1)], axis=2
    ).astype(BF16)
    expert_ws = []
    for b, n in CHUNKS:
        expert_ws.append(lax.all_gather(expert_w[b : b + n], "dp", axis=0, tiled=False))

    tagged = jnp.concatenate(
        [cotangent, routes.astype(BF16), jnp.zeros((ROWS, EXTRA - routes.shape[1]), BF16)], axis=1
    )
    cots = [jnp.concatenate(relay_col(tagged), axis=0)]
    theirs = other_row(tagged)
    cots.append(jnp.concatenate(relay_col(theirs), axis=0))
    attn_full = after(attn_full, normed_pieces, cots)
    normed_full, qkv, att, lse, near, far = attend(
        order, doc_row, doc_col, normed_pieces, attn_full
    )
    attn_out = total(collect_col(scatter_blocks(near, other_core(far))))
    cots = cots + [other_core(v) for v in cots]
    router_low = router_w.astype(BF16)
    router_t = jnp.roll(router_low.T, -EXPERTS_DEV * col, axis=0)
    first = (EXPERTS_DEV * col).astype(jnp.int32).reshape(1)

    residual = residual_in + attn_out
    inverse_two = inv_rms(residual)
    normed_two = (residual * inverse_two * norm_gains[1]).astype(BF16)
    normed_two = after(normed_two, cots)
    rows_all = [
        jnp.concatenate(relay_col(v), axis=0) for v in (normed_two, other_row(normed_two))
    ]
    rows_all = rows_all + [other_core(v) for v in rows_all]
    logits = jnp.dot(normed_two, router_low, preferred_element_type=F32)
    route_hits = jnp.any(
        routes[:, None, :] == jnp.arange(EXPERTS, dtype=jnp.int32)[None, :, None], axis=-1
    )
    gates = jax.nn.softmax(jnp.where(route_hits, logits, NEG_FILL), axis=-1)

    previous = None
    for chunk, weights in zip(CHUNKS, expert_ws):
        previous = moe(chunk, first, router_t, weights, rows_all, cots, previous)
    mix_near, dn_near, mix_far, dn_far, expert_grads = previous
    expert_sum = lax.psum_scatter(expert_grads, "dp", scatter_dimension=0, tiled=False)

    far = other_core(dn_far)
    theirs = collect_col(scatter_blocks(dn_near[TILE:], far[TILE:]))
    mine = collect_col(scatter_blocks(dn_near[:TILE], far[:TILE]))
    mix_far = other_core(after(mix_far, far))
    mix_blocks = []
    for d in range(4):
        parts = [slice(start + d * ROWS, start + (d + 1) * ROWS) for start in (0, TILE)]
        parts = [total([mix_near[part], mix_far[part]]) for part in parts]
        mix_blocks.append(jnp.concatenate(parts, axis=0).astype(BF16))
    mine = after(mine, mix_blocks)
    dn = total(mine) + other_row(total(theirs).astype(BF16)).astype(F32)
    dgate = dn[:, MODEL : MODEL + EXPERTS] + dn[:, MODEL + EXPERTS : MODEL + 2 * EXPERTS]
    dlogits = gates * (dgate - jnp.sum(gates * dgate, axis=-1, keepdims=True))
    dnormed_two = dn[:, :MODEL] + jnp.dot(dlogits, router_low.astype(F32).T, precision=EXACT_MATH)
    upstream = cotangent.astype(F32)
    dresid_norm, grad_gain_two = norm_back(residual, inverse_two, norm_gains[1], dnormed_two)
    dresidual = upstream + dresid_norm
    dattn_near = spread_col(dresidual.astype(BF16))
    dattn_far = [other_core(v) for v in dattn_near]

    grad_router = lax.dot_general(
        dlogits, normed_two.astype(F32), (((0,), (0,)), ((), ())), precision=EXACT_MATH
    )
    small = jnp.concatenate(
        [grad_router, grad_gain_two[None], jnp.zeros((SMALL - EXPERTS - 1, MODEL), F32)], axis=0
    )
    dattn_pieces = after(dattn_near + dattn_far, small)
    near, far, *attn_grads = attend_back(
        order,
        spread,
        doc_row,
        doc_col,
        norm_gains[:1],
        small,
        attn_full,
        normed_full,
        qkv,
        att,
        lse,
        dattn_pieces,
    )
    theirs = other_core(far)
    blocks = scatter_blocks(near, theirs)
    small = total([far[GROUP // 2 :], theirs[GROUP // 2 :]]).astype(BF16)
    moved = [across_col(jnp.concatenate([blocks[d], small], axis=0), -d) for d in (1, 2, 3)]
    attn_moved = other_y(after(attn_grads[1], blocks))
    moved, = lax.optimization_barrier((moved,))
    attn_moved = after(attn_moved, moved)
    mix_moved = collect_col(after(mix_blocks, moved))
    pairs = total([small, moved[1][ROWS:]]), total([moved[0][ROWS:], moved[2][ROWS:]])
    small = (pairs[0] + pairs[1]).astype(BF16).reshape(-1, 2 * PAIR)
    dnormed = total([blocks[0]] + [v[:ROWS] for v in moved])
    dtokens_norm, _ = norm_back(residual_in, inverse_one, norm_gains[0], dnormed)
    dtokens = dresidual + dtokens_norm
    halves = total([attn_grads[0], attn_moved]).astype(BF16)
    sent = jnp.concatenate([halves[2:].reshape(-1, 2 * PAIR), small], axis=0)
    kept = jnp.concatenate([halves[:2].reshape(-1, 2 * PAIR), small], axis=0)
    experts_new = update_experts(
        expert_sum, (w_gate_up, gate_up_first, gate_up_second), (w_down, down_first, down_second)
    )
    kept = total([kept, after(along_z(sent, 2), experts_new)]).astype(BF16)
    mix_moved = after(mix_moved, kept)
    sent = kept[STORED:]
    kept = jnp.concatenate([kept[:STORED], kept[2 * STORED :]], axis=0)
    kept = total([kept, flip_z(sent)]).astype(BF16)
    kept = add_both(kept, other_row)
    attn_sums = kept[:STORED]
    small = add_both(kept[STORED:], other_y)
    sum_qkv = attn_sums[:, None, :QKV].astype(F32)
    proj_new = update_proj(attn_sums, w_proj, proj_first, proj_second)
    mixed = total(mix_moved)
    mix_theirs = after(other_row(mixed[ROWS:].astype(BF16)), proj_new, small)
    mixture = mixed[:ROWS] + mix_theirs.astype(F32)
    output = (residual + mixture).astype(BF16)
    small = small.reshape(-1, MODEL).astype(F32)
    sum_router = small[:EXPERTS].T
    sum_gains = jnp.stack([small[EXPERTS + 1], small[EXPERTS]])
    return (
        output,
        dtokens,
        *adamw(norm_gains, sum_gains, gain_first, gain_second, RATE_GAIN, 0.0),
        *adamw(router_w, sum_router, router_first, router_second, RATE_ROUTER, DECAY_RATE),
        *adamw(
            projection_weight,
            sum_qkv,
            projection_first_moment,
            projection_second_moment,
            RATE_NARROW,
            DECAY_RATE,
        ),
        *proj_new,
        *experts_new,
    )


def solution(mesh):
    by_token = P(("dp", "row", "col"), None)
    qkv_at, proj_at = P("dp", "col", None), P("col", "dp")
    gate_up_at, down_at = P("col", "dp", None, "row"), P("col", "row", "dp")
    return jax.shard_map(
        per_device,
        mesh=mesh,
        in_specs=(by_token, by_token, P(("dp", "row"), None), by_token)
        + (P(),) * 6
        + (qkv_at,) * 3
        + (proj_at,) * 3
        + (gate_up_at,) * 3
        + (down_at,) * 3,
        out_specs=(by_token, by_token)
        + (P(),) * 6
        + (qkv_at,) * 3
        + (proj_at,) * 3
        + (gate_up_at,) * 3
        + (down_at,) * 3,
        check_vma=False,
    )
```

```python
import functools

import jax
import jax.numpy as jnp
from jax import lax
from jax.experimental import pallas as pl
from jax.experimental.pallas import tpu as pltpu
from jax.sharding import PartitionSpec as P

HEAD_SIZE = 64
STEP = 10
QUERY_PER_KEY = 3
SPAN = QUERY_PER_KEY * HEAD_SIZE
QKV = SPAN + 2 * HEAD_SIZE
MODEL = 1536
ROWS = 128
STORED = 192
GROUP = 1024
PLANE = 2048
FF_DEV = 256
EXPERTS = 40
EXPERTS_DEV = 5
TOP = 8
SLOTS = 112
TILE = 512
PAIR = 256
QUERY_TILE = 512
EXTRA = 128
SMALL = 48
CHUNKS = ((0, 3), (3, 2))

EXACT_MATH = lax.Precision.HIGHEST
NORM_EPS = 1e-05
NEG_FILL = -1e30
BETA_ONE = 0.9
BETA_TWO = 0.95
ADAM_EPS = 1e-08
DECAY_RATE = 0.1
RATE_GAIN = 0.5
RATE_ROUTER = 0.03
RATE_NARROW = 0.05
RATE_WIDE = 0.4
SCALE = HEAD_SIZE ** (-0.5)
F32 = jnp.float32
BF16 = jnp.bfloat16
VMEM_LIMIT = 60 * 1024 * 1024


def row_pairs(stored):
    parts = stored.reshape(EXPERTS_DEV, STORED, 2, FF_DEV // 128, 128)
    return parts.transpose(0, 1, 3, 2, 4).reshape(-1, 128)


def paired_rows(rows):
    parts = rows.reshape(EXPERTS_DEV, STORED, FF_DEV // 128, 2, 128)
    return parts.transpose(0, 1, 3, 2, 4).reshape(EXPERTS_DEV, STORED, 2, FF_DEV)


def adamw_kernel(g_ref, *refs):
    olds, news = refs[:6], refs[6:]
    for half in range(FF_DEV // 128):
        for kind in range(2):
            at = pl.ds(2 * half + kind, STORED, stride=4)
            start = kind * FF_DEV + half * 128
            gradient = g_ref[0, :, start : start + 128].astype(F32)
            weight, first, second = (ref[at, :] for ref in olds[:3])
            results = adamw(weight, gradient, first, second, RATE_NARROW, DECAY_RATE)
            for ref, result in zip(news[:3], results):
                ref[at, :] = result
    gradient = g_ref[0, :, 2 * FF_DEV :].astype(F32)
    weight, first, second = (ref[0] for ref in olds[3:])
    results = adamw(weight, gradient, first, second, RATE_WIDE, DECAY_RATE)
    for ref, result in zip(news[3:], results):
        ref[0] = result


def update_experts(gradient, gate_up, down):
    pair_rows = pl.BlockSpec((4 * STORED, 128), lambda i: (i, 0))
    down_rows = pl.BlockSpec((1, STORED, FF_DEV), lambda i: (i, 0, 0))
    specs = [pair_rows] * 3 + [down_rows] * 3
    pair_shape = jax.ShapeDtypeStruct((EXPERTS_DEV * 4 * STORED, 128), F32)
    down_shape = jax.ShapeDtypeStruct((EXPERTS_DEV, STORED, FF_DEV), F32)
    new = pl.pallas_call(
        adamw_kernel,
        grid=(EXPERTS_DEV,),
        in_specs=[pl.BlockSpec((1, STORED, 3 * FF_DEV), lambda i: (i, 0, 0))] + specs,
        out_specs=specs,
        out_shape=[pair_shape] * 3 + [down_shape] * 3,
        cost_estimate=pl.CostEstimate(
            flops=20 * 10**6, bytes_accessed=20 * 10**6, transcendentals=10**6
        ),
        name="update_experts",
    )(gradient, *[row_pairs(v) for v in gate_up], *[v.transpose(0, 2, 1) for v in down])
    return [paired_rows(v) for v in new[:3]] + [v.transpose(0, 2, 1) for v in new[3:]]


def proj_kernel(g_ref, *refs):
    olds, news = refs[:3], refs[3:]
    gradient = g_ref[:, PAIR : 2 * PAIR].astype(F32).T[HEAD_SIZE:]
    weight, first, second = (ref[...] for ref in olds)
    results = adamw(weight, gradient, first, second, RATE_WIDE, DECAY_RATE)
    for ref, result in zip(news, results):
        ref[...] = result


def update_proj(sums, *states):
    return pl.pallas_call(
        proj_kernel,
        out_shape=[jax.ShapeDtypeStruct((SPAN, STORED), F32)] * 3,
        name="update_proj",
    )(sums, *states)


def inv_rms(values):
    return lax.rsqrt(jnp.mean(values * values, axis=-1, keepdims=True) + NORM_EPS)


def adamw(weight, gradient, moment_one, moment_two, step_rate, weight_decay):
    first_new = BETA_ONE * moment_one + (1.0 - BETA_ONE) * gradient
    second_new = BETA_TWO * moment_two + (1.0 - BETA_TWO) * gradient * gradient
    boost_one = 1.0 / (1.0 - BETA_ONE**STEP)
    boost_two = 1.0 / (1.0 - BETA_TWO**STEP)
    direction = first_new * boost_one / (jnp.sqrt(second_new * boost_two) + ADAM_EPS)
    return (weight - step_rate * (direction + weight_decay * weight), first_new, second_new)


def norm_back(values, inverse, gain_row, upstream):
    normalized = values * inverse
    scaled = upstream * gain_row
    grad_gain = jnp.sum(upstream * normalized, axis=0)
    grad_values = inverse * (
        scaled - normalized * jnp.mean(scaled * normalized, axis=-1, keepdims=True)
    )
    return (grad_values, grad_gain)


def dot(a, b):
    return jnp.dot(a, b, preferred_element_type=F32)


def dot_nt(a, b):
    return lax.dot_general(a, b, (((1,), (1,)), ((), ())), preferred_element_type=F32)


def dot_tn(a, b):
    return lax.dot_general(a, b, (((0,), (0,)), ((), ())), preferred_element_type=F32)


def row_blocks(refs):
    blocks = []
    for ref in refs:
        for start in range(0, ref.shape[0], ROWS):
            blocks.append((ref, start))
    return blocks


def place(order_ref, block):
    return pl.ds(pl.multiple_of(order_ref[block] * ROWS, ROWS), ROWS)


def stored_rows(spread_ref, block):
    return pl.ds(pl.multiple_of(spread_ref[block] * STORED, STORED), STORED)


def visible(doc_row_ref, doc_col_ref, tile):
    keys = (tile + 1) * QUERY_TILE
    key_at = lax.broadcasted_iota(jnp.int32, (keys, QUERY_TILE), 0)
    query_at = lax.broadcasted_iota(jnp.int32, (keys, QUERY_TILE), 1) + tile * QUERY_TILE
    same = doc_col_ref[:keys, :] == doc_row_ref[:, tile * QUERY_TILE : keys]
    return same & (key_at <= query_at)


def attend_kernel(order_ref, doc_row_ref, doc_col_ref, *refs):
    normed_ref, qkv_ref, att_ref, lse_ref, near_ref, far_ref = refs[-6:]
    pieces, w_ref = refs[:2], refs[2]
    for block, (ref, start) in enumerate(row_blocks(pieces)):
        normed_ref[place(order_ref, block), :] = ref[start : start + ROWS, :]
    for tile in range(GROUP // QUERY_TILE):
        rows = slice(tile * QUERY_TILE, (tile + 1) * QUERY_TILE)
        qkv_ref[rows, :] = dot(normed_ref[rows, :], w_ref[...])[:, :QKV].astype(BF16)
    keys_all = qkv_ref[:, SPAN : SPAN + HEAD_SIZE]
    values_t = qkv_ref[:, SPAN + HEAD_SIZE : QKV].astype(F32).T.astype(BF16)
    lse_ref[...] = jnp.zeros_like(lse_ref)
    for tile in range(GROUP // QUERY_TILE):
        keys = (tile + 1) * QUERY_TILE
        rows = slice(tile * QUERY_TILE, keys)
        allowed = visible(doc_row_ref, doc_col_ref, tile)
        outs = [jnp.zeros((HEAD_SIZE, QUERY_TILE), F32)]
        for head in range(QUERY_PER_KEY):
            query = qkv_ref[rows, head * HEAD_SIZE : (head + 1) * HEAD_SIZE]
            scores = jnp.where(allowed, dot_nt(keys_all[:keys], query) * SCALE, NEG_FILL)
            peak = jnp.max(scores, axis=0, keepdims=True)
            weights = jnp.exp(scores - peak)
            total = jnp.sum(weights, axis=0, keepdims=True)
            probs = (weights * (1.0 / total)).astype(BF16)
            outs.append(dot(values_t[:, :keys], probs))
            lse_ref[head : head + 1, rows] = peak + jnp.log(total)
        att_ref[rows, :] = jnp.concatenate(outs, axis=0).T.astype(BF16)
    proj = w_ref[:, SPAN + HEAD_SIZE :]
    for side, part_ref in enumerate((near_ref, far_ref)):
        rows = [att_ref[place(order_ref, 4 * side + block), :] for block in range(4)]
        part_ref[...] = dot_nt(jnp.concatenate(rows, axis=0), proj).astype(BF16)


def attend_back_kernel(
    order_ref,
    spread_ref,
    doc_row_ref,
    doc_col_ref,
    gain_ref,
    small_ref,
    w_ref,
    normed_ref,
    qkv_ref,
    att_ref,
    lse_ref,
    *refs,
):
    pieces, refs = refs[:8], refs[8:]
    near_ref, far_ref, *grads_refs = refs[:4]
    dattn_ref, datt_ref, dqkv_ref, dkv_ref, whole_ref = refs[4:]
    for block, (ref, start) in enumerate(row_blocks(pieces)):
        dattn_ref[place(order_ref, block), :] = ref[start : start + ROWS, :]
    proj = w_ref[:, SPAN + HEAD_SIZE :]
    for tile in range(GROUP // QUERY_TILE):
        rows = slice(tile * QUERY_TILE, (tile + 1) * QUERY_TILE)
        datt_ref[rows, :] = dot(dattn_ref[rows, :], proj).astype(BF16)
    keys_all = qkv_ref[:, SPAN : SPAN + HEAD_SIZE]
    values_all = qkv_ref[:, SPAN + HEAD_SIZE : QKV]
    keys_t = keys_all.astype(F32).T.astype(BF16)
    dkv_ref[...] = jnp.zeros_like(dkv_ref)
    for tile in range(GROUP // QUERY_TILE):
        keys = (tile + 1) * QUERY_TILE
        rows = slice(tile * QUERY_TILE, keys)
        allowed = visible(doc_row_ref, doc_col_ref, tile)
        outs = []
        for head in range(QUERY_PER_KEY):
            query = qkv_ref[rows, head * HEAD_SIZE : (head + 1) * HEAD_SIZE]
            dout = datt_ref[rows, (head + 1) * HEAD_SIZE : (head + 2) * HEAD_SIZE]
            scores = jnp.where(allowed, dot_nt(keys_all[:keys], query) * SCALE, NEG_FILL)
            probs = jnp.exp(scores - lse_ref[head : head + 1, rows])
            dprobs = dot_nt(values_all[:keys], dout)
            shift = jnp.sum(probs * dprobs, axis=0, keepdims=True)
            dscores = (probs * (dprobs - shift)).astype(BF16)
            dkv_ref[:keys, :HEAD_SIZE] += dot(dscores, query)
            dkv_ref[:keys, HEAD_SIZE:] += dot(probs.astype(BF16), dout)
            outs.append(dot(keys_t[:, :keys], dscores))
        dqkv_ref[rows, :SPAN] = (jnp.concatenate(outs, axis=0).T * SCALE).astype(BF16)
    dqkv_ref[:, SPAN : SPAN + HEAD_SIZE] = (dkv_ref[:, :HEAD_SIZE] * SCALE).astype(BF16)
    dqkv_ref[:, SPAN + HEAD_SIZE :] = dkv_ref[:, HEAD_SIZE:].astype(BF16)
    qkv_mat = w_ref[:, :QKV]
    dgain = jnp.zeros((1, MODEL), F32)
    for side, part_ref in enumerate((near_ref, far_ref)):
        places = [place(order_ref, 4 * side + block) for block in range(4)]
        rows = jnp.concatenate([dqkv_ref[at, :] for at in places], axis=0)
        part = dot_nt(rows, qkv_mat)
        for block, at in enumerate(places):
            here = part[block * ROWS : (block + 1) * ROWS] * normed_ref[at, :].astype(F32)
            dgain = dgain + jnp.sum(here, axis=0, keepdims=True)
        part_ref[: GROUP // 2, :] = part.astype(BF16)
    small_at = lax.broadcasted_iota(jnp.int32, (SMALL, MODEL), 0)
    small = jnp.where(small_at == EXPERTS + 1, dgain / gain_ref[...], small_ref[...])
    far_ref[GROUP // 2 :, :] = small.astype(BF16)
    for start in range(0, MODEL, PAIR):
        cols = slice(start, start + PAIR)
        qkv_part = dot_tn(dqkv_ref[...], normed_ref[:, cols])
        proj_part = dot_tn(att_ref[...], dattn_ref[:, cols])[HEAD_SIZE:]
        both = jnp.concatenate([qkv_part, proj_part], axis=0)
        whole_ref[cols, :] = both.T.astype(BF16)
    for block in range(8):
        grads_refs[block // 4][block % 4] = whole_ref[stored_rows(spread_ref, block), :]


def vmem_spec():
    return pl.BlockSpec(memory_space=pltpu.VMEM)


def smem_spec():
    return pl.BlockSpec(memory_space=pltpu.SMEM)


def attend(order, doc_row, doc_col, pieces, weights):
    return pl.pallas_call(
        attend_kernel,
        in_specs=[smem_spec()] + [vmem_spec()] * (3 + len(pieces)),
        out_specs=[vmem_spec()] * 6,
        out_shape=[
            jax.ShapeDtypeStruct((GROUP, MODEL), BF16),
            jax.ShapeDtypeStruct((GROUP, QKV), BF16),
            jax.ShapeDtypeStruct((GROUP, PAIR), BF16),
            jax.ShapeDtypeStruct((8, GROUP), F32),
            jax.ShapeDtypeStruct((GROUP // 2, MODEL), BF16),
            jax.ShapeDtypeStruct((GROUP // 2, MODEL), BF16),
        ],
        compiler_params=pltpu.CompilerParams(vmem_limit_bytes=VMEM_LIMIT),
        cost_estimate=pl.CostEstimate(
            flops=10**6, bytes_accessed=10**5, transcendentals=0
        ),
        name="attend",
    )(order, doc_row, doc_col, *pieces, weights)


def attend_back(order, spread, doc_row, doc_col, gain, small, weights, normed, qkv, att, lse, pieces):
    return pl.pallas_call(
        attend_back_kernel,
        in_specs=[smem_spec()] * 2 + [vmem_spec()] * (9 + len(pieces)),
        out_specs=[vmem_spec()] * 4,
        out_shape=[
            jax.ShapeDtypeStruct((GROUP // 2, MODEL), BF16),
            jax.ShapeDtypeStruct((GROUP // 2 + SMALL, MODEL), BF16),
        ]
        + [jax.ShapeDtypeStruct((4, STORED, 2 * PAIR), BF16)] * 2,
        scratch_shapes=[
            pltpu.VMEM((GROUP, MODEL), BF16),
            pltpu.VMEM((GROUP, PAIR), BF16),
            pltpu.VMEM((GROUP, QKV), BF16),
            pltpu.VMEM((GROUP, 2 * HEAD_SIZE), F32),
            pltpu.VMEM((MODEL, 2 * PAIR), BF16),
        ],
        compiler_params=pltpu.CompilerParams(vmem_limit_bytes=VMEM_LIMIT),
        cost_estimate=pl.CostEstimate(
            flops=10**6, bytes_accessed=10**5, transcendentals=0
        ),
        name="attend_back",
    )(order, spread, doc_row, doc_col, gain, small, weights, normed, qkv, att, lse, *pieces)


def moe_kernel(first_ref, router_ref, stored_ref, *refs, begin, count, more):
    sources, refs = (refs[:4], refs[4:8]), refs[8:]
    if more:
        prev_out_ref, prev_dn_ref = refs[:2]
        refs = refs[3:]
        outs, refs = (refs[:2], refs[2:4]), refs[4:]
    else:
        out_ref, dn_ref = refs[:2]
        refs = refs[2:]
    g_ref, in_all, dout_all, hid_all, dgu_all, held_t, held_c, sems, done, done_sems = refs[:10]
    w_ref, w_sems = refs[10:]
    step = pl.program_id(0)
    pairs = TILE // PAIR
    height = pairs * SLOTS
    last = PLANE // TILE - 1

    def copies(tile):
        return [
            pltpu.make_async_copy(
                sources[kind][tile], held.at[tile % 2], sems.at[kind, tile % 2]
            )
            for kind, held in enumerate((held_t, held_c))
        ]

    def fetch(e):
        return pltpu.make_async_copy(stored_ref.at[:, e], w_ref.at[:, e], w_sems.at[e])

    for tile in range(last + 1):

        @pl.when(step == max(tile - 1, 0))
        def _():
            for copy in copies(tile):
                copy.start()
            if tile == 0:
                for e in range(count):
                    fetch(e).start()

    for tile in range(last + 1):

        @pl.when(step == tile)
        def _():
            for copy in copies(tile):
                copy.wait()

    t_ref, c_ref = held_t.at[lax.rem(step, 2)], held_c.at[lax.rem(step, 2)]
    ids = c_ref[:, MODEL:].astype(F32).T.astype(jnp.int32)
    expert_at = lax.broadcasted_iota(jnp.int32, (EXPERTS, TILE), 0) + first_ref[0]
    expert_at = jnp.where(expert_at >= EXPERTS, expert_at - EXPERTS, expert_at)
    hits = ids[:1] == expert_at
    for choice in range(1, TOP):
        hits = hits | (ids[choice : choice + 1] == expert_at)
    mine = jnp.where(hits[:8], 1.0, 0.0)
    upto = lax.broadcasted_iota(jnp.int32, (PAIR, PAIR), 0) <= lax.broadcasted_iota(
        jnp.int32, (PAIR, PAIR), 1
    )
    upto = jnp.where(upto, 1.0, 0.0).astype(BF16)
    ranks = []
    for pair in range(pairs):
        here = mine[:, pair * PAIR : (pair + 1) * PAIR]
        ranks.append(jnp.where(here > 0.5, dot(here.astype(BF16), upto) - 1.0, -1.0).astype(jnp.int32))
    spot = pl.ds(pl.multiple_of(step * height, 16), height)
    logits = jnp.where(hits, dot_nt(router_ref[...], t_ref[...]), NEG_FILL)
    logits = jnp.exp(logits - jnp.max(logits, axis=0, keepdims=True))
    gates = logits / jnp.sum(logits, axis=0, keepdims=True)
    slot_at = lax.broadcasted_iota(jnp.int32, (SLOTS, PAIR), 0)
    picks, slot_gates, ins, cots = [], [], [], []
    for pair in range(pairs):
        cols = slice(pair * PAIR, (pair + 1) * PAIR)
        taken = [slot_at == ranks[pair][begin + e : begin + e + 1, :] for e in range(count)]
        slot_gates.append(
            [
                jnp.sum(
                    jnp.where(taken[e], gates[begin + e : begin + e + 1, cols], 0.0),
                    axis=1,
                    keepdims=True,
                )
                for e in range(count)
            ]
        )
        pick = jnp.concatenate([jnp.where(h, 1.0, 0.0).astype(BF16) for h in taken], axis=0)
        picks.append(pick)
        ins.append(dot(pick, t_ref[cols, :]).astype(BF16))
        cots.append(dot(pick, c_ref[cols, :MODEL]).astype(BF16))
    mixed = [[] for _ in range(pairs)]
    dins = [[] for _ in range(pairs)]
    lane = lax.broadcasted_iota(jnp.int32, (height, EXTRA), 1)
    for e in range(count):
        part = slice(e * SLOTS, (e + 1) * SLOTS)

        @pl.when(step == 0)
        def _():
            fetch(e).wait()

        rows_in = jnp.concatenate([v[part] for v in ins], axis=0)
        rows_cot = jnp.concatenate([v[part] for v in cots], axis=0)
        gate = jnp.concatenate([v[e] for v in slot_gates], axis=0)
        gate_up_w = w_ref[:, e, :, : 2 * FF_DEV].reshape(MODEL, 2 * FF_DEV)
        down_w = w_ref[:, e, :, 2 * FF_DEV :].reshape(MODEL, FF_DEV)
        gate_up = dot(rows_in, gate_up_w)
        pre, up = gate_up[:, :FF_DEV], gate_up[:, FF_DEV:]
        sig = 0.5 * jnp.tanh(0.5 * pre) + 0.5
        silu = pre * sig
        hidden = (silu * up).astype(BF16)
        plain = dot(rows_cot, down_w)
        dgate = jnp.sum(hidden.astype(F32) * plain, axis=1, keepdims=True)
        dhidden = plain * gate
        dpre = dhidden * up * sig * (1.0 + pre * (1.0 - sig))
        dgu = jnp.concatenate([dpre, dhidden * silu], axis=1).astype(BF16)
        in_all[e, spot, :] = rows_in
        dout_all[e, spot, :] = (rows_cot.astype(F32) * gate).astype(BF16)
        hid_all[e, spot, :] = hidden
        dgu_all[e, spot, :] = dgu
        mix = (dot_nt(hidden, down_w) * gate).astype(BF16)
        din = dot_nt(dgu, gate_up_w).astype(BF16)
        high = dgate.astype(BF16).astype(F32)
        tail = jnp.where(lane == first_ref[0] + (begin + e), high, 0.0) + jnp.where(
            lane == first_ref[0] + (begin + e + EXPERTS), dgate - high, 0.0
        )
        din = jnp.concatenate([din, tail.astype(BF16)], axis=1)
        for pair in range(pairs):
            rows = slice(pair * SLOTS, (pair + 1) * SLOTS)
            mixed[pair].append(mix[rows])
            dins[pair].append(din[rows])
    for pair in range(pairs):
        cols = slice(pair * PAIR, (pair + 1) * PAIR)
        out = dot_tn(picks[pair], jnp.concatenate(mixed[pair], axis=0))
        dn = dot_tn(picks[pair], jnp.concatenate(dins[pair], axis=0))
        if more:
            out = out + prev_out_ref[cols, :].astype(F32)
            dn = dn + prev_dn_ref[cols, :].astype(F32)
        if not more:
            out_ref[cols, :] = out.astype(BF16)
            dn_ref[cols, :] = dn.astype(BF16)
            continue

        for side in range(2):

            @pl.when(step // 2 == side)
            def _():
                outs[side][0][cols, :] = out.astype(BF16)
                outs[side][1][cols, :] = dn.astype(BF16)

    @pl.when(step == last)
    def _():
        sent = []
        for e in range(count):
            if e >= 2:
                sent[e - 2].wait()
            for start in range(0, MODEL, 2 * STORED):
                cols = slice(start, start + 2 * STORED)
                gate_up_g = dot_tn(in_all[e, :, cols], dgu_all[e])
                down_g = dot_tn(dout_all[e, :, cols], hid_all[e])
                both = jnp.concatenate([gate_up_g, down_g], axis=1).astype(BF16)
                for half in range(2):
                    at = slice(half * STORED, (half + 1) * STORED)
                    done[e % 2, start // STORED + half, :, :] = both[at, :]
            sent.append(
                pltpu.make_async_copy(done.at[e % 2], g_ref.at[:, begin + e], done_sems.at[e % 2])
            )
            sent[e].start()
        for copy in sent[-2:]:
            copy.wait()


def moe(chunk, first, router_t, weights, rows, cots, previous):
    begin, count = chunk
    height = PLANE // PAIR * SLOTS
    wide = pl.BlockSpec((TILE, MODEL), lambda i: (i, 0))
    wider = pl.BlockSpec((TILE, MODEL + EXTRA), lambda i: (i, 0))
    if previous is None:
        sums = [wide, wider]
        shapes = [(PLANE, MODEL), (PLANE, MODEL + EXTRA)]
    else:
        sides = (lambda i: (jnp.minimum(i, 1), 0)), (lambda i: (jnp.maximum(i - 2, 0), 0))
        sums = [pl.BlockSpec((TILE, w), side) for side in sides for w in (MODEL, MODEL + EXTRA)]
        shapes = [(PLANE // 2, MODEL), (PLANE // 2, MODEL + EXTRA)] * 2
    flops = 2 * count * height * MODEL * (9 * FF_DEV + 5 * PAIR)
    return pl.pallas_call(
        functools.partial(moe_kernel, begin=begin, count=count, more=previous is not None),
        grid=(PLANE // TILE,),
        in_specs=[
            smem_spec(),
            pl.BlockSpec((EXPERTS, MODEL), lambda i: (0, 0)),
            pl.BlockSpec(memory_space=pl.ANY),
        ]
        + [pl.BlockSpec(memory_space=pl.ANY)] * 8
        + ([wide, wider, pl.BlockSpec(memory_space=pl.ANY)] if previous is not None else []),
        out_specs=sums + [pl.BlockSpec(memory_space=pl.ANY)],
        out_shape=[jax.ShapeDtypeStruct(shape, BF16) for shape in shapes]
        + [
            jax.ShapeDtypeStruct((8, EXPERTS_DEV, STORED, 3 * FF_DEV), BF16),
        ],
        input_output_aliases={} if previous is None else {13: 4},
        scratch_shapes=[
            pltpu.VMEM((count, height, MODEL), BF16),
            pltpu.VMEM((count, height, MODEL), BF16),
            pltpu.VMEM((count, height, FF_DEV), BF16),
            pltpu.VMEM((count, height, 2 * FF_DEV), BF16),
            pltpu.VMEM((2, TILE, MODEL), BF16),
            pltpu.VMEM((2, TILE, MODEL + EXTRA), BF16),
            pltpu.SemaphoreType.DMA((2, 2)),
            pltpu.VMEM((2, 8, STORED, 3 * FF_DEV), BF16),
            pltpu.SemaphoreType.DMA((2,)),
            pltpu.VMEM((8, count, STORED, 3 * FF_DEV), BF16),
            pltpu.SemaphoreType.DMA((count,)),
        ],
        compiler_params=pltpu.CompilerParams(vmem_limit_bytes=VMEM_LIMIT),
        cost_estimate=pl.CostEstimate(
            flops=10**6, bytes_accessed=10**5, transcendentals=0
        ),
        name="moe",
    )(first, router_t, weights, *rows, *cots, *(previous or ()))


def across_col(value, distance):
    pairs = [(2 * x + c, 2 * ((x + distance) % 4) + c) for x in range(4) for c in range(2)]
    return lax.ppermute(value, "col", pairs)


def other_core(value):
    return lax.ppermute(value, "col", [(s, s ^ 1) for s in range(8)])


def other_row(value):
    return lax.ppermute(value, "row", [(0, 1), (1, 0)])


def along_z(value, distance):
    pairs = [(4 * y + z, 4 * y + (z + distance) % 4) for y in range(2) for z in range(4)]
    return lax.ppermute(value, "dp", pairs)


def other_y(value):
    return lax.ppermute(value, "dp", [(s, s ^ 4) for s in range(8)])


def total(values):
    result = values[0].astype(F32)
    for value in values[1:]:
        result = result + value.astype(F32)
    return result


def after(value, *before):
    return lax.optimization_barrier((value, before))[0]


def spread_col(value):
    return [value] + [across_col(value, d) for d in (1, 2, 3)]


def relay_col(value):
    ahead, behind = across_col(value, 1), across_col(value, -1)
    half = value.shape[0] // 2
    opposite = [across_col(ahead[:half], 1), across_col(behind[half:], -1)]
    return [value, ahead, jnp.concatenate(opposite, axis=0), behind]


def gather_col(value):
    near = spread_col(value)
    return near + [other_core(v) for v in near]


def scatter_blocks(near, far):
    sums = [
        total([near[d * ROWS : (d + 1) * ROWS], far[d * ROWS : (d + 1) * ROWS]]) for d in range(4)
    ]
    return sums[:1] + [v.astype(BF16) for v in sums[1:]]


def collect_col(blocks):
    return [blocks[0]] + [across_col(blocks[d], -d) for d in (1, 2, 3)]


def flip_x(value):
    return lax.ppermute(value, "col", [(s, s ^ 2) for s in range(8)])


def flip_z(value):
    return lax.ppermute(value, "dp", [(s, s ^ 1) for s in range(8)])


def add_both(value, move):
    return (value.astype(F32) + move(value).astype(F32)).astype(value.dtype)


def per_device(
    tokens,
    cotangent,
    lengths,
    routes,
    norm_gains,
    gain_first,
    gain_second,
    router_w,
    router_first,
    router_second,
    projection_weight,
    projection_first_moment,
    projection_second_moment,
    w_proj,
    proj_first,
    proj_second,
    w_gate_up,
    gate_up_first,
    gate_up_second,
    w_down,
    down_first,
    down_second,
):
    col, row, dp = lax.axis_index("col"), lax.axis_index("row"), lax.axis_index("dp")
    across, core = col // 2, col % 2
    steps = jnp.arange(4, dtype=jnp.int32)
    away = 2 * jnp.remainder(across - steps, 4)
    order = jnp.concatenate([away + core, away + 1 - core])
    spread = jnp.bitwise_xor(dp, jnp.arange(8, dtype=jnp.int32))
    token_places = jnp.arange(GROUP, dtype=jnp.int32)
    doc_ends = jnp.cumsum(lengths[0])
    documents = jnp.sum((token_places[:, None] >= doc_ends[None, :]).astype(jnp.int32), axis=1)
    doc_row, doc_col = documents[None, :], documents[:, None]

    residual_in = tokens.astype(F32)
    inverse_one = inv_rms(residual_in)
    normed_one = (residual_in * inverse_one * norm_gains[0]).astype(BF16)
    attn_w = jnp.concatenate([projection_weight[:, 0, :], w_proj.T], axis=1).astype(BF16)
    normed_near = relay_col(normed_one)
    normed_near = jnp.concatenate(normed_near, axis=0)
    normed_pieces = [normed_near, other_core(normed_near)]
    attn_full = lax.all_gather(attn_w, "dp", axis=0, tiled=True)

    gate_up_w, down_w = after((w_gate_up, w_down), attn_w, normed_one)
    expert_w = jnp.concatenate(
        [gate_up_w.reshape(EXPERTS_DEV, 192, 2 * FF_DEV), down_w.transpose(0, 2, 1)], axis=2
    ).astype(BF16)
    expert_ws = []
    for b, n in CHUNKS:
        expert_ws.append(lax.all_gather(expert_w[b : b + n], "dp", axis=0, tiled=False))

    tagged = jnp.concatenate(
        [cotangent, routes.astype(BF16), jnp.zeros((ROWS, EXTRA - routes.shape[1]), BF16)], axis=1
    )
    cots = [jnp.concatenate(relay_col(tagged), axis=0)]
    theirs = other_row(tagged)
    cots.append(jnp.concatenate(relay_col(theirs), axis=0))
    attn_full = after(attn_full, normed_pieces, cots)
    normed_full, qkv, att, lse, near, far = attend(
        order, doc_row, doc_col, normed_pieces, attn_full
    )
    attn_out = total(collect_col(scatter_blocks(near, other_core(far))))
    cots = cots + [other_core(v) for v in cots]
    router_low = router_w.astype(BF16)
    router_t = jnp.roll(router_low.T, -EXPERTS_DEV * col, axis=0)
    first = (EXPERTS_DEV * col).astype(jnp.int32).reshape(1)

    residual = residual_in + attn_out
    inverse_two = inv_rms(residual)
    normed_two = (residual * inverse_two * norm_gains[1]).astype(BF16)
    normed_two = after(normed_two, cots)
    rows_all = [
        jnp.concatenate(relay_col(v), axis=0) for v in (normed_two, other_row(normed_two))
    ]
    rows_all = rows_all + [other_core(v) for v in rows_all]
    logits = jnp.dot(normed_two, router_low, preferred_element_type=F32)
    route_hits = jnp.any(
        routes[:, None, :] == jnp.arange(EXPERTS, dtype=jnp.int32)[None, :, None], axis=-1
    )
    gates = jax.nn.softmax(jnp.where(route_hits, logits, NEG_FILL), axis=-1)

    previous = None
    for chunk, weights in zip(CHUNKS, expert_ws):
        previous = moe(chunk, first, router_t, weights, rows_all, cots, previous)
    mix_near, dn_near, mix_far, dn_far, expert_grads = previous
    expert_sum = lax.psum_scatter(expert_grads, "dp", scatter_dimension=0, tiled=False)

    far = other_core(dn_far)
    theirs = collect_col(scatter_blocks(dn_near[TILE:], far[TILE:]))
    mine = collect_col(scatter_blocks(dn_near[:TILE], far[:TILE]))
    mix_far = other_core(after(mix_far, far))
    mix_blocks = []
    for d in range(4):
        parts = [slice(start + d * ROWS, start + (d + 1) * ROWS) for start in (0, TILE)]
        parts = [total([mix_near[part], mix_far[part]]) for part in parts]
        mix_blocks.append(jnp.concatenate(parts, axis=0).astype(BF16))
    mine = after(mine, mix_blocks)
    dn = total(mine) + other_row(total(theirs).astype(BF16)).astype(F32)
    dgate = dn[:, MODEL : MODEL + EXPERTS] + dn[:, MODEL + EXPERTS : MODEL + 2 * EXPERTS]
    dlogits = gates * (dgate - jnp.sum(gates * dgate, axis=-1, keepdims=True))
    dnormed_two = dn[:, :MODEL] + jnp.dot(dlogits, router_low.astype(F32).T, precision=EXACT_MATH)
    upstream = cotangent.astype(F32)
    dresid_norm, grad_gain_two = norm_back(residual, inverse_two, norm_gains[1], dnormed_two)
    dresidual = upstream + dresid_norm
    dattn_near = spread_col(dresidual.astype(BF16))
    dattn_far = [other_core(v) for v in dattn_near]

    grad_router = lax.dot_general(
        dlogits, normed_two.astype(F32), (((0,), (0,)), ((), ())), precision=EXACT_MATH
    )
    small = jnp.concatenate(
        [grad_router, grad_gain_two[None], jnp.zeros((SMALL - EXPERTS - 1, MODEL), F32)], axis=0
    )
    dattn_pieces = after(dattn_near + dattn_far, small)
    near, far, *attn_grads = attend_back(
        order,
        spread,
        doc_row,
        doc_col,
        norm_gains[:1],
        small,
        attn_full,
        normed_full,
        qkv,
        att,
        lse,
        dattn_pieces,
    )
    theirs = other_core(far)
    blocks = scatter_blocks(near, theirs)
    small = total([far[GROUP // 2 :], theirs[GROUP // 2 :]]).astype(BF16)
    moved = [across_col(jnp.concatenate([blocks[d], small], axis=0), -d) for d in (1, 2, 3)]
    attn_moved = other_y(after(attn_grads[1], blocks))
    moved, = lax.optimization_barrier((moved,))
    attn_moved = after(attn_moved, moved)
    mix_moved = collect_col(after(mix_blocks, moved))
    pairs = total([small, moved[1][ROWS:]]), total([moved[0][ROWS:], moved[2][ROWS:]])
    small = (pairs[0] + pairs[1]).astype(BF16).reshape(-1, 2 * PAIR)
    dnormed = total([blocks[0]] + [v[:ROWS] for v in moved])
    dtokens_norm, _ = norm_back(residual_in, inverse_one, norm_gains[0], dnormed)
    dtokens = dresidual + dtokens_norm
    halves = total([attn_grads[0], attn_moved]).astype(BF16)
    sent = jnp.concatenate([halves[2:].reshape(-1, 2 * PAIR), small], axis=0)
    kept = jnp.concatenate([halves[:2].reshape(-1, 2 * PAIR), small], axis=0)
    experts_new = update_experts(
        expert_sum, (w_gate_up, gate_up_first, gate_up_second), (w_down, down_first, down_second)
    )
    kept = total([kept, after(along_z(sent, 2), experts_new)]).astype(BF16)
    sent = kept[STORED:]
    kept = jnp.concatenate([kept[:STORED], kept[2 * STORED :]], axis=0)
    kept = total([kept, flip_z(sent)]).astype(BF16)
    kept = add_both(kept, other_row)
    attn_sums = kept[:STORED]
    small = add_both(kept[STORED:], other_y)
    sum_qkv = attn_sums[:, None, :QKV].astype(F32)
    proj_new = update_proj(attn_sums, w_proj, proj_first, proj_second)
    mix_moved = after(mix_moved, dtokens, attn_sums)
    mixed = total(mix_moved)
    mix_theirs = after(other_row(mixed[ROWS:].astype(BF16)), proj_new, small)
    mixture = mixed[:ROWS] + mix_theirs.astype(F32)
    output = (residual + mixture).astype(BF16)
    small = small.reshape(-1, MODEL).astype(F32)
    sum_router = small[:EXPERTS].T
    sum_gains = jnp.stack([small[EXPERTS + 1], small[EXPERTS]])
    return (
        output,
        dtokens,
        *adamw(norm_gains, sum_gains, gain_first, gain_second, RATE_GAIN, 0.0),
        *adamw(router_w, sum_router, router_first, router_second, RATE_ROUTER, DECAY_RATE),
        *adamw(
            projection_weight,
            sum_qkv,
            projection_first_moment,
            projection_second_moment,
            RATE_NARROW,
            DECAY_RATE,
        ),
        *proj_new,
        *experts_new,
    )


def solution(mesh):
    by_token = P(("dp", "row", "col"), None)
    qkv_at, proj_at = P("dp", "col", None), P("col", "dp")
    gate_up_at, down_at = P("col", "dp", None, "row"), P("col", "row", "dp")
    return jax.shard_map(
        per_device,
        mesh=mesh,
        in_specs=(by_token, by_token, P(("dp", "row"), None), by_token)
        + (P(),) * 6
        + (qkv_at,) * 3
        + (proj_at,) * 3
        + (gate_up_at,) * 3
        + (down_at,) * 3,
        out_specs=(by_token, by_token)
        + (P(),) * 6
        + (qkv_at,) * 3
        + (proj_at,) * 3
        + (gate_up_at,) * 3
        + (down_at,) * 3,
        check_vma=False,
    )
```
